32 devices in a mesh: dp: 8 (over z, x), tensor: 4 (over y, core).
Axes of the slice: x: 2, y: 2, z: 4, core: 2. Of those that a mesh axis runs over, the one named last changes fastest.
Arguments:
- tokens: bfloat16 [16384, 1024], P(('dp', 'tensor')), may hold values from -6 to 6
- cotangent: bfloat16 [16384, 1024], P(('dp', 'tensor')), may hold values from -6 to 6
- qkv_weight: bfloat16 [2, 1024, 3072], P(None, None, 'tensor'), may hold values from -0.25 to 0.25
- qkv_bias: bfloat16 [2, 3072], P(None, 'tensor'), may hold values from -3 to 3
- out_weight: bfloat16 [2, 1024, 1024], P(None, 'tensor'), may hold values from -0.5 to 0.5
- out_bias: bfloat16 [2, 1024], replicated, may hold values from -3 to 3
- up_weight: bfloat16 [2, 1024, 4096], P(None, None, 'tensor'), may hold values from -0.1875 to 0.1875
- up_bias: bfloat16 [2, 4096], P(None, 'tensor'), may hold values from -3 to 3
- down_weight: bfloat16 [2, 4096, 1024], P(None, 'tensor'), may hold values from -0.125 to 0.125
- down_bias: bfloat16 [2, 1024], replicated, may hold values from -3 to 3
- norm_gain: bfloat16 [2, 2, 1024], replicated, may hold values from 0.5 to 1.5
- norm_shift: bfloat16 [2, 2, 1024], replicated, may hold values from -2 to 2
Outputs:
- output: float32 [16384, 1024], P(('dp', 'tensor'))
- input_grad: float32 [16384, 1024], P(('dp', 'tensor'))
- qkv_weight_grad: float32 [2, 1024, 3072], P(None, None, 'tensor')
- qkv_bias_grad: float32 [2, 3072], P(None, 'tensor')
- out_weight_grad: float32 [2, 1024, 1024], P(None, 'tensor')
- out_bias_grad: float32 [2, 1024], replicated
- up_weight_grad: float32 [2, 1024, 4096], P(None, None, 'tensor')
- up_bias_grad: float32 [2, 4096], P(None, 'tensor')
- down_weight_grad: float32 [2, 4096, 1024], P(None, 'tensor')
- down_bias_grad: float32 [2, 1024], replicated
- norm_gain_grad: float32 [2, 2, 1024], replicated
- norm_shift_grad: float32 [2, 2, 1024], replicated
- layer_stats: float32 [2, 3], replicated
The draws below stay inside these ranges and needn't reach their ends.
All inputs are finite; a program needn't handle non-finite values.
Results may differ from the reference program's by a relative error of at most 0.025.
The reference program's roundings to bfloat16 on the way count: a program that leaves them out, or rounds other values in their place, can miss the bound.
Values may be sent and summed in bfloat16 or wider, within the bound.
A program may use at most 512 MiB of HBM per device.

```python
import math
import jax
import jax.numpy as jnp
from jax import lax

D = 1024
HEADS = 16
HEAD = 64
ROT = 16
FF = 4096
LAYERS = 2
SEQ_LEN = 1024
BLOCK = 512
TOKENS = 16384


def draw_tokens(key, part):
    position = jnp.arange(TOKENS, dtype=jnp.float32)[:, None] / TOKENS
    factor = 1.0 + 0.75 * position
    base = jax.random.truncated_normal(key, -3.0, 3.0, (TOKENS, D), jnp.float32)
    return (base * factor).astype(jnp.bfloat16)


def block_levels(stream_key, extent, pieces, smallest, top_value):
    loudness, own = 1.0, jax.random.fold_in(stream_key, 6)
    for axis_at, shards_of in pieces:
        draws = jnp.exp(jax.random.uniform(jax.random.fold_in(own, axis_at), (shards_of,), jnp.float32, smallest / len(pieces), top_value / len(pieces)))
        loudness = loudness * jnp.repeat(draws, extent[axis_at] // shards_of).reshape([-1 if axis == axis_at else 1 for axis in range(len(extent))])
    return loudness


def gaussian(key, shape, width, reach, split=(), held_as=jnp.bfloat16):
    loudness = block_levels(key, shape, split, -0.22, 0.18) if split else 1.0
    values = jax.random.normal(key, shape, jnp.float32) * width * loudness
    return jnp.minimum(jnp.maximum(values, -reach), reach).astype(held_as)


def setup_inputs(seed: int = 0) -> dict:
    key_list = jax.random.split(jax.random.key(seed), 13)
    tokens = draw_tokens(jax.random.fold_in(key_list[12], 71), 0)
    cotangent = gaussian(key_list[1], (TOKENS, D), 1.0, 6.0, ((0, 32),))
    qkv_weight = gaussian(key_list[2], (LAYERS, D, 3 * D), (D // 2) ** -0.5, 0.25, ((2, 4),))
    qkv_bias = gaussian(key_list[3], (LAYERS, 3 * D), 0.5, 3.0, ((1, 4),))
    out_weight = gaussian(key_list[4], (LAYERS, D, D), (D // 8) ** -0.5, 0.5, ((1, 4),))
    out_bias = gaussian(key_list[5], (LAYERS, D), 0.5, 3.0)
    up_weight = gaussian(key_list[6], (LAYERS, D, FF), D ** -0.5, 0.1875, ((2, 4),))
    up_bias = gaussian(key_list[7], (LAYERS, FF), 0.5, 3.0, ((1, 4),))
    down_weight = gaussian(key_list[8], (LAYERS, FF, D), (FF // 2) ** -0.5, 0.125, ((1, 4),))
    down_bias = gaussian(key_list[9], (LAYERS, D), 0.5, 3.0)
    norm_gain = jnp.clip(1.0 + 0.1 * jax.random.normal(key_list[10], (LAYERS, 2, D), jnp.float32), 0.5, 1.5).astype(jnp.bfloat16)
    norm_shift = gaussian(key_list[11], (LAYERS, 2, D), 0.3, 2.0)
    return {"tokens": tokens, "cotangent": cotangent, "qkv_weight": qkv_weight, "qkv_bias": qkv_bias, "out_weight": out_weight, "out_bias": out_bias, "up_weight": up_weight, "up_bias": up_bias, "down_weight": down_weight, "down_bias": down_bias, "norm_gain": norm_gain, "norm_shift": norm_shift}


EPS = 1e-05
NEG = -1e+30
HIGHEST = lax.Precision.HIGHEST

@jax.custom_vjp
def low(v):
    return lax.optimization_barrier(v.astype(jnp.bfloat16)).astype(jnp.float32)

@jax.custom_vjp
def low_back(v):
    return v

def low_keep(v):
    return (low(v), None)

def low_pass(kept, grad):
    return (grad,)

def back_keep(v):
    return (v, None)

def back_low(kept, grad):
    return (low(grad),)
low.defvjp(low_keep, low_pass)
low_back.defvjp(back_keep, back_low)

def layer_norm(stream, gain_vec, shift_vec):
    average = lax.optimization_barrier(jnp.mean(stream, axis=-1, keepdims=True))
    centred = stream - average
    variance = lax.optimization_barrier(jnp.mean(centred * centred, axis=-1, keepdims=True))
    return centred * lax.rsqrt(variance + EPS) * gain_vec + shift_vec

def rope_tables(length):
    positions = (jnp.arange(length, dtype=jnp.int32) % SEQ_LEN).astype(jnp.float32)
    inverse = jnp.exp(jnp.arange(ROT // 2, dtype=jnp.float32) * (-2.0 * math.log(10000.0) / ROT))
    angles = positions[:, None] * inverse[None, :]
    angles = jnp.concatenate([angles, angles], axis=1)
    return (jnp.cos(angles), jnp.sin(angles))

def rotate(tensor_in, cosine_table, sine_table):
    head_part = tensor_in[..., :ROT]
    front_half = head_part[..., :ROT // 2]
    back_half = head_part[..., ROT // 2:]
    turned = jnp.concatenate([-back_half, front_half], axis=-1)
    return jnp.concatenate([head_part * cosine_table + turned * sine_table, tensor_in[..., ROT:]], axis=-1)

def product(left, right):
    return jnp.dot(left, right, precision=HIGHEST, preferred_element_type=jnp.float32)

def attend(queries, key_rows, value_rows):
    scaling = HEAD ** (-0.5)
    columns = jnp.arange(SEQ_LEN, dtype=jnp.int32)

    def one_block(first_row):
        q_block = lax.dynamic_slice_in_dim(queries, first_row, BLOCK, 0)
        scores = low_back(jnp.einsum('qhe,khe->hqk', q_block, key_rows, precision=HIGHEST) * scaling)
        row_index = first_row + jnp.arange(BLOCK, dtype=jnp.int32)
        scores = jnp.where(columns[None, None, :] <= row_index[None, :, None], scores, NEG)
        row_max = lax.optimization_barrier(jnp.max(scores, axis=-1, keepdims=True))
        exponent = jnp.exp(scores - row_max)
        weights = exponent / lax.optimization_barrier(jnp.sum(exponent, axis=-1, keepdims=True))
        return jnp.einsum('hqk,khe->qhe', low(weights), value_rows, precision=HIGHEST)
    starts = jnp.arange(SEQ_LEN // BLOCK, dtype=jnp.int32) * BLOCK
    return lax.map(jax.checkpoint(one_block), starts).reshape(SEQ_LEN, HEADS, HEAD)

def model(stream, params):
    qkv_w, qkv_b, out_w, out_b, up_w, up_b, down_w, down_b, gains, shifts = params
    row_total = stream.shape[0]
    sequences = row_total // SEQ_LEN
    cosine_table, sine_table = rope_tables(SEQ_LEN)
    cosine_table = cosine_table[None, :, None, None, :]
    sine_table = sine_table[None, :, None, None, :]
    stat_rows = []
    for layer_index in range(LAYERS):
        normed_a = low(layer_norm(stream, gains[layer_index, 0], shifts[layer_index, 0]))
        normed_b = low(layer_norm(stream, gains[layer_index, 1], shifts[layer_index, 1]))
        qkv_rows = low_back(product(normed_a, qkv_w[layer_index]) + qkv_b[layer_index])
        qkv_rows = qkv_rows.reshape(sequences, SEQ_LEN, HEADS, 3, HEAD)
        turned = rotate(qkv_rows[:, :, :, :2], cosine_table, sine_table)
        queries = low(turned[:, :, :, 0])
        key_rows = low(turned[:, :, :, 1])
        value_rows = low(qkv_rows[:, :, :, 2])
        context = lax.map(lambda parts: attend(parts[0], parts[1], parts[2]), (queries, key_rows, value_rows))
        context = low(low_back(context.reshape(row_total, D)))
        attention_out = low_back(product(context, out_w[layer_index]) + out_b[layer_index])
        pre_gelu = low_back(product(normed_b, up_w[layer_index]) + up_b[layer_index])
        hidden = low(jax.nn.gelu(pre_gelu, approximate=False))
        ffn_out = low_back(product(hidden, down_w[layer_index]) + down_b[layer_index])
        stream = stream + attention_out + ffn_out
        stat_rows.append(jnp.stack([jnp.sum(stream * stream), jnp.sum(attention_out * attention_out), jnp.sum(ffn_out * ffn_out)]))
    return (stream, jnp.stack(stat_rows))

def reference(tokens, cotangent, qkv_weight, qkv_bias, out_weight, out_bias, up_weight, up_bias, down_weight, down_bias, norm_gain, norm_shift):
    params = (qkv_weight.astype(jnp.float32), qkv_bias.astype(jnp.float32), out_weight.astype(jnp.float32), out_bias.astype(jnp.float32), up_weight.astype(jnp.float32), up_bias.astype(jnp.float32), down_weight.astype(jnp.float32), down_bias.astype(jnp.float32), norm_gain.astype(jnp.float32), norm_shift.astype(jnp.float32))
    start = tokens.astype(jnp.float32)
    result, pullback, stat_sums = jax.vjp(model, start, params, has_aux=True)
    grad_tokens, grad_params = pullback(cotangent.astype(jnp.float32))
    layer_stats = jnp.sqrt(stat_sums / (TOKENS * D))
    return (result, grad_tokens, grad_params[0], grad_params[1], grad_params[2], grad_params[3], grad_params[4], grad_params[5], grad_params[6], grad_params[7], grad_params[8], grad_params[9], layer_stats)
```

```python
import functools
import math

import jax
import jax.numpy as jnp
from jax import lax
from jax.experimental import pallas as pl
from jax.experimental.pallas import tpu as pltpu
from jax.sharding import PartitionSpec as P

HEAD = 64
ROT = 16
LAYERS = 2
SEQ_LEN = 1024
QB = 256
SCALE = HEAD ** (-0.5)

EPS = 1e-05
NEG = -1e30
F32 = jnp.float32
B16 = jnp.bfloat16
MIB = 1024 * 1024


def dot_nn(left, right):
    return lax.dot_general(left, right, (((1,), (0,)), ((), ())), preferred_element_type=F32)


def dot_nt(left, right):
    return lax.dot_general(left, right, (((1,), (1,)), ((), ())), preferred_element_type=F32)


def dot_tn(left, right):
    return lax.dot_general(left, right, (((0,), (0,)), ((), ())), preferred_element_type=F32)


def rope_tables(seq, width):
    positions = jnp.arange(seq, dtype=jnp.int32).astype(F32)
    inverse = jnp.exp(jnp.arange(ROT // 2, dtype=F32) * (-2.0 * math.log(10000.0) / ROT))
    angles = positions[:, None] * inverse[None, :]
    cosine, sine = jnp.cos(angles), jnp.sin(angles)
    zero = jnp.zeros_like(sine)
    rest = jnp.zeros((seq, HEAD - ROT), F32)
    repeat = lambda parts: jnp.tile(jnp.concatenate(parts, axis=1), (1, width // HEAD))
    return (
        repeat([cosine, cosine, rest + 1.0]),
        repeat([-sine, zero, rest]),
        repeat([zero, sine, rest]),
    )


def rope(rows, cos, sin_lo, sin_hi, sign):
    width = cos.shape[1]
    parts = []
    for j in range(rows.shape[1] // width):
        part = rows[:, j * width : (j + 1) * width]
        turned = (
            pltpu.roll(part, width - ROT // 2, 1) * sin_lo + pltpu.roll(part, ROT // 2, 1) * sin_hi
        )
        parts.append(part * cos + turned if sign > 0 else part * cos - turned)
    return parts[0] if len(parts) == 1 else jnp.concatenate(parts, axis=1)


def attend_forward_kernel(
    w, seq, x_ref, w_ref, b_ref, cos_ref, lo_ref, hi_ref, qkv_ref, ctx_ref, lse_ref
):
    h = pl.program_id(0)
    blocks = seq // QB
    shift = (lax.axis_index("tensor") % 2) * (blocks // 2)
    swapped = lambda i: pl.ds(pl.multiple_of(lax.rem(i + shift, blocks) * QB, QB), QB)

    @pl.when(h == 0)
    def _():
        lse_ref[...] = jnp.zeros_like(lse_ref)
        ctx_ref[...] = jnp.zeros_like(ctx_ref)

        @pl.loop(0, seq // QB)
        def _(r):
            rows = pl.ds(pl.multiple_of(r * QB, QB), QB)
            acc = dot_nn(x_ref[swapped(r), :], w_ref[...]) + b_ref[...]
            turned = rope(acc[:, : 2 * w], cos_ref[rows, :], lo_ref[rows, :], hi_ref[rows, :], 1)
            qkv_ref[rows, : 2 * w] = turned.astype(B16)
            qkv_ref[rows, 2 * w :] = acc[:, 2 * w :].astype(B16)

    mine = (lax.broadcasted_iota(jnp.int32, (1, w), 1) // HEAD) == h
    keep = jnp.where(mine, SCALE, 0.0).astype(B16)
    for i in range(seq // QB):
        n = (i + 1) * QB
        q = qkv_ref[i * QB : n, :w] * keep
        s = dot_nt(q, qkv_ref[:n, w : 2 * w])
        tri = lax.broadcasted_iota(jnp.int32, (QB, QB), 0) >= lax.broadcasted_iota(
            jnp.int32, (QB, QB), 1
        )
        last = jnp.where(tri, s[:, n - QB :], NEG)
        s = last if i == 0 else jnp.concatenate([s[:, : n - QB], last], axis=1)
        top = jnp.max(s, axis=1, keepdims=True)
        p = jnp.exp(s - top)
        total = jnp.sum(p, axis=1, keepdims=True)
        low = (p * (1.0 / total)).astype(B16)
        c = dot_nn(low, qkv_ref[:n, 2 * w :])
        old = ctx_ref[swapped(i), :]
        ctx_ref[swapped(i), :] = jnp.where(mine, c, old.astype(F32)).astype(B16)
        lane = lax.broadcasted_iota(jnp.int32, (QB, 128), 1)
        lse_ref[i * QB : n, :] = jnp.where(lane == h, top + jnp.log(total), lse_ref[i * QB : n, :])


def whole(shape):
    return pl.BlockSpec(shape, lambda h: (0,) * len(shape))


def attend_forward(x, weight, bias, tables):
    seq, features = x.shape
    w = weight.shape[1] // 3
    heads = w // HEAD
    table = tables[0].shape
    return pl.pallas_call(
        functools.partial(attend_forward_kernel, w, seq),
        grid=(heads,),
        in_specs=[
            whole((seq, features)),
            whole((features, 3 * w)),
            whole((1, 3 * w)),
            whole(table),
            whole(table),
            whole(table),
        ],
        out_specs=[whole((seq, 3 * w)), whole((seq, w)), whole((seq, 128))],
        out_shape=[
            jax.ShapeDtypeStruct((seq, 3 * w), B16),
            jax.ShapeDtypeStruct((seq, w), B16),
            jax.ShapeDtypeStruct((seq, 128), F32),
        ],
        compiler_params=pltpu.CompilerParams(
            vmem_limit_bytes=40 * MIB, dimension_semantics=("arbitrary",)
        ),
        cost_estimate=pl.CostEstimate(
            flops=2 * seq * features * 3 * w + 4 * seq * seq * 256 * heads,
            bytes_accessed=2 * seq * features + 6 * features * w + 8 * seq * w,
            transcendentals=seq * seq * heads // 2,
        ),
        name="attend_forward",
    )(x, weight, bias, *tables)


def attend_backward_kernel(
    w,
    seq,
    qkv_ref,
    d_ref,
    lse_ref,
    cos_ref,
    lo_ref,
    hi_ref,
    out_ref,
    bias_ref,
    dq_ref,
    dk_ref,
    dv_ref,
):
    h = pl.program_id(0)
    heads = w // HEAD
    blocks = seq // QB
    shift = (lax.axis_index("tensor") % 2) * (blocks // 2)
    swapped = lambda i: pl.ds(pl.multiple_of(lax.rem(i + shift, blocks) * QB, QB), QB)

    @pl.when(h == 0)
    def _():
        dq_ref[...] = jnp.zeros_like(dq_ref)
        dk_ref[...] = jnp.zeros_like(dk_ref)
        dv_ref[...] = jnp.zeros_like(dv_ref)

    mine = (lax.broadcasted_iota(jnp.int32, (1, w), 1) // HEAD) == h
    keep = jnp.where(mine, SCALE, 0.0).astype(B16)
    keep_value = jnp.where(mine, 1.0, 0.0).astype(B16)
    for i in range(seq // QB):
        n = (i + 1) * QB
        q = qkv_ref[i * QB : n, :w] * keep
        d = d_ref[swapped(i), :] * keep_value
        s = dot_nt(q, qkv_ref[:n, w : 2 * w])
        lane = lax.broadcasted_iota(jnp.int32, (QB, 128), 1)
        lse = jnp.sum(jnp.where(lane == h, lse_ref[i * QB : n, :], 0.0), axis=1, keepdims=True)
        tri = lax.broadcasted_iota(jnp.int32, (QB, QB), 0) >= lax.broadcasted_iota(
            jnp.int32, (QB, QB), 1
        )
        last = jnp.where(tri, s[:, n - QB :], NEG)
        s = last if i == 0 else jnp.concatenate([s[:, : n - QB], last], axis=1)
        p = jnp.exp(s - lse)
        dp = dot_nt(d, qkv_ref[:n, 2 * w :])
        inner = jnp.sum(p * dp, axis=1, keepdims=True)
        ds = (p * (dp - inner)).astype(B16)
        dq_ref[i * QB : n, :] += dot_nn(ds, qkv_ref[:n, w : 2 * w] * keep)
        dk_ref[:n, :] += dot_tn(ds, q)
        dv_ref[:n, :] += dot_tn(p.astype(B16), d)

    @pl.when(h == heads - 1)
    def _():
        bias_ref[...] = jnp.zeros_like(bias_ref)

        @pl.loop(0, seq // QB)
        def _(r):
            rows = pl.ds(pl.multiple_of(r * QB, QB), QB)
            qk = jnp.concatenate([dq_ref[rows, :], dk_ref[rows, :]], axis=1)
            qk = rope(qk, cos_ref[rows, :], lo_ref[rows, :], hi_ref[rows, :], -1).astype(B16)
            v = dv_ref[rows, :].astype(B16)
            out_ref[swapped(r), : 2 * w] = qk
            out_ref[swapped(r), 2 * w :] = v
            bias_ref[:, : 2 * w] += jnp.sum(qk.astype(F32), axis=0, keepdims=True)
            bias_ref[:, 2 * w :] += jnp.sum(v.astype(F32), axis=0, keepdims=True)


def attend_backward(qkv, d_context, lse, tables):
    seq = qkv.shape[0]
    w = qkv.shape[1] // 3
    heads = w // HEAD
    table = tables[0].shape
    return pl.pallas_call(
        functools.partial(attend_backward_kernel, w, seq),
        grid=(heads,),
        in_specs=[
            whole((seq, 3 * w)),
            whole((seq, w)),
            whole((seq, 128)),
            whole(table),
            whole(table),
            whole(table),
        ],
        out_specs=[whole((seq, 3 * w)), whole((1, 3 * w))],
        out_shape=[
            jax.ShapeDtypeStruct((seq, 3 * w), B16),
            jax.ShapeDtypeStruct((1, 3 * w), F32),
        ],
        scratch_shapes=[pltpu.VMEM((seq, w), F32)] * 3,
        compiler_params=pltpu.CompilerParams(
            vmem_limit_bytes=40 * MIB, dimension_semantics=("arbitrary",)
        ),
        cost_estimate=pl.CostEstimate(
            flops=10 * seq * seq * 256 * heads,
            bytes_accessed=16 * seq * w,
            transcendentals=seq * seq * heads // 2,
        ),
        name="attend_backward",
    )(qkv, d_context, lse, *tables)


def normal_parts(u):
    x = jnp.abs(u) * (0.5**0.5)
    t = 1.0 / (1.0 + 0.3275911 * x)
    bell = jnp.exp(-0.5 * u * u)
    poly = t * (
        0.254829592
        + t * (-0.284496736 + t * (1.421413741 + t * (-1.453152027 + t * 1.061405429)))
    )
    half_tail = 0.5 * poly * bell
    return jnp.where(u >= 0.0, 1.0 - half_tail, half_tail), bell


def gelu(u):
    return u * normal_parts(u)[0]


def gelu_slope(u):
    share, bell = normal_parts(u)
    return share + u * bell * ((2.0 * math.pi) ** -0.5)


def standardize(x):
    average = jnp.mean(x, axis=-1, keepdims=True)
    centred = x - average
    variance = jnp.mean(centred * centred, axis=-1, keepdims=True)
    inverse = lax.rsqrt(variance + EPS)
    return centred * inverse, inverse


def swap(x, axis, bit):
    size = lax.axis_size(axis)
    return lax.ppermute(x, axis, [(i, i ^ bit) for i in range(size)])


def all_bits(size):
    bits = []
    bit = 1
    while bit < size:
        bits.append(bit)
        bit *= 2
    return bits


def after(x, *others):
    return lax.optimization_barrier((x,) + others)[0]


def on_device(
    tokens,
    cotangent,
    qkv_weight,
    qkv_bias,
    out_weight,
    out_bias,
    up_weight,
    up_bias,
    down_weight,
    down_bias,
    norm_gain,
    norm_shift,
):
    rows, features = tokens.shape
    tensor = lax.axis_size("tensor")
    dp = lax.axis_size("dp")
    chips = tensor // 2
    dp_index = lax.axis_index("dp")
    core = lax.axis_index("tensor") % 2
    w = qkv_weight.shape[2] // 3
    ff = up_weight.shape[2]
    heads = w // HEAD
    tables = rope_tables(SEQ_LEN, min(128, 2 * w))
    streams = range(chips)
    chip_bits = all_bits(chips)
    dp_bits = all_bits(dp)

    def core_gather(half):
        return jnp.concatenate([half, swap(half, "tensor", 1)], axis=0)

    def chip_gather(half):
        found = [half]
        for bit in chip_bits:
            found = found + [swap(item, "tensor", 2 * bit) for item in found]
        return found

    def chip_scatter(parts):
        for bit in reversed(chip_bits):
            sent = [swap(part.astype(B16), "tensor", 2 * bit) for part in parts[bit:]]
            parts = [part + got.astype(F32) for part, got in zip(parts[:bit], sent)]
        return parts[0]

    def chip_reduce(parts):
        for bit in chip_bits:
            low = [part.astype(B16) for part in parts]
            sent = [swap(part, "tensor", 2 * bit) for part in low]
            parts = [low[k].astype(F32) + sent[k ^ bit].astype(F32) for k in range(len(parts))]
        return parts

    def core_product(left, right, dot):
        got = swap(dot(left[rows:], right), "tensor", 1)
        return dot(left[:rows], right) + got

    def regroup(columns, back):
        lead = columns.shape[:-1]
        order = (3, heads, HEAD) if back else (heads, 3, HEAD)
        return jnp.swapaxes(columns.reshape(lead + order), -3, -2).reshape(columns.shape)

    qkv_w = [regroup(qkv_weight[l], False) for l in range(LAYERS)]
    qkv_b = [regroup(qkv_bias[l].astype(F32), False)[None] for l in range(LAYERS)]

    share = out_weight.shape[1] // dp
    piece = lax.dynamic_slice_in_dim(out_weight, dp_index * share, share, axis=1)
    near = [out_weight]
    for j in range(1, chips):
        near.append(lax.all_gather(swap(piece, "tensor", 2 * j), "dp", axis=1, tiled=True))
    far = [swap(item, "tensor", 1) for item in near]
    out_all = jnp.concatenate([x for pair in zip(near, far) for x in pair], axis=1)

    x_half = [t.astype(F32) for t in chip_gather(tokens)]
    stored = []
    stat_terms = []
    tick = tokens
    for l in range(LAYERS):
        final = l == LAYERS - 1
        gains = norm_gain[l].astype(F32)
        shifts = norm_shift[l].astype(F32)
        order = list(streams) if l == 0 else list(reversed(streams))
        na, nb, pre, hidden, ffn, qkv, ctx, lse, near = ([None] * chips for _ in range(9))
        up_b = up_bias[l].astype(F32)

        def feed(k):
            u = dot_nn(nb[k], up_weight[l]) + up_b
            pre[k] = u
            hidden[k] = gelu(u).astype(B16)
            ffn[k] = core_product(hidden[k], down_weight[l], dot_nn)

        def attend(k):
            qkv[k], ctx[k], lse[k] = attend_forward(na[k], qkv_w[l], qkv_b[l], tables)
            got = swap(ctx[k][rows:], "tensor", 1)
            near[k] = jnp.concatenate([ctx[k][:rows], got], axis=1)

        for k in order:
            z, _ = standardize(x_half[k])
            na[k] = core_gather((z * gains[0] + shifts[0]).astype(B16))
            nb[k] = core_gather((z * gains[1] + shifts[1]).astype(B16))
        if l == 0:
            for k in order:
                nb[k] = after(nb[k], tick)
                feed(k)
                na[k] = after(na[k], hidden[k])
                attend(k)
                tick = ctx[k]
        else:
            for k in order:
                nb[k] = after(nb[k], tick)
                feed(k)
                tick = hidden[k]
            for k in order:
                na[k] = after(na[k], tick)
                attend(k)
                tick = ctx[k]
        if final:
            ffn = [chip_scatter(ffn)]
        else:
            ffn = chip_reduce(ffn)
        x_next = []
        for k in streams if not final else range(1):
            blocks = [near[k]] + [swap(near[k ^ j], "tensor", 2 * j) for j in range(1, chips)]
            attn = dot_nn(jnp.concatenate(blocks, axis=1), out_all[l]) + out_bias[l].astype(F32)
            ffn_out = ffn[k] + down_bias[l].astype(F32)
            x_next.append(x_half[k] + attn + ffn_out)
            if k == 0:
                stat_terms.append(
                    jnp.stack(
                        [
                            jnp.sum(x_next[0] * x_next[0]),
                            jnp.sum(attn * attn),
                            jnp.sum(ffn_out * ffn_out),
                        ]
                    )
                )
        stored.append((x_half, na, nb, pre, hidden, qkv, ctx, lse))
        if l == 0:
            grad_low_half = chip_gather(after(cotangent, x_next[0]))
        x_half = x_next
    output = x_half[0]

    grad = cotangent.astype(F32)
    big = [None] * LAYERS
    small_all = [None] * LAYERS
    small_dp = [None] * LAYERS
    summed = None
    for l in reversed(range(LAYERS)):
        x_half, na, nb, pre, hidden, qkv, ctx, lse = stored[l]
        gains = norm_gain[l].astype(F32)
        low = grad.astype(B16)
        if l < LAYERS - 1:
            grad_low_half = chip_gather(low)
        g = [core_gather(item) for item in grad_low_half]
        g[0] = after(g[0], tick)
        d_pre, d_qkv, d_z = [None] * chips, [None] * chips, [None] * chips
        down_g = sum(dot_tn(hidden[k], g[k]) for k in streams)
        up_bias_g = jnp.zeros((ff,), F32)
        qkv_bias_g = jnp.zeros((1, 3 * w), F32)
        sums = 0.0
        for k in streams:
            d_pre[k] = (dot_nt(g[k], down_weight[l]) * gelu_slope(pre[k])).astype(B16)
            up_bias_g = up_bias_g + jnp.sum(d_pre[k], axis=0, dtype=F32)
        up_g = sum(dot_tn(nb[k], d_pre[k]) for k in streams)
        first = (down_g.astype(B16), up_g.astype(B16))
        if summed is not None:
            first = lax.optimization_barrier(first + summed[:1])[:2]
        first = lax.psum(first, "dp")
        tick = up_g
        for k in reversed(streams):
            d_ctx = dot_nt(g[k], out_weight[l]).astype(B16)
            d_qkv[k], bias_k = attend_backward(qkv[k], after(d_ctx, tick), lse[k], tables)
            tick = d_qkv[k]
            qkv_bias_g = qkv_bias_g + bias_k
            d_na = core_product(d_qkv[k], qkv_w[l], dot_nt)
            d_nb = core_product(d_pre[k], up_weight[l], dot_nt)
            z, inverse = standardize(x_half[k])
            sums = sums + jnp.stack(
                [
                    jnp.sum(d_na * z, axis=0),
                    jnp.sum(d_nb * z, axis=0),
                    jnp.sum(d_na, axis=0),
                    jnp.sum(d_nb, axis=0),
                ]
            )
            d_z[k] = d_na * gains[0] + d_nb * gains[1]
        total = chip_scatter(d_z)
        slope = total - jnp.mean(total, axis=-1, keepdims=True)
        slope = slope - z * jnp.mean(total * z, axis=-1, keepdims=True)
        bias_g = jnp.sum(low, axis=0, dtype=F32)
        grad = grad + slope * inverse
        out_g = sum(dot_tn(ctx[k], g[k]) for k in streams)
        qkv_g = sum(dot_tn(na[k], d_qkv[k]) for k in streams)
        second = (qkv_g.astype(B16), out_g.astype(B16))
        second = lax.optimization_barrier(second + first[:1])[:2]
        second = lax.psum(second, "dp")
        small_all[l] = jnp.concatenate(
            [sums, bias_g[None], jnp.pad(stat_terms[l], (0, features - 3))[None]], axis=0
        )
        small_dp[l] = jnp.concatenate([up_bias_g, qkv_bias_g[0]])
        big[l] = first + second
        summed = second
    small = jnp.stack(small_all)
    for bit in all_bits(tensor):
        small = small + swap(small, "tensor", bit)
    vector = jnp.stack(small_dp)
    for bit in dp_bits:
        small = small + swap(small, "dp", bit)
        vector = vector + swap(vector, "dp", bit)
    down_all = jnp.stack([item[0] for item in big]).astype(F32)
    up_all = jnp.stack([item[1] for item in big]).astype(F32)
    qkv_all = jnp.stack([regroup(item[2], True) for item in big]).astype(F32)
    out_w_all = jnp.stack([item[3] for item in big]).astype(F32)
    layer_stats = jnp.sqrt(small[:, 5, :3] / (rows * dp * tensor * features))
    bias_all = small[:, 4]
    return (
        output,
        grad,
        qkv_all,
        regroup(vector[:, ff:], True),
        out_w_all,
        bias_all,
        up_all,
        vector[:, :ff],
        down_all,
        bias_all,
        small[:, 0:2],
        small[:, 2:4],
        layer_stats,
    )


MESH = pl.DeviceIdType.MESH
ANY = pl.BlockSpec(memory_space=pl.ANY)
VMEM = pl.BlockSpec(memory_space=pltpu.VMEM)
DMA = pltpu.SemaphoreType.DMA


def partners():
    me = lax.axis_index("tensor")
    return me + 1 - 2 * lax.rem(me, 2), lax.rem(me + 2, 4)


def greet(others):
    barrier = pltpu.get_barrier_semaphore()
    for other in others:
        pl.semaphore_signal(barrier, inc=1, device_id={"tensor": other}, device_id_type=MESH)
    pl.semaphore_wait(barrier, len(others))


def remote(src, dst, sems, index, target):
    return pltpu.make_async_remote_copy(
        src_ref=src,
        dst_ref=dst,
        send_sem=sems[0].at[index],
        recv_sem=sems[1].at[index],
        device_id={"tensor": target},
        device_id_type=MESH,
    )


def block(i, size=QB):
    return pl.ds(pl.multiple_of(i * size, size), size)


def by_kind(rows, heads):
    return jnp.concatenate(
        [
            rows[:, (3 * h + j) * HEAD : (3 * h + j + 1) * HEAD]
            for j in range(3)
            for h in range(heads)
        ],
        axis=1,
    )


def by_head(rows, heads):
    return jnp.concatenate(
        [
            rows[:, (heads * j + h) * HEAD : (heads * j + h + 1) * HEAD]
            for h in range(heads)
            for j in range(3)
        ],
        axis=1,
    )


def causal(s, n):
    tri = lax.broadcasted_iota(jnp.int32, (QB, QB), 0) >= lax.broadcasted_iota(
        jnp.int32, (QB, QB), 1
    )
    last = jnp.where(tri, s[:, n - QB :], NEG)
    return last if n == QB else jnp.concatenate([s[:, : n - QB], last], axis=1)


def forward_layer_kernel(first, final, rows, w, *refs):
    it = iter(refs)
    x_ref, up_ref, upb_ref, down_ref, qkvw_ref, qkvb_ref = (next(it) for _ in range(6))
    out_ref, ob_ref, gain_ref, shift_ref = (next(it) for _ in range(4))
    cos_ref, lo_ref, hi_ref = (next(it) for _ in range(3))
    cot_ref = next(it) if final else None
    na_o, nb_o, u_o, hid_o, qkv_o, ctx_o, lse_o, x_o = (next(it) for _ in range(8))
    far_o = next(it) if first or final else None
    na_s, nb_s, u_s, hid_s, psend, precv, ysend, yrecv = (next(it) for _ in range(8))
    qkv_s, ctx_s, lse_s = (next(it) for _ in range(3))
    far_s = next(it) if first or final else None
    mine_s = next(it)
    send, recv, local, u_sem = (next(it) for _ in range(4))
    sems = (send, recv)

    seq = 2 * rows
    heads = w // HEAD
    blocks = seq // QB
    half_blocks = rows // QB
    shift = lax.rem(lax.axis_index("tensor"), 2) * half_blocks
    core, far = partners()
    greet((core, far))
    outs = []

    def keep(src, dst, index):
        copy = pltpu.make_async_copy(src, dst, local.at[index])
        copy.start()
        outs.append(copy)

    far_copy = None
    if first or final:
        far_copy = remote(x_ref if first else cot_ref, far_s, sems, 0, far)
        far_copy.start()

    def x_rows(k, r):
        if not first:
            return x_ref[block(r + k * half_blocks), :]
        return (far_s if k else x_ref)[block(r), :].astype(F32)

    gathers = {}

    def norms(k):
        @pl.loop(0, half_blocks)
        def _(r):
            z, _ = standardize(x_rows(k, r))
            na_s[k, block(r), :] = (z * gain_ref[0:1, :] + shift_ref[0:1, :]).astype(B16)
            nb_s[k, block(r), :] = (z * gain_ref[1:2, :] + shift_ref[1:2, :]).astype(B16)

        gathers[k] = []
        for at, buf in ((0, nb_s), (1, na_s)):
            copy = remote(
                buf.at[k, pl.ds(0, rows), :],
                buf.at[k, pl.ds(rows, rows), :],
                sems,
                1 + 2 * k + at,
                core,
            )
            copy.start()
            gathers[k].append(copy)

    products = {}
    u_out = []

    def feed(k):
        gathers[k][0].wait()
        keep(nb_s.at[k], nb_o.at[pl.ds(k * seq, seq), :], 2 * k)
        for h in (1, 0):
            for copy in u_out:
                copy.wait()
            u_out.clear()

            @pl.loop(0, half_blocks)
            def _(r):
                at = block(r + h * half_blocks)
                u = dot_nn(nb_s[k, at, :], up_ref[...]) + upb_ref[...]
                u_s[r] = u
                hid_s[k, at, :] = gelu(u).astype(B16)

            for r in range(half_blocks):
                copy = pltpu.make_async_copy(
                    u_s.at[r], u_o.at[pl.ds(k * seq + h * rows + r * QB, QB), :], u_sem.at[r]
                )
                copy.start()
                u_out.append(copy)
        keep(hid_s.at[k], hid_o.at[pl.ds(k * seq, seq), :], 2 * k + 1)

    def join(k):
        @pl.loop(0, half_blocks)
        def _(r):
            at = block(r + half_blocks)
            psend[k, block(r), :] = dot_nn(hid_s[k, at, :], down_ref[...]) + dot_nn(
                ctx_s[k, at, :], out_ref[...]
            )

        product = remote(psend.at[k], precv.at[k], sems, 5 + k, core)
        product.start()
        products[k] = product

        @pl.loop(0, half_blocks)
        def _(r):
            at = block(r)
            mine_s[at, :] = dot_nn(hid_s[k, at, :], down_ref[...]) + dot_nn(
                ctx_s[k, at, :], out_ref[...]
            )

        product.wait_recv()

        @pl.loop(0, half_blocks)
        def _(r):
            at = block(r)
            total = precv[k, at, :] + mine_s[at, :]
            if final and k == 0:
                precv[k, at, :] = total
            else:
                ysend[k, at, :] = total.astype(B16)

        if not (final and k == 0):
            sums[k] = remote(ysend.at[k], yrecv.at[1 - k], sems, 7 + k, far)
            sums[k].start()

    sums = {}

    def attend(k):
        gathers[k][1].wait()
        keep(na_s.at[k], na_o.at[pl.ds(k * seq, seq), :], 4 + 2 * k)
        swapped = lambda i: block(lax.rem(i + shift, blocks))

        @pl.loop(0, blocks)
        def _(r):
            acc = dot_nn(na_s[k, swapped(r), :], qkvw_ref[...]) + qkvb_ref[...]
            acc = by_kind(acc, heads)
            turned = rope(
                acc[:, : 2 * w], cos_ref[block(r), :], lo_ref[block(r), :], hi_ref[block(r), :], 1
            )
            qkv_s[k, block(r), : 2 * w] = turned.astype(B16)
            qkv_s[k, block(r), 2 * w :] = acc[:, 2 * w :].astype(B16)
            ctx_s[k, block(r), :] = jnp.zeros((QB, w), B16)
            lse_s[k, block(r), :] = jnp.zeros((QB, 128), F32)

        @pl.loop(0, heads)
        def _(h):
            mine = (lax.broadcasted_iota(jnp.int32, (1, w), 1) // HEAD) == h
            scale = jnp.where(mine, SCALE, 0.0).astype(B16)
            lane = lax.broadcasted_iota(jnp.int32, (QB, 128), 1)
            for i in range(blocks):
                n = (i + 1) * QB
                q = qkv_s[k, i * QB : n, :w] * scale
                s = causal(dot_nt(q, qkv_s[k, :n, w : 2 * w]), n)
                top = jnp.max(s, axis=1, keepdims=True)
                p = jnp.exp(s - top)
                total = jnp.sum(p, axis=1, keepdims=True)
                low = (p * (1.0 / total)).astype(B16)
                c = dot_nn(low, qkv_s[k, :n, 2 * w :])
                old = ctx_s[k, swapped(i), :]
                ctx_s[k, swapped(i), :] = jnp.where(mine, c, old.astype(F32)).astype(B16)
                lse_s[k, i * QB : n, :] = jnp.where(
                    lane == h, top + jnp.log(total), lse_s[k, i * QB : n, :]
                )

        keep(qkv_s.at[k], qkv_o.at[pl.ds(k * seq, seq), :], 5 + 2 * k)
        keep(ctx_s.at[k], ctx_o.at[pl.ds(k * seq, seq), :], 8 + 2 * k)
        keep(lse_s.at[k], lse_o.at[pl.ds(k * seq, seq), :], 9 + 2 * k)

    def finish(k):
        sums[1 - k].wait_recv()

        @pl.loop(0, half_blocks)
        def _(r):
            at = block(r)
            mine = precv[k, at, :] if final else ysend[k, at, :].astype(F32)
            both = mine + yrecv[k, at, :].astype(F32)
            precv[k, at, :] = x_rows(k, r) + (both + ob_ref[...])

        keep(precv.at[k], x_o.at[pl.ds(k * rows, rows), :], 12 + k)

    if first:
        norms(0)
        feed(0)
        attend(0)
        join(0)
        far_copy.wait_recv()
        norms(1)
        feed(1)
        attend(1)
        join(1)
    else:
        norms(1)
        norms(0)
        feed(1)
        attend(1)
        join(1)
        feed(0)
        attend(0)
        join(0)
    if final and not first:
        far_copy.wait_recv()
    if first or final:
        keep(far_s, far_o, 14)
    finish(0)
    if not final:
        finish(1)

    if first or final:
        far_copy.wait_send()
    for copy in u_out + outs:
        copy.wait()
    for copy in products.values():
        copy.wait_send()
    for copy in sums.values():
        copy.wait_send()


def forward_layer(l, layers, x, up, upb, down, qkvw, qkvb, out, ob, gains, shifts, tables, cot):
    first, final = l == 0, l == layers - 1
    features = x.shape[1]
    rows = x.shape[0] if first else x.shape[0] // 2
    seq = 2 * rows
    w = qkvw.shape[1] // 3
    ff = up.shape[1]
    shape = jax.ShapeDtypeStruct
    out_shape = [
        shape((2 * seq, features), B16),
        shape((2 * seq, features), B16),
        shape((2 * seq, ff), F32),
        shape((2 * seq, ff), B16),
        shape((2 * seq, 3 * w), B16),
        shape((2 * seq, w), B16),
        shape((2 * seq, 128), F32),
        shape((rows if final else 2 * rows, features), F32),
    ]
    if first or final:
        out_shape.append(shape((rows, features), B16))
    args = [x, up, upb, down, qkvw, qkvb, out, ob, gains, shifts, *tables]
    if final:
        args.append(cot)
    scratch = [
        pltpu.VMEM((2, seq, features), B16),
        pltpu.VMEM((2, seq, features), B16),
        pltpu.VMEM((rows // QB, QB, ff), F32),
        pltpu.VMEM((2, seq, ff), B16),
        pltpu.VMEM((2, rows, features), F32),
        pltpu.VMEM((2, rows, features), F32),
        pltpu.VMEM((2, rows, features), B16),
        pltpu.VMEM((2, rows, features), B16),
        pltpu.VMEM((2, seq, 3 * w), B16),
        pltpu.VMEM((2, seq, w), B16),
        pltpu.VMEM((2, seq, 128), F32),
    ]
    if first or final:
        scratch.append(pltpu.VMEM((rows, features), B16))
    scratch.append(pltpu.VMEM((rows, features), F32))
    scratch += [DMA((9,)), DMA((9,)), DMA((15,)), DMA((rows // QB,))]
    return pl.pallas_call(
        functools.partial(forward_layer_kernel, first, final, rows, w),
        in_specs=[VMEM] * len(args),
        out_specs=[ANY] * len(out_shape),
        out_shape=out_shape,
        scratch_shapes=scratch,
        compiler_params=pltpu.CompilerParams(
            vmem_limit_bytes=63 * MIB, collective_id=l, has_side_effects=True
        ),
        cost_estimate=pl.CostEstimate(
            flops=2 * 2 * seq * features * (3 * w + 2 * ff + w) * 2,
            bytes_accessed=40 * MIB,
            transcendentals=4 * seq * seq * w // HEAD,
        ),
        name="forward_layer",
    )(*args)


def backward_layer_kernel(first, final, rows, w, *refs):
    it = iter(refs)
    grad_ref, u_ref, down_ref, up_ref, ow_ref, qkvw_ref = (next(it) for _ in range(6))
    qkv_ref, lse_ref, ctx_ref, outall_ref, ob_ref, xn_ref, x_ref = (next(it) for _ in range(7))
    far_ref = next(it) if first else None
    farg_ref = next(it) if final else None
    gain_ref, cos_ref, lo_ref, hi_ref = (next(it) for _ in range(4))
    g_o, dpre_o, dqkv_o = (next(it) for _ in range(3))
    dx_ref, small_ref = (next(it) for _ in range(2))
    g_s, dpre_s, dqkv_s, dq_s, dk_s, dv_s, dctx_s = (next(it) for _ in range(7))
    u_s, bsend, brecv, asend, arecv, zown, ysend, yrecv = (next(it) for _ in range(8))
    cfull, got_s = (next(it) for _ in range(2))
    send, recv, local, u_sem = (next(it) for _ in range(4))
    sems = (send, recv)

    seq = 2 * rows
    ff = up_ref.shape[1]
    heads = w // HEAD
    blocks = seq // QB
    half_blocks = rows // QB
    shift = lax.rem(lax.axis_index("tensor"), 2) * half_blocks
    swapped = lambda i: block(lax.rem(i + shift, blocks))
    core, far = partners()
    diag = lax.rem(core + 2, 4)
    greet((core, far, diag))
    outs = []

    def keep(src, dst, index):
        copy = pltpu.make_async_copy(src, dst, local.at[index])
        copy.start()
        outs.append(copy)

    def load_u(k, i):
        return pltpu.make_async_copy(
            u_ref.at[pl.ds(k * seq + i * QB, QB), :], u_s.at[i % 2], u_sem.at[i % 2]
        )

    small_ref[...] = jnp.zeros_like(small_ref)
    load_u(0, 0).start()
    load_u(0, 1).start()

    @pl.loop(0, half_blocks)
    def _(r):
        low = grad_ref[block(r), :].astype(B16)
        g_s[0, block(r), :] = low
        small_ref[4:5, :] += jnp.sum(low.astype(F32), axis=0, keepdims=True)

    own_half = lambda buf, k: buf.at[k, pl.ds(0, rows), :]
    other_half = lambda buf, k: buf.at[k, pl.ds(rows, rows), :]
    if final:
        g_s[1, :rows, :] = farg_ref[...]
    else:
        across = remote(own_half(g_s, 0), own_half(g_s, 1), sems, 0, far)
        across.start()
    near0 = remote(own_half(g_s, 0), other_half(g_s, 0), sems, 1, core)
    near0.start()
    cfull[:, :w] = ctx_ref[:rows, :]
    contexts = [
        remote(ctx_ref.at[pl.ds(rows, rows), :], cfull.at[:, pl.ds(w, w)], sems, 8, core),
        remote(ctx_ref.at[pl.ds(seq, rows), :], cfull.at[:, pl.ds(2 * w, w)], sems, 9, far),
        remote(ctx_ref.at[pl.ds(seq + rows, rows), :], cfull.at[:, pl.ds(3 * w, w)], sems, 10, diag),
    ]
    for copy in contexts:
        copy.start()

    swaps = {}

    def feed(k):
        for i in range(blocks):
            load_u(k, i).wait()
            at = pl.ds(i * QB, QB)
            d_hidden = dot_nt(g_s[k, at, :], down_ref[...])
            d_pre = (d_hidden * gelu_slope(u_s[i % 2])).astype(B16)
            dpre_s[k, at, :] = d_pre
            small_ref[8:9, :ff] += jnp.sum(d_pre.astype(F32), axis=0, keepdims=True)
            if i + 2 < blocks:
                load_u(k, i + 2).start()
            elif k == 0:
                load_u(1, i + 2 - blocks).start()

        @pl.loop(0, half_blocks)
        def _(r):
            bsend[k, block(r), :] = dot_nt(
                dpre_s[k, block(r + half_blocks), :], up_ref[...]
            ).astype(B16)

        swaps[k] = [remote(bsend.at[k], brecv.at[k], sems, 3 + 2 * k, core)]
        swaps[k][0].start()
        keep(dpre_s.at[k], dpre_o.at[pl.ds(k * seq, seq), :], k)

    def attend(k):
        @pl.loop(0, blocks)
        def _(r):
            dctx_s[block(r), :] = dot_nt(g_s[k, swapped(r), :], ow_ref[...]).astype(B16)
            dq_s[block(r), :] = jnp.zeros((QB, w), F32)
            dk_s[block(r), :] = jnp.zeros((QB, w), F32)
            dv_s[block(r), :] = jnp.zeros((QB, w), F32)

        base = k * seq

        @pl.loop(0, heads)
        def _(h):
            mine = (lax.broadcasted_iota(jnp.int32, (1, w), 1) // HEAD) == h
            scale = jnp.where(mine, SCALE, 0.0).astype(B16)
            only = jnp.where(mine, 1.0, 0.0).astype(B16)
            lane = lax.broadcasted_iota(jnp.int32, (QB, 128), 1)
            for i in range(blocks):
                n = (i + 1) * QB
                q = qkv_ref[base + i * QB : base + n, :w] * scale
                d = dctx_s[i * QB : n, :] * only
                s = causal(dot_nt(q, qkv_ref[base : base + n, w : 2 * w]), n)
                lse = jnp.sum(
                    jnp.where(lane == h, lse_ref[base + i * QB : base + n, :], 0.0),
                    axis=1,
                    keepdims=True,
                )
                p = jnp.exp(s - lse)
                dp = dot_nt(d, qkv_ref[base : base + n, 2 * w :])
                inner = jnp.sum(p * dp, axis=1, keepdims=True)
                ds = (p * (dp - inner)).astype(B16)
                dq_s[i * QB : n, :] += dot_nn(ds, qkv_ref[base : base + n, w : 2 * w] * scale)
                dk_s[:n, :] += dot_tn(ds, q)
                dv_s[:n, :] += dot_tn(p.astype(B16), d)

        @pl.loop(0, blocks)
        def _(r):
            at = block(r)
            qk = jnp.concatenate([dq_s[at, :], dk_s[at, :]], axis=1)
            qk = rope(qk, cos_ref[at, :], lo_ref[at, :], hi_ref[at, :], -1)
            low = by_head(jnp.concatenate([qk, dv_s[at, :]], axis=1), heads).astype(B16)
            dqkv_s[k, swapped(r), :] = low
            small_ref[9:10, : 3 * w] += jnp.sum(low.astype(F32), axis=0, keepdims=True)

        @pl.loop(0, half_blocks)
        def _(r):
            asend[k, block(r), :] = dot_nt(
                dqkv_s[k, block(r + half_blocks), :], qkvw_ref[...]
            ).astype(B16)

        swaps[k].append(remote(asend.at[k], arecv.at[k], sems, 4 + 2 * k, core))
        swaps[k][1].start()
        keep(dqkv_s.at[k], dqkv_o.at[pl.ds(base, seq), :], 2 + k)

    def x_rows(k, r):
        if not first:
            return x_ref[block(r + k * half_blocks), :]
        return (far_ref if k else x_ref)[block(r), :].astype(F32)

    def fold(k):
        for copy in swaps[k]:
            copy.wait()

        @pl.loop(0, half_blocks)
        def _(r):
            at = block(r)
            d_na = dot_nt(dqkv_s[k, at, :], qkvw_ref[...]) + arecv[k, at, :].astype(F32)
            d_nb = dot_nt(dpre_s[k, at, :], up_ref[...]) + brecv[k, at, :].astype(F32)
            z, _ = standardize(x_rows(k, r))
            small_ref[0:1, :] += jnp.sum(d_na * z, axis=0, keepdims=True)
            small_ref[1:2, :] += jnp.sum(d_nb * z, axis=0, keepdims=True)
            small_ref[2:3, :] += jnp.sum(d_na, axis=0, keepdims=True)
            small_ref[3:4, :] += jnp.sum(d_nb, axis=0, keepdims=True)
            d_z = d_na * gain_ref[0:1, :] + d_nb * gain_ref[1:2, :]
            if k == 0:
                zown[at, :] = d_z
            else:
                ysend[at, :] = d_z.astype(B16)

    near0.wait()
    keep(g_s.at[0], g_o.at[pl.ds(0, seq), :], 4)
    feed(0)
    if not final:
        across.wait()
    near1 = remote(own_half(g_s, 1), other_half(g_s, 1), sems, 2, core)
    near1.start()
    near1.wait()
    keep(g_s.at[1], g_o.at[pl.ds(seq, seq), :], 5)
    feed(1)
    attend(1)
    fold(1)
    back = remote(ysend, yrecv, sems, 7, far)
    back.start()
    attend(0)
    fold(0)
    for copy in contexts:
        copy.wait()

    @pl.loop(0, half_blocks)
    def _(r):
        at = block(r)
        attn = dot_nn(cfull[at, :], outall_ref[...]) + ob_ref[...]
        x_next = xn_ref[at, :]
        feed_out = x_next - x_rows(0, r) - attn
        small_ref[5:6, :] += jnp.sum(x_next * x_next, axis=0, keepdims=True)
        small_ref[6:7, :] += jnp.sum(attn * attn, axis=0, keepdims=True)
        small_ref[7:8, :] += jnp.sum(feed_out * feed_out, axis=0, keepdims=True)

    for at, other in ((0, core), (1, far)):
        copy = remote(small_ref.at[pl.ds(0, 8), :], got_s.at[at], sems, 11 + at, other)
        copy.start()
        copy.wait()
        small_ref[0:8, :] += got_s[at]
    back.wait()

    @pl.loop(0, half_blocks)
    def _(r):
        at = block(r)
        total = zown[at, :] + yrecv[at, :].astype(F32)
        z, inverse = standardize(x_rows(0, r))
        slope = total - jnp.mean(total, axis=-1, keepdims=True)
        slope = slope - z * jnp.mean(total * z, axis=-1, keepdims=True)
        dx_ref[at, :] = grad_ref[at, :].astype(F32) + slope * inverse

    for copy in outs:
        copy.wait()


def backward_layer(
    l, layers, grad, u, down, up, out_w, qkvw, qkv, lse, ctx, out_all, ob, xn, x, far_x, far_g, gains, tables
):
    first, final = l == 0, l == layers - 1
    rows, features = grad.shape
    seq = 2 * rows
    w = qkvw.shape[1] // 3
    ff = up.shape[1]
    shape = jax.ShapeDtypeStruct
    args = [grad, u, down, up, out_w, qkvw, qkv, lse, ctx, out_all, ob, xn, x]
    in_specs = [VMEM, ANY] + [VMEM] * 11
    if first:
        args.append(far_x)
        in_specs.append(VMEM)
    if final:
        args.append(far_g)
        in_specs.append(VMEM)
    args += [gains, *tables]
    in_specs += [VMEM] * 4
    out_shape = [
        shape((2 * seq, features), B16),
        shape((2 * seq, ff), B16),
        shape((2 * seq, 3 * w), B16),
        shape((rows, features), F32),
        shape((16, features), F32),
    ]
    half = lambda dtype: pltpu.VMEM((2, rows, features), dtype)
    scratch = [
        pltpu.VMEM((2, seq, features), B16),
        pltpu.VMEM((2, seq, ff), B16),
        pltpu.VMEM((2, seq, 3 * w), B16),
        pltpu.VMEM((seq, w), F32),
        pltpu.VMEM((seq, w), F32),
        pltpu.VMEM((seq, w), F32),
        pltpu.VMEM((seq, w), B16),
        pltpu.VMEM((2, QB, ff), F32),
        half(B16),
        half(B16),
        half(B16),
        half(B16),
        pltpu.VMEM((rows, features), F32),
        pltpu.VMEM((rows, features), B16),
        pltpu.VMEM((rows, features), B16),
        pltpu.VMEM((rows, 4 * w), B16),
        pltpu.VMEM((2, 8, features), F32),
        DMA((13,)),
        DMA((13,)),
        DMA((6,)),
        DMA((2,)),
    ]
    return pl.pallas_call(
        functools.partial(backward_layer_kernel, first, final, rows, w),
        in_specs=in_specs,
        out_specs=[ANY] * 3 + [VMEM] * 2,
        out_shape=out_shape,
        scratch_shapes=scratch,
        compiler_params=pltpu.CompilerParams(
            vmem_limit_bytes=63 * MIB, collective_id=layers + l, has_side_effects=True
        ),
        cost_estimate=pl.CostEstimate(
            flops=2 * 2 * seq * features * (3 * w + 2 * ff + w) * 2,
            bytes_accessed=40 * MIB,
            transcendentals=4 * seq * seq * w // HEAD,
        ),
        name="backward_layer",
    )(*args)


def ring_place(index, size):
    side = lax.rem(index, 2)
    level = index // 2
    return level * (1 - side) + (size - 1 - level) * side


def ring_device(place, size):
    side = place // (size // 2)
    return (1 - side) * 2 * place + side * (2 * (size - 1 - place) + 1)


def ring_sum_kernel(n, shapes, *refs):
    count = len(shapes)
    it = iter(refs)
    ins = [next(it) for _ in range(count)]
    small_in = next(it)
    outs = [next(it) for _ in range(count)]
    small_out = next(it)
    slots = [next(it) for _ in range(count)]
    done = [next(it) for _ in range(count)]
    small_s = next(it)
    send, recv, small_send, small_recv = (next(it) for _ in range(4))

    place = ring_place(lax.axis_index("dp"), n)
    ahead = ring_device(lax.rem(place + 1, n), n)
    behind = ring_device(lax.rem(place + n - 1, n), n)
    barrier = pltpu.get_barrier_semaphore()
    for other in (ahead, behind):
        pl.semaphore_signal(barrier, inc=1, device_id={"dp": other}, device_id_type=MESH)
    pl.semaphore_wait(barrier, 2)

    def rows_of(a, way, step):
        size = shapes[a][0] // (2 * n)
        chunk = lax.rem(place + n - step, n) if way == 0 else lax.rem(place + step, n)
        return pl.ds(pl.multiple_of((chunk * 2 + way) * size, size), size)

    def copy(src, dst, a, way, step):
        return pltpu.make_async_remote_copy(
            src_ref=src,
            dst_ref=dst,
            send_sem=send.at[a, way, step],
            recv_sem=recv.at[a, way, step],
            device_id={"dp": (ahead, behind)[way]},
            device_id_type=MESH,
        )

    def small_copy(step):
        at = lax.rem(place + n - step, n)
        return pltpu.make_async_remote_copy(
            src_ref=small_s.at[at],
            dst_ref=small_s.at[at],
            send_sem=small_send.at[step],
            recv_sem=small_recv.at[step],
            device_id={"dp": ahead},
            device_id_type=MESH,
        )

    small_s[place] = small_in[...]
    flying = []

    def launch(item):
        item.start()
        flying.append(item)
        return item

    last = n - 2
    moving = {}
    for a in range(count):
        for way in (0, 1):
            moving[a, way] = launch(
                copy(ins[a].at[rows_of(a, way, 0), :], slots[a].at[way, 0], a, way, 0)
            )
    small = launch(small_copy(0))
    for step in range(n - 1):
        for a in range(count):
            for way in (0, 1):
                moving[a, way].wait_recv()
                mine = ins[a][rows_of(a, way, step + 1), :].astype(F32)
                total = slots[a][way, step].astype(F32) + mine
                low = total.astype(B16)
                slots[a][way, step] = low
                if step < last:
                    target = slots[a].at[way, step + 1]
                else:
                    target = done[a].at[rows_of(a, way, step + 1), :]
                    outs[a][rows_of(a, way, step + 1), :] = low.astype(F32)
                moving[a, way] = launch(
                    copy(slots[a].at[way, step], target, a, way, step + 1)
                )
        small.wait_recv()
        if step < last:
            small = launch(small_copy(step + 1))
    for step in range(n - 1):
        for a in range(count):
            for way in (0, 1):
                at = rows_of(a, way, step)
                moving[a, way].wait_recv()
                if step < last:
                    moving[a, way] = launch(
                        copy(done[a].at[at, :], done[a].at[at, :], a, way, n + step)
                    )
                outs[a][at, :] = done[a][at, :].astype(F32)
    total = small_s[0]
    for i in range(1, n):
        total = total + small_s[i]
    small_out[...] = total
    for item in flying:
        item.wait_send()


def ring_sum(arrays, small, collective_id):
    n = lax.axis_size("dp")
    shapes = [item.shape for item in arrays]
    shape = jax.ShapeDtypeStruct
    size = sum(a * b for a, b in shapes)
    steps = 2 * n - 2
    return pl.pallas_call(
        functools.partial(ring_sum_kernel, n, shapes),
        in_specs=[VMEM] * (len(arrays) + 1),
        out_specs=[VMEM] * (len(arrays) + 1),
        out_shape=[shape(item, F32) for item in shapes] + [shape(small.shape, F32)],
        scratch_shapes=[pltpu.VMEM((2, n - 1, a // (2 * n), b), B16) for a, b in shapes]
        + [pltpu.VMEM(item, B16) for item in shapes]
        + [pltpu.VMEM((n,) + small.shape, F32)]
        + [DMA((len(arrays), 2, steps))] * 2
        + [DMA((n - 1,))] * 2,
        compiler_params=pltpu.CompilerParams(
            vmem_limit_bytes=56 * MIB, collective_id=collective_id, has_side_effects=True
        ),
        cost_estimate=pl.CostEstimate(
            flops=size, bytes_accessed=400 * MIB, transcendentals=0
        ),
        name="ring_sum",
    )(*arrays, small)


def on_group(
    tokens,
    cotangent,
    qkv_weight,
    qkv_bias,
    out_weight,
    out_bias,
    up_weight,
    up_bias,
    down_weight,
    down_bias,
    norm_gain,
    norm_shift,
):
    rows, features = tokens.shape
    tensor = lax.axis_size("tensor")
    dp = lax.axis_size("dp")
    dp_index = lax.axis_index("dp")
    w = qkv_weight.shape[2] // 3
    ff = up_weight.shape[2]
    tables = rope_tables(SEQ_LEN, 128)

    wide = lambda v: v.astype(F32)

    share = out_weight.shape[1] // dp
    piece = lax.dynamic_slice_in_dim(out_weight, dp_index * share, share, axis=1)
    near = [out_weight, lax.all_gather(swap(piece, "tensor", 2), "dp", axis=1, tiled=True)]
    far = [swap(item, "tensor", 1) for item in near]
    out_all = jnp.concatenate([near[0], far[0], near[1], far[1]], axis=1)

    x = tokens
    stored = []
    far_x = None
    bias_sum = wide(out_bias) + wide(down_bias)
    for l in range(LAYERS):
        got = forward_layer(
            l,
            LAYERS,
            x,
            up_weight[l],
            wide(up_bias[l])[None],
            down_weight[l],
            qkv_weight[l],
            wide(qkv_bias[l])[None],
            out_weight[l],
            bias_sum[l][None],
            wide(norm_gain[l]),
            wide(norm_shift[l]),
            tables,
            cotangent,
        )
        na, nb, u, hidden, qkv, ctx, lse, x_next = got[:8]
        if l == 0:
            far_x = got[8]
        if l == LAYERS - 1:
            far_g = got[8]
        stored.append((x, na, nb, u, hidden, qkv, ctx, lse, x_next))
        x = x_next
    output = x

    grad = cotangent
    big = [None] * LAYERS
    small = [None] * LAYERS
    for l in reversed(range(LAYERS)):
        x, na, nb, u, hidden, qkv, ctx, lse, x_next = stored[l]
        g, d_pre, d_qkv, grad, small[l] = backward_layer(
            l,
            LAYERS,
            grad,
            u,
            down_weight[l],
            up_weight[l],
            out_weight[l],
            qkv_weight[l],
            qkv,
            lse,
            ctx,
            out_all[l],
            wide(out_bias[l])[None],
            x_next,
            x,
            far_x,
            far_g,
            wide(norm_gain[l]),
            tables,
        )
        grads = (dot_tn(hidden, g), dot_tn(nb, d_pre), dot_tn(na, d_qkv), dot_tn(ctx, g))
        grads = tuple(item.astype(B16) for item in grads)
        if l > 0:
            big[l] = [item.astype(F32) for item in lax.psum(grads, "dp")]
        else:
            *big[l], small = ring_sum(grads, jnp.concatenate(small), 2 * LAYERS)
    small = small.reshape(LAYERS, 16, features)
    down_all, up_all, qkv_all, out_w_all = (
        jnp.stack([item[i] for item in big]) for i in range(4)
    )
    layer_stats = jnp.sqrt(jnp.sum(small[:, 5:8], axis=2) / (rows * dp * tensor * features))
    bias_all = small[:, 4]
    return (
        output,
        grad,
        qkv_all,
        small[:, 9, : 3 * w],
        out_w_all,
        bias_all,
        up_all,
        small[:, 8, :ff],
        down_all,
        bias_all,
        small[:, 0:2],
        small[:, 2:4],
        layer_stats,
    )


def solution(mesh):
    in_specs = (
        P(("dp", "tensor"), None),
        P(("dp", "tensor"), None),
        P(None, None, "tensor"),
        P(None, "tensor"),
        P(None, "tensor", None),
        P(),
        P(None, None, "tensor"),
        P(None, "tensor"),
        P(None, "tensor", None),
        P(),
        P(),
        P(),
    )
    out_specs = (
        P(("dp", "tensor"), None),
        P(("dp", "tensor"), None),
        P(None, None, "tensor"),
        P(None, "tensor"),
        P(None, "tensor", None),
        P(),
        P(None, None, "tensor"),
        P(None, "tensor"),
        P(None, "tensor", None),
        P(),
        P(),
        P(),
        P(),
    )
    small = mesh.shape["tensor"] == 4 and mesh.shape["dp"] == 8
    return jax.shard_map(
        on_group if small else on_device,
        mesh=mesh, in_specs=in_specs, out_specs=out_specs, check_vma=False
    )
```

```python
import functools
import math

import jax
import jax.numpy as jnp
from jax import lax
from jax.experimental import pallas as pl
from jax.experimental.pallas import tpu as pltpu
from jax.sharding import PartitionSpec as P

HEAD = 64
ROT = 16
LAYERS = 2
SEQ_LEN = 1024
QB = 256
SCALE = HEAD ** (-0.5)

EPS = 1e-05
NEG = -1e30
F32 = jnp.float32
B16 = jnp.bfloat16
MIB = 1024 * 1024


def dot_nn(left, right):
    return lax.dot_general(left, right, (((1,), (0,)), ((), ())), preferred_element_type=F32)


def dot_nt(left, right):
    return lax.dot_general(left, right, (((1,), (1,)), ((), ())), preferred_element_type=F32)


def dot_tn(left, right):
    return lax.dot_general(left, right, (((0,), (0,)), ((), ())), preferred_element_type=F32)


def rope_tables(seq, width):
    positions = jnp.arange(seq, dtype=jnp.int32).astype(F32)
    inverse = jnp.exp(jnp.arange(ROT // 2, dtype=F32) * (-2.0 * math.log(10000.0) / ROT))
    angles = positions[:, None] * inverse[None, :]
    cosine, sine = jnp.cos(angles), jnp.sin(angles)
    zero = jnp.zeros_like(sine)
    rest = jnp.zeros((seq, HEAD - ROT), F32)
    repeat = lambda parts: jnp.tile(jnp.concatenate(parts, axis=1), (1, width // HEAD))
    return (
        repeat([cosine, cosine, rest + 1.0]),
        repeat([-sine, zero, rest]),
        repeat([zero, sine, rest]),
    )


def rope(rows, cos, sin_lo, sin_hi, sign):
    width = cos.shape[1]
    parts = []
    for j in range(rows.shape[1] // width):
        part = rows[:, j * width : (j + 1) * width]
        turned = (
            pltpu.roll(part, width - ROT // 2, 1) * sin_lo + pltpu.roll(part, ROT // 2, 1) * sin_hi
        )
        parts.append(part * cos + turned if sign > 0 else part * cos - turned)
    return parts[0] if len(parts) == 1 else jnp.concatenate(parts, axis=1)


def attend_forward_kernel(
    w, seq, x_ref, w_ref, b_ref, cos_ref, lo_ref, hi_ref, qkv_ref, ctx_ref, lse_ref
):
    h = pl.program_id(0)
    blocks = seq // QB
    shift = (lax.axis_index("tensor") % 2) * (blocks // 2)
    swapped = lambda i: pl.ds(pl.multiple_of(lax.rem(i + shift, blocks) * QB, QB), QB)

    @pl.when(h == 0)
    def _():
        lse_ref[...] = jnp.zeros_like(lse_ref)
        ctx_ref[...] = jnp.zeros_like(ctx_ref)

        @pl.loop(0, seq // QB)
        def _(r):
            rows = pl.ds(pl.multiple_of(r * QB, QB), QB)
            acc = dot_nn(x_ref[swapped(r), :], w_ref[...]) + b_ref[...]
            turned = rope(acc[:, : 2 * w], cos_ref[rows, :], lo_ref[rows, :], hi_ref[rows, :], 1)
            qkv_ref[rows, : 2 * w] = turned.astype(B16)
            qkv_ref[rows, 2 * w :] = acc[:, 2 * w :].astype(B16)

    mine = (lax.broadcasted_iota(jnp.int32, (1, w), 1) // HEAD) == h
    keep = jnp.where(mine, SCALE, 0.0).astype(B16)
    for i in range(seq // QB):
        n = (i + 1) * QB
        q = qkv_ref[i * QB : n, :w] * keep
        s = dot_nt(q, qkv_ref[:n, w : 2 * w])
        tri = lax.broadcasted_iota(jnp.int32, (QB, QB), 0) >= lax.broadcasted_iota(
            jnp.int32, (QB, QB), 1
        )
        last = jnp.where(tri, s[:, n - QB :], NEG)
        s = last if i == 0 else jnp.concatenate([s[:, : n - QB], last], axis=1)
        top = jnp.max(s, axis=1, keepdims=True)
        p = jnp.exp(s - top)
        total = jnp.sum(p, axis=1, keepdims=True)
        low = (p * (1.0 / total)).astype(B16)
        c = dot_nn(low, qkv_ref[:n, 2 * w :])
        old = ctx_ref[swapped(i), :]
        ctx_ref[swapped(i), :] = jnp.where(mine, c, old.astype(F32)).astype(B16)
        lane = lax.broadcasted_iota(jnp.int32, (QB, 128), 1)
        lse_ref[i * QB : n, :] = jnp.where(lane == h, top + jnp.log(total), lse_ref[i * QB : n, :])


def whole(shape):
    return pl.BlockSpec(shape, lambda h: (0,) * len(shape))


def attend_forward(x, weight, bias, tables):
    seq, features = x.shape
    w = weight.shape[1] // 3
    heads = w // HEAD
    table = tables[0].shape
    return pl.pallas_call(
        functools.partial(attend_forward_kernel, w, seq),
        grid=(heads,),
        in_specs=[
            whole((seq, features)),
            whole((features, 3 * w)),
            whole((1, 3 * w)),
            whole(table),
            whole(table),
            whole(table),
        ],
        out_specs=[whole((seq, 3 * w)), whole((seq, w)), whole((seq, 128))],
        out_shape=[
            jax.ShapeDtypeStruct((seq, 3 * w), B16),
            jax.ShapeDtypeStruct((seq, w), B16),
            jax.ShapeDtypeStruct((seq, 128), F32),
        ],
        compiler_params=pltpu.CompilerParams(
            vmem_limit_bytes=40 * MIB, dimension_semantics=("arbitrary",)
        ),
        cost_estimate=pl.CostEstimate(
            flops=2 * seq * features * 3 * w + 4 * seq * seq * 256 * heads,
            bytes_accessed=2 * seq * features + 6 * features * w + 8 * seq * w,
            transcendentals=seq * seq * heads // 2,
        ),
        name="attend_forward",
    )(x, weight, bias, *tables)


def attend_backward_kernel(
    w,
    seq,
    qkv_ref,
    d_ref,
    lse_ref,
    cos_ref,
    lo_ref,
    hi_ref,
    out_ref,
    bias_ref,
    dq_ref,
    dk_ref,
    dv_ref,
):
    h = pl.program_id(0)
    heads = w // HEAD
    blocks = seq // QB
    shift = (lax.axis_index("tensor") % 2) * (blocks // 2)
    swapped = lambda i: pl.ds(pl.multiple_of(lax.rem(i + shift, blocks) * QB, QB), QB)

    @pl.when(h == 0)
    def _():
        dq_ref[...] = jnp.zeros_like(dq_ref)
        dk_ref[...] = jnp.zeros_like(dk_ref)
        dv_ref[...] = jnp.zeros_like(dv_ref)

    mine = (lax.broadcasted_iota(jnp.int32, (1, w), 1) // HEAD) == h
    keep = jnp.where(mine, SCALE, 0.0).astype(B16)
    keep_value = jnp.where(mine, 1.0, 0.0).astype(B16)
    for i in range(seq // QB):
        n = (i + 1) * QB
        q = qkv_ref[i * QB : n, :w] * keep
        d = d_ref[swapped(i), :] * keep_value
        s = dot_nt(q, qkv_ref[:n, w : 2 * w])
        lane = lax.broadcasted_iota(jnp.int32, (QB, 128), 1)
        lse = jnp.sum(jnp.where(lane == h, lse_ref[i * QB : n, :], 0.0), axis=1, keepdims=True)
        tri = lax.broadcasted_iota(jnp.int32, (QB, QB), 0) >= lax.broadcasted_iota(
            jnp.int32, (QB, QB), 1
        )
        last = jnp.where(tri, s[:, n - QB :], NEG)
        s = last if i == 0 else jnp.concatenate([s[:, : n - QB], last], axis=1)
        p = jnp.exp(s - lse)
        dp = dot_nt(d, qkv_ref[:n, 2 * w :])
        inner = jnp.sum(p * dp, axis=1, keepdims=True)
        ds = (p * (dp - inner)).astype(B16)
        dq_ref[i * QB : n, :] += dot_nn(ds, qkv_ref[:n, w : 2 * w] * keep)
        dk_ref[:n, :] += dot_tn(ds, q)
        dv_ref[:n, :] += dot_tn(p.astype(B16), d)

    @pl.when(h == heads - 1)
    def _():
        bias_ref[...] = jnp.zeros_like(bias_ref)

        @pl.loop(0, seq // QB)
        def _(r):
            rows = pl.ds(pl.multiple_of(r * QB, QB), QB)
            qk = jnp.concatenate([dq_ref[rows, :], dk_ref[rows, :]], axis=1)
            qk = rope(qk, cos_ref[rows, :], lo_ref[rows, :], hi_ref[rows, :], -1).astype(B16)
            v = dv_ref[rows, :].astype(B16)
            out_ref[swapped(r), : 2 * w] = qk
            out_ref[swapped(r), 2 * w :] = v
            bias_ref[:, : 2 * w] += jnp.sum(qk.astype(F32), axis=0, keepdims=True)
            bias_ref[:, 2 * w :] += jnp.sum(v.astype(F32), axis=0, keepdims=True)


def attend_backward(qkv, d_context, lse, tables):
    seq = qkv.shape[0]
    w = qkv.shape[1] // 3
    heads = w // HEAD
    table = tables[0].shape
    return pl.pallas_call(
        functools.partial(attend_backward_kernel, w, seq),
        grid=(heads,),
        in_specs=[
            whole((seq, 3 * w)),
            whole((seq, w)),
            whole((seq, 128)),
            whole(table),
            whole(table),
            whole(table),
        ],
        out_specs=[whole((seq, 3 * w)), whole((1, 3 * w))],
        out_shape=[
            jax.ShapeDtypeStruct((seq, 3 * w), B16),
            jax.ShapeDtypeStruct((1, 3 * w), F32),
        ],
        scratch_shapes=[pltpu.VMEM((seq, w), F32)] * 3,
        compiler_params=pltpu.CompilerParams(
            vmem_limit_bytes=40 * MIB, dimension_semantics=("arbitrary",)
        ),
        cost_estimate=pl.CostEstimate(
            flops=10 * seq * seq * 256 * heads,
            bytes_accessed=16 * seq * w,
            transcendentals=seq * seq * heads // 2,
        ),
        name="attend_backward",
    )(qkv, d_context, lse, *tables)


def normal_parts(u):
    x = jnp.abs(u) * (0.5**0.5)
    t = 1.0 / (1.0 + 0.3275911 * x)
    bell = jnp.exp(-0.5 * u * u)
    poly = t * (
        0.254829592
        + t * (-0.284496736 + t * (1.421413741 + t * (-1.453152027 + t * 1.061405429)))
    )
    half_tail = 0.5 * poly * bell
    return jnp.where(u >= 0.0, 1.0 - half_tail, half_tail), bell


def gelu(u):
    return u * normal_parts(u)[0]


def gelu_slope(u):
    share, bell = normal_parts(u)
    return share + u * bell * ((2.0 * math.pi) ** -0.5)


def standardize(x):
    average = jnp.mean(x, axis=-1, keepdims=True)
    centred = x - average
    variance = jnp.mean(centred * centred, axis=-1, keepdims=True)
    inverse = lax.rsqrt(variance + EPS)
    return centred * inverse, inverse


def swap(x, axis, bit):
    size = lax.axis_size(axis)
    return lax.ppermute(x, axis, [(i, i ^ bit) for i in range(size)])


def all_bits(size):
    bits = []
    bit = 1
    while bit < size:
        bits.append(bit)
        bit *= 2
    return bits


def after(x, *others):
    return lax.optimization_barrier((x,) + others)[0]


def on_device(
    tokens,
    cotangent,
    qkv_weight,
    qkv_bias,
    out_weight,
    out_bias,
    up_weight,
    up_bias,
    down_weight,
    down_bias,
    norm_gain,
    norm_shift,
):
    rows, features = tokens.shape
    tensor = lax.axis_size("tensor")
    dp = lax.axis_size("dp")
    chips = tensor // 2
    dp_index = lax.axis_index("dp")
    core = lax.axis_index("tensor") % 2
    w = qkv_weight.shape[2] // 3
    ff = up_weight.shape[2]
    heads = w // HEAD
    tables = rope_tables(SEQ_LEN, min(128, 2 * w))
    streams = range(chips)
    chip_bits = all_bits(chips)
    dp_bits = all_bits(dp)

    def core_gather(half):
        return jnp.concatenate([half, swap(half, "tensor", 1)], axis=0)

    def chip_gather(half):
        found = [half]
        for bit in chip_bits:
            found = found + [swap(item, "tensor", 2 * bit) for item in found]
        return found

    def chip_scatter(parts):
        for bit in reversed(chip_bits):
            sent = [swap(part.astype(B16), "tensor", 2 * bit) for part in parts[bit:]]
            parts = [part + got.astype(F32) for part, got in zip(parts[:bit], sent)]
        return parts[0]

    def chip_reduce(parts):
        for bit in chip_bits:
            low = [part.astype(B16) for part in parts]
            sent = [swap(part, "tensor", 2 * bit) for part in low]
            parts = [low[k].astype(F32) + sent[k ^ bit].astype(F32) for k in range(len(parts))]
        return parts

    def core_product(left, right, dot):
        got = swap(dot(left[rows:], right), "tensor", 1)
        return dot(left[:rows], right) + got

    def regroup(columns, back):
        lead = columns.shape[:-1]
        order = (3, heads, HEAD) if back else (heads, 3, HEAD)
        return jnp.swapaxes(columns.reshape(lead + order), -3, -2).reshape(columns.shape)

    qkv_w = [regroup(qkv_weight[l], False) for l in range(LAYERS)]
    qkv_b = [regroup(qkv_bias[l].astype(F32), False)[None] for l in range(LAYERS)]

    share = out_weight.shape[1] // dp
    piece = lax.dynamic_slice_in_dim(out_weight, dp_index * share, share, axis=1)
    near = [out_weight]
    for j in range(1, chips):
        near.append(lax.all_gather(swap(piece, "tensor", 2 * j), "dp", axis=1, tiled=True))
    far = [swap(item, "tensor", 1) for item in near]
    out_all = jnp.concatenate([x for pair in zip(near, far) for x in pair], axis=1)

    x_half = [t.astype(F32) for t in chip_gather(tokens)]
    stored = []
    stat_terms = []
    tick = tokens
    for l in range(LAYERS):
        final = l == LAYERS - 1
        gains = norm_gain[l].astype(F32)
        shifts = norm_shift[l].astype(F32)
        order = list(streams) if l == 0 else list(reversed(streams))
        na, nb, pre, hidden, ffn, qkv, ctx, lse, near = ([None] * chips for _ in range(9))
        up_b = up_bias[l].astype(F32)

        def feed(k):
            u = dot_nn(nb[k], up_weight[l]) + up_b
            pre[k] = u
            hidden[k] = gelu(u).astype(B16)
            ffn[k] = core_product(hidden[k], down_weight[l], dot_nn)

        def attend(k):
            qkv[k], ctx[k], lse[k] = attend_forward(na[k], qkv_w[l], qkv_b[l], tables)
            got = swap(ctx[k][rows:], "tensor", 1)
            near[k] = jnp.concatenate([ctx[k][:rows], got], axis=1)

        for k in order:
            z, _ = standardize(x_half[k])
            na[k] = core_gather((z * gains[0] + shifts[0]).astype(B16))
            nb[k] = core_gather((z * gains[1] + shifts[1]).astype(B16))
        if l == 0:
            for k in order:
                nb[k] = after(nb[k], tick)
                feed(k)
                na[k] = after(na[k], hidden[k])
                attend(k)
                tick = ctx[k]
        else:
            for k in order:
                nb[k] = after(nb[k], tick)
                feed(k)
                tick = hidden[k]
            for k in order:
                na[k] = after(na[k], tick)
                attend(k)
                tick = ctx[k]
        if final:
            ffn = [chip_scatter(ffn)]
        else:
            ffn = chip_reduce(ffn)
        x_next = []
        for k in streams if not final else range(1):
            blocks = [near[k]] + [swap(near[k ^ j], "tensor", 2 * j) for j in range(1, chips)]
            attn = dot_nn(jnp.concatenate(blocks, axis=1), out_all[l]) + out_bias[l].astype(F32)
            ffn_out = ffn[k] + down_bias[l].astype(F32)
            x_next.append(x_half[k] + attn + ffn_out)
            if k == 0:
                stat_terms.append(
                    jnp.stack(
                        [
                            jnp.sum(x_next[0] * x_next[0]),
                            jnp.sum(attn * attn),
                            jnp.sum(ffn_out * ffn_out),
                        ]
                    )
                )
        stored.append((x_half, na, nb, pre, hidden, qkv, ctx, lse))
        if l == 0:
            grad_low_half = chip_gather(after(cotangent, x_next[0]))
        x_half = x_next
    output = x_half[0]

    grad = cotangent.astype(F32)
    big = [None] * LAYERS
    small_all = [None] * LAYERS
    small_dp = [None] * LAYERS
    summed = None
    for l in reversed(range(LAYERS)):
        x_half, na, nb, pre, hidden, qkv, ctx, lse = stored[l]
        gains = norm_gain[l].astype(F32)
        low = grad.astype(B16)
        if l < LAYERS - 1:
            grad_low_half = chip_gather(low)
        g = [core_gather(item) for item in grad_low_half]
        g[0] = after(g[0], tick)
        d_pre, d_qkv, d_z = [None] * chips, [None] * chips, [None] * chips
        down_g = sum(dot_tn(hidden[k], g[k]) for k in streams)
        up_bias_g = jnp.zeros((ff,), F32)
        qkv_bias_g = jnp.zeros((1, 3 * w), F32)
        sums = 0.0
        for k in streams:
            d_pre[k] = (dot_nt(g[k], down_weight[l]) * gelu_slope(pre[k])).astype(B16)
            up_bias_g = up_bias_g + jnp.sum(d_pre[k], axis=0, dtype=F32)
        up_g = sum(dot_tn(nb[k], d_pre[k]) for k in streams)
        first = (down_g.astype(B16), up_g.astype(B16))
        if summed is not None:
            first = lax.optimization_barrier(first + summed[:1])[:2]
        first = lax.psum(first, "dp")
        tick = up_g
        for k in reversed(streams):
            d_ctx = dot_nt(g[k], out_weight[l]).astype(B16)
            d_qkv[k], bias_k = attend_backward(qkv[k], after(d_ctx, tick), lse[k], tables)
            tick = d_qkv[k]
            qkv_bias_g = qkv_bias_g + bias_k
            d_na = core_product(d_qkv[k], qkv_w[l], dot_nt)
            d_nb = core_product(d_pre[k], up_weight[l], dot_nt)
            z, inverse = standardize(x_half[k])
            sums = sums + jnp.stack(
                [
                    jnp.sum(d_na * z, axis=0),
                    jnp.sum(d_nb * z, axis=0),
                    jnp.sum(d_na, axis=0),
                    jnp.sum(d_nb, axis=0),
                ]
            )
            d_z[k] = d_na * gains[0] + d_nb * gains[1]
        total = chip_scatter(d_z)
        slope = total - jnp.mean(total, axis=-1, keepdims=True)
        slope = slope - z * jnp.mean(total * z, axis=-1, keepdims=True)
        bias_g = jnp.sum(low, axis=0, dtype=F32)
        grad = grad + slope * inverse
        out_g = sum(dot_tn(ctx[k], g[k]) for k in streams)
        qkv_g = sum(dot_tn(na[k], d_qkv[k]) for k in streams)
        second = (qkv_g.astype(B16), out_g.astype(B16))
        second = lax.optimization_barrier(second + first[:1])[:2]
        second = lax.psum(second, "dp")
        small_all[l] = jnp.concatenate(
            [sums, bias_g[None], jnp.pad(stat_terms[l], (0, features - 3))[None]], axis=0
        )
        small_dp[l] = jnp.concatenate([up_bias_g, qkv_bias_g[0]])
        big[l] = first + second
        summed = second
    small = jnp.stack(small_all)
    for bit in all_bits(tensor):
        small = small + swap(small, "tensor", bit)
    vector = jnp.stack(small_dp)
    for bit in dp_bits:
        small = small + swap(small, "dp", bit)
        vector = vector + swap(vector, "dp", bit)
    down_all = jnp.stack([item[0] for item in big]).astype(F32)
    up_all = jnp.stack([item[1] for item in big]).astype(F32)
    qkv_all = jnp.stack([regroup(item[2], True) for item in big]).astype(F32)
    out_w_all = jnp.stack([item[3] for item in big]).astype(F32)
    layer_stats = jnp.sqrt(small[:, 5, :3] / (rows * dp * tensor * features))
    bias_all = small[:, 4]
    return (
        output,
        grad,
        qkv_all,
        regroup(vector[:, ff:], True),
        out_w_all,
        bias_all,
        up_all,
        vector[:, :ff],
        down_all,
        bias_all,
        small[:, 0:2],
        small[:, 2:4],
        layer_stats,
    )


MESH = pl.DeviceIdType.MESH
ANY = pl.BlockSpec(memory_space=pl.ANY)
VMEM = pl.BlockSpec(memory_space=pltpu.VMEM)
DMA = pltpu.SemaphoreType.DMA


def partners():
    me = lax.axis_index("tensor")
    return me + 1 - 2 * lax.rem(me, 2), lax.rem(me + 2, 4)


def greet(others, more=0):
    barrier = pltpu.get_barrier_semaphore()
    for other in others:
        pl.semaphore_signal(barrier, inc=1, device_id={"tensor": other}, device_id_type=MESH)
    pl.semaphore_wait(barrier, len(others) + more)


def remote(src, dst, sems, index, target):
    return pltpu.make_async_remote_copy(
        src_ref=src,
        dst_ref=dst,
        send_sem=sems[0].at[index],
        recv_sem=sems[1].at[index],
        device_id={"tensor": target},
        device_id_type=MESH,
    )


def block(i, size=QB):
    return pl.ds(pl.multiple_of(i * size, size), size)


def loader(sems, **pairs):
    waiting = {}
    for i, (name, (src, dst)) in enumerate(pairs.items()):
        waiting[name] = pltpu.make_async_copy(src, dst, sems.at[i])
        waiting[name].start()

    def need(*names):
        for name in names:
            if name in waiting:
                waiting.pop(name).wait()

    return need


def by_kind(rows, heads):
    return jnp.concatenate(
        [
            rows[:, (3 * h + j) * HEAD : (3 * h + j + 1) * HEAD]
            for j in range(3)
            for h in range(heads)
        ],
        axis=1,
    )


def by_head(rows, heads):
    return jnp.concatenate(
        [
            rows[:, (heads * j + h) * HEAD : (heads * j + h + 1) * HEAD]
            for h in range(heads)
            for j in range(3)
        ],
        axis=1,
    )


def causal(s, n):
    tri = lax.broadcasted_iota(jnp.int32, (QB, QB), 0) >= lax.broadcasted_iota(
        jnp.int32, (QB, QB), 1
    )
    last = jnp.where(tri, s[:, n - QB :], NEG)
    return last if n == QB else jnp.concatenate([s[:, : n - QB], last], axis=1)


def forward_layer_kernel(l, first, final, rows, w, *refs):
    it = iter(refs)
    x_ref, up_h, down_h, qkvw_h, out_h, cos_h, lo_h, hi_h = (next(it) for _ in range(8))
    upb_ref, qkvb_ref, ob_ref, gain_ref, shift_ref = (next(it) for _ in range(5))
    cot_ref = next(it) if final else None
    na_o, nb_o, u_o, hid_o, qkv_o, ctx_o, lse_o, x_o = (next(it) for _ in range(8))
    far_o = next(it) if first or final else None
    na_s, nb_s, u_s, hid_s, psend, precv, ysend, yrecv = (next(it) for _ in range(8))
    qkv_s, ctx_s, lse_s = (next(it) for _ in range(3))
    far_s = next(it) if first or final else None
    mine_s = next(it)
    up_ref, down_ref, qkvw_ref, out_ref, cos_ref, lo_ref, hi_ref = (next(it) for _ in range(7))
    send, recv, local, u_sem, load_sem = (next(it) for _ in range(5))
    sems = (send, recv)
    need = loader(
        load_sem,
        up=(up_h.at[l], up_ref),
        qkvw=(qkvw_h.at[l], qkvw_ref),
        cos=(cos_h, cos_ref),
        lo=(lo_h, lo_ref),
        hi=(hi_h, hi_ref),
        down=(down_h.at[l], down_ref),
        out=(out_h.at[l], out_ref),
    )

    seq = 2 * rows
    heads = w // HEAD
    blocks = seq // QB
    half_blocks = rows // QB
    shift = lax.rem(lax.axis_index("tensor"), 2) * half_blocks
    core, far = partners()
    greet((core, far))
    outs = []

    def keep(src, dst, index):
        copy = pltpu.make_async_copy(src, dst, local.at[index])
        copy.start()
        outs.append(copy)

    far_copy = None
    if first or final:
        far_copy = remote(x_ref if first else cot_ref, far_s, sems, 0, far)
        far_copy.start()

    def x_rows(k, r):
        if not first:
            return x_ref[block(r + k * half_blocks), :]
        return (far_s if k else x_ref)[block(r), :].astype(F32)

    gathers = {}

    def norms(k):
        @pl.loop(0, half_blocks)
        def _(r):
            z, _ = standardize(x_rows(k, r))
            na_s[k, block(r), :] = (z * gain_ref[0:1, :] + shift_ref[0:1, :]).astype(B16)
            nb_s[k, block(r), :] = (z * gain_ref[1:2, :] + shift_ref[1:2, :]).astype(B16)

        gathers[k] = []
        for at, buf in ((0, nb_s), (1, na_s)):
            copy = remote(
                buf.at[k, pl.ds(0, rows), :],
                buf.at[k, pl.ds(rows, rows), :],
                sems,
                1 + 2 * k + at,
                core,
            )
            copy.start()
            gathers[k].append(copy)

    products = {}
    u_out = []

    def feed(k):
        gathers[k][0].wait()
        need("up")
        keep(nb_s.at[k], nb_o.at[pl.ds(k * seq, seq), :], 2 * k)
        for h in (1, 0):
            for copy in u_out:
                copy.wait()
            u_out.clear()

            @pl.loop(0, half_blocks)
            def _(r):
                at = block(r + h * half_blocks)
                u = dot_nn(nb_s[k, at, :], up_ref[...]) + upb_ref[...]
                u_s[r] = u
                hid_s[k, at, :] = gelu(u).astype(B16)

            for r in range(half_blocks):
                copy = pltpu.make_async_copy(
                    u_s.at[r], u_o.at[pl.ds(k * seq + h * rows + r * QB, QB), :], u_sem.at[r]
                )
                copy.start()
                u_out.append(copy)
        keep(hid_s.at[k], hid_o.at[pl.ds(k * seq, seq), :], 2 * k + 1)

    def join(k):
        need("down", "out")

        @pl.loop(0, half_blocks)
        def _(r):
            at = block(r + half_blocks)
            psend[k, block(r), :] = dot_nn(hid_s[k, at, :], down_ref[...]) + dot_nn(
                ctx_s[k, at, :], out_ref[...]
            )

        product = remote(psend.at[k], precv.at[k], sems, 5 + k, core)
        product.start()
        products[k] = product

        @pl.loop(0, half_blocks)
        def _(r):
            at = block(r)
            mine_s[at, :] = dot_nn(hid_s[k, at, :], down_ref[...]) + dot_nn(
                ctx_s[k, at, :], out_ref[...]
            )

        product.wait_recv()

        @pl.loop(0, half_blocks)
        def _(r):
            at = block(r)
            total = precv[k, at, :] + mine_s[at, :]
            precv[k, at, :] = total
            if not (final and k == 0):
                ysend[k, at, :] = total.astype(B16)

        if not (final and k == 0):
            sums[k] = remote(ysend.at[k], yrecv.at[1 - k], sems, 7 + k, far)
            sums[k].start()

    sums = {}

    def attend(k):
        gathers[k][1].wait()
        need("qkvw", "cos", "lo", "hi")
        keep(na_s.at[k], na_o.at[pl.ds(k * seq, seq), :], 4 + 2 * k)
        swapped = lambda i: block(lax.rem(i + shift, blocks))

        @pl.loop(0, blocks)
        def _(r):
            acc = dot_nn(na_s[k, swapped(r), :], qkvw_ref[...]) + qkvb_ref[...]
            acc = by_kind(acc, heads)
            turned = rope(
                acc[:, : 2 * w], cos_ref[block(r), :], lo_ref[block(r), :], hi_ref[block(r), :], 1
            )
            qkv_s[k, block(r), : 2 * w] = turned.astype(B16)
            qkv_s[k, block(r), 2 * w :] = acc[:, 2 * w :].astype(B16)
            ctx_s[k, block(r), :] = jnp.zeros((QB, w), B16)
            lse_s[k, block(r), :] = jnp.zeros((QB, 128), F32)

        @pl.loop(0, heads)
        def _(h):
            mine = (lax.broadcasted_iota(jnp.int32, (1, w), 1) // HEAD) == h
            scale = jnp.where(mine, SCALE, 0.0).astype(B16)
            lane = lax.broadcasted_iota(jnp.int32, (QB, 128), 1)
            for i in range(blocks):
                n = (i + 1) * QB
                q = qkv_s[k, i * QB : n, :w] * scale
                s = causal(dot_nt(q, qkv_s[k, :n, w : 2 * w]), n)
                top = jnp.max(s, axis=1, keepdims=True)
                p = jnp.exp(s - top)
                total = jnp.sum(p, axis=1, keepdims=True)
                low = (p * (1.0 / total)).astype(B16)
                c = dot_nn(low, qkv_s[k, :n, 2 * w :])
                old = ctx_s[k, swapped(i), :]
                ctx_s[k, swapped(i), :] = jnp.where(mine, c, old.astype(F32)).astype(B16)
                lse_s[k, i * QB : n, :] = jnp.where(
                    lane == h, top + jnp.log(total), lse_s[k, i * QB : n, :]
                )

        keep(qkv_s.at[k], qkv_o.at[pl.ds(k * seq, seq), :], 5 + 2 * k)
        keep(ctx_s.at[k], ctx_o.at[pl.ds(k * seq, seq), :], 8 + 2 * k)
        keep(lse_s.at[k], lse_o.at[pl.ds(k * seq, seq), :], 9 + 2 * k)

    def finish(k):
        sums[1 - k].wait_recv()

        @pl.loop(0, half_blocks)
        def _(r):
            at = block(r)
            both = precv[k, at, :] + yrecv[k, at, :].astype(F32)
            precv[k, at, :] = x_rows(k, r) + (both + ob_ref[...])

        keep(precv.at[k], x_o.at[pl.ds(k * rows, rows), :], 12 + k)

    if first:
        norms(0)
        feed(0)
        attend(0)
        join(0)
        far_copy.wait_recv()
        norms(1)
        feed(1)
        attend(1)
        join(1)
    else:
        norms(1)
        norms(0)
        feed(1)
        attend(1)
        join(1)
        feed(0)
        attend(0)
        join(0)
    if final and not first:
        far_copy.wait_recv()
    if first or final:
        keep(far_s, far_o, 14)
    finish(0)
    if not final:
        finish(1)

    if first or final:
        far_copy.wait_send()
    for copy in u_out + outs:
        copy.wait()
    for copy in products.values():
        copy.wait_send()
    for copy in sums.values():
        copy.wait_send()


def forward_layer(l, layers, x, up, down, qkvw, out, tables, upb, qkvb, ob, gains, shifts, cot):
    first, final = l == 0, l == layers - 1
    features = x.shape[1]
    rows = x.shape[0] if first else x.shape[0] // 2
    seq = 2 * rows
    w = qkvw.shape[2] // 3
    ff = up.shape[2]
    shape = jax.ShapeDtypeStruct
    out_shape = [
        shape((2 * seq, features), B16),
        shape((2 * seq, features), B16),
        shape((2 * seq, ff), F32),
        shape((2 * seq, ff), B16),
        shape((2 * seq, 3 * w), B16),
        shape((2 * seq, w), B16),
        shape((2 * seq, 128), F32),
        shape((rows if final else 2 * rows, features), F32),
    ]
    if first or final:
        out_shape.append(shape((rows, features), B16))
    args = [x, up, down, qkvw, out, *tables, upb, qkvb, ob, gains, shifts]
    if final:
        args.append(cot)
    scratch = [
        pltpu.VMEM((2, seq, features), B16),
        pltpu.VMEM((2, seq, features), B16),
        pltpu.VMEM((rows // QB, QB, ff), F32),
        pltpu.VMEM((2, seq, ff), B16),
        pltpu.VMEM((2, rows, features), F32),
        pltpu.VMEM((2, rows, features), F32),
        pltpu.VMEM((2, rows, features), B16),
        pltpu.VMEM((2, rows, features), B16),
        pltpu.VMEM((2, seq, 3 * w), B16),
        pltpu.VMEM((2, seq, w), B16),
        pltpu.VMEM((2, seq, 128), F32),
    ]
    if first or final:
        scratch.append(pltpu.VMEM((rows, features), B16))
    scratch.append(pltpu.VMEM((rows, features), F32))
    scratch += [pltpu.VMEM(item.shape[1:], B16) for item in (up, down, qkvw, out)]
    scratch += [pltpu.VMEM(item.shape, F32) for item in tables]
    scratch += [DMA((9,)), DMA((9,)), DMA((15,)), DMA((rows // QB,)), DMA((7,))]
    return pl.pallas_call(
        functools.partial(forward_layer_kernel, l, first, final, rows, w),
        in_specs=[VMEM] + [ANY] * 7 + [VMEM] * (len(args) - 8),
        out_specs=[ANY] * len(out_shape),
        out_shape=out_shape,
        scratch_shapes=scratch,
        compiler_params=pltpu.CompilerParams(
            vmem_limit_bytes=63 * MIB, collective_id=l, has_side_effects=True
        ),
        cost_estimate=pl.CostEstimate(
            flops=2 * 2 * seq * features * (3 * w + 2 * ff + w) * 2,
            bytes_accessed=40 * MIB,
            transcendentals=4 * seq * seq * w // HEAD,
        ),
        name="forward_layer",
    )(*args)


def ring_place(index, size):
    side = lax.rem(index, 2)
    level = index // 2
    return level * (1 - side) + (size - 1 - level) * side


def ring_device(place, size):
    side = place // (size // 2)
    return (1 - side) * 2 * place + side * (2 * (size - 1 - place) + 1)


class Ring:
    def __init__(self, n):
        self.n = n
        self.place = ring_place(lax.axis_index("dp"), n)
        self.targets = (
            ring_device(lax.rem(self.place + 1, n), n),
            ring_device(lax.rem(self.place + n - 1, n), n),
        )
        far = n // 2
        self.routes = ((0, 0, far), (0, 1, n - 1 - far), (1, 0, n - 1 - far), (1, 1, far))

    def greet(self):
        barrier = pltpu.get_barrier_semaphore()
        for other in self.targets:
            pl.semaphore_signal(barrier, inc=1, device_id={"dp": other}, device_id_type=MESH)

    def rows(self, array, half, offset):
        size = array.shape[0] // (2 * self.n)
        chunk = lax.rem(self.place + offset + 2 * self.n, self.n)
        return pl.ds(pl.multiple_of((chunk * 2 + half) * size, size), size)

    def copy(self, src, dst, sems, at, way):
        return pltpu.make_async_remote_copy(
            src_ref=src,
            dst_ref=dst,
            send_sem=sems[0].at[at],
            recv_sem=sems[1].at[at],
            device_id={"dp": self.targets[way]},
            device_id_type=MESH,
        )


class Scatter:
    def __init__(self, ring, ins, chunk, it):
        self.ring, self.ins, self.chunk = ring, ins, chunk
        self.slots = [next(it) for _ in ins]
        self.mine = [next(it) for _ in ins]
        self.sems = (next(it), next(it))
        self.load = next(it)
        self.parts = [(a, m) for a in range(len(ins)) for m in range(4)]

    @staticmethod
    def scratch(n, shapes):
        count = len(shapes)
        size = lambda a: a // (2 * n)
        return (
            [pltpu.VMEM((4, n // 2, size(a), b), B16) for a, b in shapes]
            + [pltpu.VMEM((4, size(a), b), B16) for a, b in shapes]
            + [DMA((count, 4, n // 2)), DMA((count, 4, n // 2)), DMA((count, 4))]
        )

    def sent(self, a, m, step):
        half, way, steps = self.ring.routes[m]
        offset = steps - step
        if step:
            src = self.slots[a].at[m, step - 1]
        else:
            src = self.ins[a].at[self.ring.rows(self.ins[a], half, -offset if way else offset), :]
        return self.ring.copy(src, self.slots[a].at[m, step], self.sems, (a, m, step), way)

    def fetch(self, a, m, step):
        half, way, steps = self.ring.routes[m]
        offset = steps - step - 1
        return pltpu.make_async_copy(
            self.ins[a].at[self.ring.rows(self.ins[a], half, -offset if way else offset), :],
            self.mine[a].at[m],
            self.load.at[a, m],
        )

    def start(self):
        for a, m in self.parts:
            self.sent(a, m, 0).start()
        for a, m in self.parts:
            self.fetch(a, m, 0).start()

    def step(self, step):
        for a, m in self.parts:
            half, way, steps = self.ring.routes[m]
            if step >= steps:
                continue
            self.sent(a, m, step).wait_recv()
            if step + 1 < steps:
                self.fetch(a, m, step).wait()
                total = self.slots[a][m, step].astype(F32) + self.mine[a][m].astype(F32)
                self.slots[a][m, step] = total.astype(B16)
                self.sent(a, m, step + 1).start()
                if way == 0 or step + 2 < steps:
                    self.fetch(a, m, step + 1).start()
        if step == self.ring.n // 2 - 1:
            for a in range(len(self.ins)):
                for half in (0, 1):
                    m, other = 2 * half, 2 * half + 1
                    self.fetch(a, m, self.ring.routes[m][2] - 1).wait()
                    total = self.mine[a][m].astype(F32)
                    for route in (m, other):
                        last = self.ring.routes[route][2] - 1
                        total = total + self.slots[a][route, last].astype(F32)
                    size = total.shape[0]
                    self.chunk[a][half * size : (half + 1) * size, :] = total.astype(B16)

    def finish(self):
        for a, m in self.parts:
            for step in range(self.ring.routes[m][2]):
                self.sent(a, m, step).wait_send()


class Gather:
    def __init__(self, ring, chunk, done, it):
        self.ring, self.chunk, self.done = ring, chunk, done
        self.sems = (next(it), next(it))
        self.local = next(it)
        self.parts = [(a, m) for a in range(len(chunk)) for m in range(4)]

    @staticmethod
    def scratch(n, count):
        return [DMA((count, 4, n // 2)), DMA((count, 4, n // 2)), DMA((count, 2))]

    def sent(self, a, m, step):
        half, way, steps = self.ring.routes[m]
        at = self.ring.rows(self.done[a], half, step if way else -step)
        size = self.done[a].shape[0] // (2 * self.ring.n)
        src = self.done[a].at[at, :] if step else self.chunk[a].at[pl.ds(half * size, size), :]
        return self.ring.copy(src, self.done[a].at[at, :], self.sems, (a, m, step), way)

    def own(self, a, half):
        size = self.done[a].shape[0] // (2 * self.ring.n)
        return pltpu.make_async_copy(
            self.chunk[a].at[pl.ds(half * size, size), :],
            self.done[a].at[self.ring.rows(self.done[a], half, 0), :],
            self.local.at[a, half],
        )

    def start(self):
        for a, m in self.parts:
            self.sent(a, m, 0).start()
        for a in range(len(self.chunk)):
            for half in (0, 1):
                self.own(a, half).start()

    def step(self, step):
        for a, m in self.parts:
            steps = self.ring.routes[m][2]
            if step < steps:
                self.sent(a, m, step).wait_recv()
                if step + 1 < steps:
                    self.sent(a, m, step + 1).start()

    def finish(self):
        for a, m in self.parts:
            for step in range(self.ring.routes[m][2]):
                self.sent(a, m, step).wait_send()
        for a in range(len(self.chunk)):
            for half in (0, 1):
                self.own(a, half).wait()


def last_sums_kernel(n, *refs):
    it = iter(refs)
    ready = [next(it) for _ in range(2)]
    ins = [next(it) for _ in range(2)]
    small_in = next(it)
    done = [next(it) for _ in range(4)]
    small_out = next(it)
    ring = Ring(n)
    chunk = [next(it) for _ in range(2)]
    first = Gather(ring, ready, done[:2], it)
    sums = Scatter(ring, ins, chunk, it)
    second = Gather(ring, chunk, done[2:], it)
    small_s, small_send, small_recv = (next(it) for _ in range(3))
    ring.greet()
    pl.semaphore_wait(pltpu.get_barrier_semaphore(), 2)

    def small_copy(step):
        at = lax.rem(ring.place + n - step, n)
        return pltpu.make_async_remote_copy(
            src_ref=small_s.at[at],
            dst_ref=small_s.at[at],
            send_sem=small_send.at[step],
            recv_sem=small_recv.at[step],
            device_id={"dp": ring.targets[0]},
            device_id_type=MESH,
        )

    small_s[ring.place] = small_in[...]
    sums.start()
    small_copy(0).start()
    first.start()
    for step in range(n // 2):
        sums.step(step)
        if step == n // 2 - 1:
            second.start()
        first.step(step)
        small_copy(step).wait_recv()
        small_copy(step + 1).start()
    for step in range(n // 2):
        second.step(step)
        if n // 2 + step < n - 1:
            small_copy(n // 2 + step).wait_recv()
            if n // 2 + step < n - 2:
                small_copy(n // 2 + step + 1).start()
    total = small_s[0]
    for i in range(1, n):
        total = total + small_s[i]
    small_out[...] = total
    for part in (first, sums, second):
        part.finish()
    for step in range(n - 1):
        small_copy(step).wait_send()


def last_sums(ready, arrays, small, collective_id):
    n = lax.axis_size("dp")
    shape = jax.ShapeDtypeStruct
    shapes = [item.shape for item in arrays]
    full = [(item.shape[0] * n, item.shape[1]) for item in ready] + shapes
    size = sum(a * b for a, b in full)
    return pl.pallas_call(
        functools.partial(last_sums_kernel, n),
        in_specs=[ANY] * 4 + [VMEM],
        out_specs=[ANY] * 4 + [VMEM],
        out_shape=[shape(item, B16) for item in full] + [shape(small.shape, F32)],
        scratch_shapes=[pltpu.VMEM((a // n, b), B16) for a, b in shapes]
        + Gather.scratch(n, 2)
        + Scatter.scratch(n, shapes)
        + Gather.scratch(n, 2)
        + [pltpu.VMEM((n,) + small.shape, F32)]
        + [DMA((n - 1,))] * 2,
        compiler_params=pltpu.CompilerParams(
            vmem_limit_bytes=40 * MIB, collective_id=collective_id, has_side_effects=True
        ),
        cost_estimate=pl.CostEstimate(flops=size, bytes_accessed=400 * MIB, transcendentals=0),
        name="last_sums",
    )(*ready, *arrays, small)


def backward_layer_kernel(l, first, final, rows, w, n, *refs):
    it = iter(refs)
    grad_ref, u_ref, down_h, up_h, ow_h, qkvw_h = (next(it) for _ in range(6))
    outall_h, cos_h, lo_h, hi_h = (next(it) for _ in range(4))
    qkv_h, lse_h, ctx_ref, xn_h, x_ref = (next(it) for _ in range(5))
    far_ref = next(it) if first else None
    farg_ref = next(it) if final else None
    gain_ref, ob_ref = (next(it) for _ in range(2))
    hid_h, nb_h, na_h = (next(it) for _ in range(3))
    ready = [next(it) for _ in range(4)] if first else []
    dx_o, small_ref = (next(it) for _ in range(2))
    wide_g = [next(it) for _ in range(2)]
    narrow_g = [next(it) for _ in range(2)]
    chunk_ref = [next(it) for _ in range(2)]
    done = [next(it) for _ in range(4)] if first else []
    g_s, dpre_s, dqkv_s, dq_s, dk_s, dv_s, dctx_s = (next(it) for _ in range(7))
    u_s, osend, brecv, arecv, ysend, yrecv = (next(it) for _ in range(6))
    cfull, got_s = (next(it) for _ in range(2))
    down_ref, up_ref, ow_ref, qkvw_ref, outall_ref = (next(it) for _ in range(5))
    cos_ref, lo_ref, hi_ref, qkv_ref, lse_ref = (next(it) for _ in range(5))
    send, recv, local, u_sem, load_sem = (next(it) for _ in range(5))
    sems = (send, recv)
    a_s, o_s, a_sem, o_sem = (next(it) for _ in range(4))
    ring = Ring(n)
    wide_sum = Scatter(ring, wide_g, chunk_ref, it)
    if first:
        chunk_s = [next(it) for _ in range(2)]
        wide_last = Gather(ring, ready[:2], done[:2], it)
        narrow_sum = Scatter(ring, ready[2:], chunk_s, it)
        narrow_last = Gather(ring, chunk_s, done[2:], it)
    need = loader(
        load_sem,
        down=(down_h.at[l], down_ref),
        up=(up_h.at[l], up_ref),
        ow=(ow_h.at[l], ow_ref),
        qkv=(qkv_h, qkv_ref),
        lse=(lse_h, lse_ref),
        cos=(cos_h, cos_ref),
        lo=(lo_h, lo_ref),
        hi=(hi_h, hi_ref),
        qkvw=(qkvw_h.at[l], qkvw_ref),
        outall=(outall_h.at[l], outall_ref),
    )

    seq = 2 * rows
    ff = up_ref.shape[1]
    heads = w // HEAD
    blocks = seq // QB
    half_blocks = rows // QB
    shift = lax.rem(lax.axis_index("tensor"), 2) * half_blocks
    swapped = lambda i: block(lax.rem(i + shift, blocks))
    core, far = partners()
    diag = lax.rem(core + 2, 4)
    ring.greet()
    greet((core, far, diag), 2)
    def load_u(k, i):
        return pltpu.make_async_copy(
            u_ref.at[pl.ds(k * seq + i * QB, QB), :], u_s.at[i % 2], u_sem.at[i % 2]
        )

    small_ref[...] = jnp.zeros_like(small_ref)
    load_u(0, 0).start()
    load_u(0, 1).start()

    @pl.loop(0, half_blocks)
    def _(r):
        low = grad_ref[block(r), :].astype(B16)
        g_s[0, block(r), :] = low
        small_ref[4:5, :] += jnp.sum(low.astype(F32), axis=0, keepdims=True)

    own_half = lambda buf, k: buf.at[k, pl.ds(0, rows), :]
    other_half = lambda buf, k: buf.at[k, pl.ds(rows, rows), :]
    if final:
        g_s[1, :rows, :] = farg_ref[...]
    else:
        across = remote(own_half(g_s, 0), own_half(g_s, 1), sems, 0, far)
        across.start()
    near0 = remote(own_half(g_s, 0), other_half(g_s, 0), sems, 1, core)
    near0.start()
    if first:
        wide_last.start()
        narrow_sum.start()
    cfull[:, :w] = ctx_ref[:rows, :]
    contexts = [
        remote(ctx_ref.at[pl.ds(rows, rows), :], cfull.at[:, pl.ds(w, w)], sems, 8, core),
        remote(ctx_ref.at[pl.ds(seq, rows), :], cfull.at[:, pl.ds(2 * w, w)], sems, 9, far),
        remote(ctx_ref.at[pl.ds(seq + rows, rows), :], cfull.at[:, pl.ds(3 * w, w)], sems, 10, diag),
    ]
    for copy in contexts:
        copy.start()

    swaps = {}

    def feed(k):
        need("down")
        for i in range(blocks):
            load_u(k, i).wait()
            at = pl.ds(i * QB, QB)
            d_hidden = dot_nt(g_s[k, at, :], down_ref[...])
            d_pre = (d_hidden * gelu_slope(u_s[i % 2])).astype(B16)
            dpre_s[k, at, :] = d_pre
            small_ref[8:9, :ff] += jnp.sum(d_pre.astype(F32), axis=0, keepdims=True)
            if i + 2 < blocks:
                load_u(k, i + 2).start()
            elif k == 0:
                load_u(1, i + 2 - blocks).start()

        need("up")
        if k == 1:
            swaps[0][0].wait_send()

        @pl.loop(0, half_blocks)
        def _(r):
            osend[block(r), :] = dot_nt(dpre_s[k, block(r + half_blocks), :], up_ref[...])

        swaps[k] = [remote(osend, brecv.at[k], sems, 3 + 2 * k, core)]
        swaps[k][0].start()

    def attend(k, pump):
        need("ow", "qkv", "lse", "cos", "lo", "hi", "qkvw")

        @pl.loop(0, blocks)
        def _(r):
            dctx_s[block(r), :] = dot_nt(g_s[k, swapped(r), :], ow_ref[...]).astype(B16)
            dq_s[block(r), :] = jnp.zeros((QB, w), F32)
            dk_s[block(r), :] = jnp.zeros((QB, w), F32)
            dv_s[block(r), :] = jnp.zeros((QB, w), F32)

        base = k * seq

        @pl.loop(0, heads)
        def _(h):
            mine = (lax.broadcasted_iota(jnp.int32, (1, w), 1) // HEAD) == h
            scale = jnp.where(mine, SCALE, 0.0).astype(B16)
            only = jnp.where(mine, 1.0, 0.0).astype(B16)
            lane = lax.broadcasted_iota(jnp.int32, (QB, 128), 1)
            for i in range(blocks):
                n = (i + 1) * QB
                q = qkv_ref[base + i * QB : base + n, :w] * scale
                d = dctx_s[i * QB : n, :] * only
                s = causal(dot_nt(q, qkv_ref[base : base + n, w : 2 * w]), n)
                lse = jnp.sum(
                    jnp.where(lane == h, lse_ref[base + i * QB : base + n, :], 0.0),
                    axis=1,
                    keepdims=True,
                )
                p = jnp.exp(s - lse)
                dp = dot_nt(d, qkv_ref[base : base + n, 2 * w :])
                inner = jnp.sum(p * dp, axis=1, keepdims=True)
                ds = (p * (dp - inner)).astype(B16)
                dq_s[i * QB : n, :] += dot_nn(ds, qkv_ref[base : base + n, w : 2 * w] * scale)
                dk_s[:n, :] += dot_tn(ds, q)
                dv_s[:n, :] += dot_tn(p.astype(B16), d)
            pump(h)

        @pl.loop(0, blocks)
        def _(r):
            at = block(r)
            qk = jnp.concatenate([dq_s[at, :], dk_s[at, :]], axis=1)
            qk = rope(qk, cos_ref[at, :], lo_ref[at, :], hi_ref[at, :], -1)
            low = by_head(jnp.concatenate([qk, dv_s[at, :]], axis=1), heads).astype(B16)
            dqkv_s[k, swapped(r), :] = low
            small_ref[9:10, : 3 * w] += jnp.sum(low.astype(F32), axis=0, keepdims=True)

        swaps[1][1 - k].wait_send()

        @pl.loop(0, half_blocks)
        def _(r):
            osend[block(r), :] = dot_nt(dqkv_s[k, block(r + half_blocks), :], qkvw_ref[...])

        swaps[k].append(remote(osend, arecv.at[k], sems, 4 + 2 * k, core))
        swaps[k][1].start()

    def x_rows(k, r):
        if not first:
            return x_ref[block(r + k * half_blocks), :]
        return (far_ref if k else x_ref)[block(r), :].astype(F32)

    def fold(k):
        for copy in swaps[k]:
            copy.wait_recv()

        @pl.loop(0, half_blocks)
        def _(r):
            at = block(r)
            d_na = dot_nt(dqkv_s[k, at, :], qkvw_ref[...]) + arecv[k, at, :]
            d_nb = dot_nt(dpre_s[k, at, :], up_ref[...]) + brecv[k, at, :]
            z, _ = standardize(x_rows(k, r))
            small_ref[0:1, :] += jnp.sum(d_na * z, axis=0, keepdims=True)
            small_ref[1:2, :] += jnp.sum(d_nb * z, axis=0, keepdims=True)
            small_ref[2:3, :] += jnp.sum(d_na, axis=0, keepdims=True)
            small_ref[3:4, :] += jnp.sum(d_nb, axis=0, keepdims=True)
            d_z = d_na * gain_ref[0:1, :] + d_nb * gain_ref[1:2, :]
            if k == 0:
                arecv[0, at, :] = d_z
            else:
                ysend[at, :] = d_z.astype(B16)

    def weight_grad(left, right, out):
        tiles = left.shape[1] // QB
        width = out.shape[1]

        def load(i):
            slot = lax.rem(i, 2)
            return pltpu.make_async_copy(left.at[:, block(i)], a_s.at[slot], a_sem.at[slot])

        def store(i):
            slot = lax.rem(i, 2)
            return pltpu.make_async_copy(
                o_s.at[slot, :, pl.ds(0, width)], out.at[block(i), :], o_sem.at[slot]
            )

        load(0).start()

        @pl.loop(0, tiles)
        def _(i):
            slot = lax.rem(i, 2)
            load(i).wait()

            @pl.when(i + 1 < tiles)
            def _():
                load(i + 1).start()

            @pl.when(i >= 2)
            def _():
                store(i - 2).wait()

            total = dot_tn(a_s[slot, :seq, :], right[0]) + dot_tn(a_s[slot, seq:, :], right[1])
            o_s[slot, :, :width] = total.astype(B16)
            store(i).start()

        for i in range(max(tiles - 2, 0), tiles):
            store(i).wait()

    def at_heads(**calls):
        def pump(h):
            for name, todo in calls.items():

                @pl.when(h == int(name[1:]))
                def _():
                    todo()

        return pump

    near0.wait()
    feed(0)
    if first:
        narrow_sum.step(0)
        across.wait()
    near1 = remote(own_half(g_s, 1), other_half(g_s, 1), sems, 2, core)
    near1.start()
    if first:
        wide_last.step(0)
    near1.wait()
    feed(1)
    if first:
        narrow_sum.step(1)
    weight_grad(hid_h, g_s, wide_g[0])
    if first:
        wide_last.step(1)
    weight_grad(nb_h, dpre_s, wide_g[1])
    wide_sum.start()
    if first:
        narrow_sum.step(2)

        def later():
            wide_last.step(2)
            narrow_sum.step(3)
            narrow_last.start()

        attend(1, at_heads(h2=later))
    else:
        attend(1, at_heads(h2=lambda: wide_sum.step(0)))
    fold(1)
    back = remote(ysend, yrecv, sems, 7, far)
    back.start()
    next_rows = pltpu.make_async_copy(xn_h.at[pl.ds(0, rows), :], arecv.at[1], local.at[0])
    next_rows.start()
    if first:
        wide_sum.step(0)

        def later():
            wide_last.step(3)
            narrow_last.step(0)
            wide_sum.step(1)

        attend(0, at_heads(h2=later))
        narrow_last.step(1)
    else:
        wide_sum.step(1)
        attend(0, at_heads(h2=lambda: wide_sum.step(2)))
    fold(0)
    if first:
        wide_sum.step(2)
        narrow_last.step(2)
    else:
        wide_sum.step(3)
    weight_grad(na_h, dqkv_s, narrow_g[0])
    weight_grad(ctx_ref, g_s, narrow_g[1])
    if first:
        wide_sum.step(3)
        narrow_last.step(3)
    need("outall")
    next_rows.wait()
    for copy in contexts:
        copy.wait()

    @pl.loop(0, half_blocks)
    def _(r):
        at = block(r)
        attn = dot_nn(cfull[at, :], outall_ref[...]) + ob_ref[...]
        x_next = arecv[1, at, :]
        feed_out = x_next - x_rows(0, r) - attn
        small_ref[5:6, :] += jnp.sum(x_next * x_next, axis=0, keepdims=True)
        small_ref[6:7, :] += jnp.sum(attn * attn, axis=0, keepdims=True)
        small_ref[7:8, :] += jnp.sum(feed_out * feed_out, axis=0, keepdims=True)

    for at, other in ((0, core), (1, far)):
        copy = remote(small_ref.at[pl.ds(0, 8), :], got_s.at[at], sems, 11 + at, other)
        copy.start()
        copy.wait()
        small_ref[0:8, :] += got_s[at]
    back.wait()

    @pl.loop(0, half_blocks)
    def _(r):
        at = block(r)
        total = arecv[0, at, :] + yrecv[at, :].astype(F32)
        z, inverse = standardize(x_rows(0, r))
        slope = total - jnp.mean(total, axis=-1, keepdims=True)
        slope = slope - z * jnp.mean(total * z, axis=-1, keepdims=True)
        arecv[0, at, :] = grad_ref[at, :].astype(F32) + slope * inverse

    grad_out = pltpu.make_async_copy(arecv.at[0], dx_o, local.at[1])
    grad_out.start()
    swaps[0][1].wait_send()
    wide_sum.finish()
    if first:
        wide_last.finish()
        narrow_sum.finish()
        narrow_last.finish()
    grad_out.wait()


def backward_layer(
    l,
    layers,
    grad,
    u,
    down,
    up,
    out_w,
    qkvw,
    out_all,
    tables,
    qkv,
    lse,
    ctx,
    xn,
    x,
    far_x,
    far_g,
    gains,
    ob,
    hidden,
    nb,
    na,
    ready,
):
    first, final = l == 0, l == layers - 1
    rows, features = grad.shape
    seq = 2 * rows
    w = qkvw.shape[2] // 3
    ff = up.shape[2]
    n = lax.axis_size("dp")
    wide_shapes = [(ff, features), (features, ff)]
    narrow_shapes = [(features, 3 * w), (w, features)]
    shape = jax.ShapeDtypeStruct
    args = [grad, u, down, up, out_w, qkvw, out_all, *tables, qkv, lse, ctx, xn, x]
    in_specs = [VMEM] + [ANY] * 11 + [VMEM, ANY, VMEM]
    if first:
        args.append(far_x)
        in_specs.append(VMEM)
    if final:
        args.append(far_g)
        in_specs.append(VMEM)
    args += [gains, ob, hidden, nb, na, *ready]
    in_specs += [VMEM] * 2 + [ANY] * (3 + len(ready))
    low = lambda shapes: [shape(item, B16) for item in shapes]
    chunks = [(a // n, b) for a, b in wide_shapes]
    out_shape = [shape((rows, features), F32), shape((16, features), F32)]
    out_shape += low(wide_shapes + narrow_shapes + chunks)
    out_specs = [ANY, VMEM] + [ANY] * 4 + [VMEM] * 2
    if first:
        out_shape += low(wide_shapes + narrow_shapes)
        out_specs += [ANY] * 4
    scratch = [
        pltpu.VMEM((2, seq, features), B16),
        pltpu.VMEM((2, seq, ff), B16),
        pltpu.VMEM((2, seq, 3 * w), B16),
        pltpu.VMEM((seq, w), F32),
        pltpu.VMEM((seq, w), F32),
        pltpu.VMEM((seq, w), F32),
        pltpu.VMEM((seq, w), B16),
        pltpu.VMEM((2, QB, ff), F32),
        pltpu.VMEM((rows, features), F32),
        pltpu.VMEM((2, rows, features), F32),
        pltpu.VMEM((2, rows, features), F32),
        pltpu.VMEM((rows, features), B16),
        pltpu.VMEM((rows, features), B16),
        pltpu.VMEM((rows, 4 * w), B16),
        pltpu.VMEM((2, 8, features), F32),
    ]
    scratch += [pltpu.VMEM(item.shape[1:], B16) for item in (down, up, out_w, qkvw, out_all)]
    scratch += [pltpu.VMEM(item.shape, F32) for item in tables]
    scratch += [pltpu.VMEM(qkv.shape, B16), pltpu.VMEM(lse.shape, F32)]
    scratch += [DMA((13,)), DMA((13,)), DMA((2,)), DMA((2,)), DMA((10,))]
    scratch += [pltpu.VMEM((2, 2 * seq, QB), B16), pltpu.VMEM((2, QB, features), B16)]
    scratch += [DMA((2,)), DMA((2,))]
    scratch += Scatter.scratch(n, wide_shapes)
    if first:
        scratch += [pltpu.VMEM((a // n, b), B16) for a, b in narrow_shapes]
        scratch += Gather.scratch(n, 2)
        scratch += Scatter.scratch(n, narrow_shapes)
        scratch += Gather.scratch(n, 2)
    return pl.pallas_call(
        functools.partial(backward_layer_kernel, l, first, final, rows, w, n),
        in_specs=in_specs,
        out_specs=out_specs,
        out_shape=out_shape,
        scratch_shapes=scratch,
        compiler_params=pltpu.CompilerParams(
            vmem_limit_bytes=63 * MIB, collective_id=layers + l, has_side_effects=True
        ),
        cost_estimate=pl.CostEstimate(
            flops=2 * 2 * seq * features * (3 * w + 2 * ff + w) * 2,
            bytes_accessed=40 * MIB,
            transcendentals=4 * seq * seq * w // HEAD,
        ),
        name="backward_layer",
    )(*args)


def on_group(
    tokens,
    cotangent,
    qkv_weight,
    qkv_bias,
    out_weight,
    out_bias,
    up_weight,
    up_bias,
    down_weight,
    down_bias,
    norm_gain,
    norm_shift,
):
    rows, features = tokens.shape
    tensor = lax.axis_size("tensor")
    dp = lax.axis_size("dp")
    dp_index = lax.axis_index("dp")
    w = qkv_weight.shape[2] // 3
    ff = up_weight.shape[2]
    tables = rope_tables(SEQ_LEN, 128)

    wide = lambda v: v.astype(F32)

    share = out_weight.shape[1] // dp
    piece = lax.dynamic_slice_in_dim(out_weight, dp_index * share, share, axis=1)
    near = [out_weight, lax.all_gather(swap(piece, "tensor", 2), "dp", axis=1, tiled=True)]
    far = [swap(item, "tensor", 1) for item in near]
    out_all = jnp.concatenate([near[0], far[0], near[1], far[1]], axis=1)

    x = tokens
    stored = []
    far_x = None
    bias_sum = wide(out_bias) + wide(down_bias)
    for l in range(LAYERS):
        got = forward_layer(
            l,
            LAYERS,
            x,
            up_weight,
            down_weight,
            qkv_weight,
            out_weight,
            tables,
            wide(up_bias[l])[None],
            wide(qkv_bias[l])[None],
            bias_sum[l][None],
            wide(norm_gain[l]),
            wide(norm_shift[l]),
            cotangent,
        )
        na, nb, u, hidden, qkv, ctx, lse, x_next = got[:8]
        if l == 0:
            far_x = got[8]
        if l == LAYERS - 1:
            far_g = got[8]
        stored.append((x, na, nb, u, hidden, qkv, ctx, lse, x_next))
        x = x_next
    output = x

    grad = cotangent
    big = [None] * LAYERS
    ready = ()
    small = [None] * LAYERS
    for l in reversed(range(LAYERS)):
        x, na, nb, u, hidden, qkv, ctx, lse, x_next = stored[l]
        grad, small[l], *found = backward_layer(
            l,
            LAYERS,
            grad,
            u,
            down_weight,
            up_weight,
            out_weight,
            qkv_weight,
            out_all,
            tables,
            qkv,
            lse,
            ctx,
            x_next,
            x,
            far_x,
            far_g,
            wide(norm_gain[l]),
            wide(out_bias[l])[None],
            hidden,
            nb,
            na,
            ready,
        )
        ready = (*found[4:6], *found[2:4])
        if l < LAYERS - 1:
            big[l + 1] = found[6:]
    *big[0], small = last_sums(ready[:2], ready[2:], jnp.concatenate(small), 2 * LAYERS)
    small = small.reshape(LAYERS, 16, features)
    down_all, up_all, qkv_all, out_w_all = (
        jnp.stack([item[i] for item in big]).astype(F32) for i in range(4)
    )
    layer_stats = jnp.sqrt(jnp.sum(small[:, 5:8], axis=2) / (rows * dp * tensor * features))
    bias_all = small[:, 4]
    return (
        output,
        grad,
        qkv_all,
        small[:, 9, : 3 * w],
        out_w_all,
        bias_all,
        up_all,
        small[:, 8, :ff],
        down_all,
        bias_all,
        small[:, 0:2],
        small[:, 2:4],
        layer_stats,
    )


def solution(mesh):
    in_specs = (
        P(("dp", "tensor"), None),
        P(("dp", "tensor"), None),
        P(None, None, "tensor"),
        P(None, "tensor"),
        P(None, "tensor", None),
        P(),
        P(None, None, "tensor"),
        P(None, "tensor"),
        P(None, "tensor", None),
        P(),
        P(),
        P(),
    )
    out_specs = (
        P(("dp", "tensor"), None),
        P(("dp", "tensor"), None),
        P(None, None, "tensor"),
        P(None, "tensor"),
        P(None, "tensor", None),
        P(),
        P(None, None, "tensor"),
        P(None, "tensor"),
        P(None, "tensor", None),
        P(),
        P(),
        P(),
        P(),
    )
    small = mesh.shape["tensor"] == 4 and mesh.shape["dp"] == 8
    return jax.shard_map(
        on_group if small else on_device,
        mesh=mesh, in_specs=in_specs, out_specs=out_specs, check_vma=False
    )
```

```python
import functools
import math

import jax
import jax.numpy as jnp
import numpy as np
from jax import lax
from jax.experimental import pallas as pl
from jax.experimental.pallas import tpu as pltpu
from jax.sharding import PartitionSpec as P

HEAD = 64
ROT = 16
LAYERS = 2
SEQ_LEN = 1024
QB = 256
SCALE = HEAD ** (-0.5)

EPS = 1e-05
NEG = -1e30
F32 = jnp.float32
B16 = jnp.bfloat16
MIB = 1024 * 1024


def dot_nn(left, right):
    return lax.dot_general(left, right, (((1,), (0,)), ((), ())), preferred_element_type=F32)


def dot_nt(left, right):
    return lax.dot_general(left, right, (((1,), (1,)), ((), ())), preferred_element_type=F32)


def dot_tn(left, right):
    return lax.dot_general(left, right, (((0,), (0,)), ((), ())), preferred_element_type=F32)


def rope_tables(seq, width):
    positions = np.arange(seq, dtype=np.float32)
    inverse = np.exp(np.arange(ROT // 2, dtype=np.float32) * (-2.0 * math.log(10000.0) / ROT))
    angles = (positions[:, None] * inverse.astype(np.float32)[None, :]).astype(np.float64)
    cosine, sine = np.cos(angles), np.sin(angles)
    zero = np.zeros_like(sine)
    rest = np.zeros((seq, HEAD - ROT))
    repeat = lambda parts: jnp.asarray(
        np.tile(np.concatenate(parts, axis=1), (1, width // HEAD)).astype(np.float32)
    )
    return (
        repeat([cosine, cosine, rest + 1.0]),
        repeat([-sine, zero, rest]),
        repeat([zero, sine, rest]),
    )


def rope(rows, cos, sin_lo, sin_hi, sign):
    width = cos.shape[1]
    parts = []
    for j in range(rows.shape[1] // width):
        part = rows[:, j * width : (j + 1) * width]
        turned = (
            pltpu.roll(part, width - ROT // 2, 1) * sin_lo + pltpu.roll(part, ROT // 2, 1) * sin_hi
        )
        parts.append(part * cos + turned if sign > 0 else part * cos - turned)
    return parts[0] if len(parts) == 1 else jnp.concatenate(parts, axis=1)


def attend_forward_kernel(
    w, seq, x_ref, w_ref, b_ref, cos_ref, lo_ref, hi_ref, qkv_ref, ctx_ref, lse_ref
):
    h = pl.program_id(0)
    blocks = seq // QB
    shift = (lax.axis_index("tensor") % 2) * (blocks // 2)
    swapped = lambda i: pl.ds(pl.multiple_of(lax.rem(i + shift, blocks) * QB, QB), QB)

    @pl.when(h == 0)
    def _():
        lse_ref[...] = jnp.zeros_like(lse_ref)
        ctx_ref[...] = jnp.zeros_like(ctx_ref)

        @pl.loop(0, seq // QB)
        def _(r):
            rows = pl.ds(pl.multiple_of(r * QB, QB), QB)
            acc = dot_nn(x_ref[swapped(r), :], w_ref[...]) + b_ref[...]
            turned = rope(acc[:, : 2 * w], cos_ref[rows, :], lo_ref[rows, :], hi_ref[rows, :], 1)
            qkv_ref[rows, : 2 * w] = turned.astype(B16)
            qkv_ref[rows, 2 * w :] = acc[:, 2 * w :].astype(B16)

    mine = (lax.broadcasted_iota(jnp.int32, (1, w), 1) // HEAD) == h
    keep = jnp.where(mine, SCALE, 0.0).astype(B16)
    for i in range(seq // QB):
        n = (i + 1) * QB
        q = qkv_ref[i * QB : n, :w] * keep
        s = dot_nt(q, qkv_ref[:n, w : 2 * w])
        tri = lax.broadcasted_iota(jnp.int32, (QB, QB), 0) >= lax.broadcasted_iota(
            jnp.int32, (QB, QB), 1
        )
        last = jnp.where(tri, s[:, n - QB :], NEG)
        s = last if i == 0 else jnp.concatenate([s[:, : n - QB], last], axis=1)
        top = jnp.max(s, axis=1, keepdims=True)
        p = jnp.exp(s - top)
        total = jnp.sum(p, axis=1, keepdims=True)
        low = (p * (1.0 / total)).astype(B16)
        c = dot_nn(low, qkv_ref[:n, 2 * w :])
        old = ctx_ref[swapped(i), :]
        ctx_ref[swapped(i), :] = jnp.where(mine, c, old.astype(F32)).astype(B16)
        lane = lax.broadcasted_iota(jnp.int32, (QB, 128), 1)
        lse_ref[i * QB : n, :] = jnp.where(lane == h, top + jnp.log(total), lse_ref[i * QB : n, :])


def whole(shape):
    return pl.BlockSpec(shape, lambda h: (0,) * len(shape))


def attend_forward(x, weight, bias, tables):
    seq, features = x.shape
    w = weight.shape[1] // 3
    heads = w // HEAD
    table = tables[0].shape
    return pl.pallas_call(
        functools.partial(attend_forward_kernel, w, seq),
        grid=(heads,),
        in_specs=[
            whole((seq, features)),
            whole((features, 3 * w)),
            whole((1, 3 * w)),
            whole(table),
            whole(table),
            whole(table),
        ],
        out_specs=[whole((seq, 3 * w)), whole((seq, w)), whole((seq, 128))],
        out_shape=[
            jax.ShapeDtypeStruct((seq, 3 * w), B16),
            jax.ShapeDtypeStruct((seq, w), B16),
            jax.ShapeDtypeStruct((seq, 128), F32),
        ],
        compiler_params=pltpu.CompilerParams(
            vmem_limit_bytes=40 * MIB, dimension_semantics=("arbitrary",)
        ),
        cost_estimate=pl.CostEstimate(
            flops=2 * seq * features * 3 * w + 4 * seq * seq * 256 * heads,
            bytes_accessed=2 * seq * features + 6 * features * w + 8 * seq * w,
            transcendentals=seq * seq * heads // 2,
        ),
        name="attend_forward",
    )(x, weight, bias, *tables)


def attend_backward_kernel(
    w,
    seq,
    qkv_ref,
    d_ref,
    lse_ref,
    cos_ref,
    lo_ref,
    hi_ref,
    out_ref,
    bias_ref,
    dq_ref,
    dk_ref,
    dv_ref,
):
    h = pl.program_id(0)
    heads = w // HEAD
    blocks = seq // QB
    shift = (lax.axis_index("tensor") % 2) * (blocks // 2)
    swapped = lambda i: pl.ds(pl.multiple_of(lax.rem(i + shift, blocks) * QB, QB), QB)

    @pl.when(h == 0)
    def _():
        dq_ref[...] = jnp.zeros_like(dq_ref)
        dk_ref[...] = jnp.zeros_like(dk_ref)
        dv_ref[...] = jnp.zeros_like(dv_ref)

    mine = (lax.broadcasted_iota(jnp.int32, (1, w), 1) // HEAD) == h
    keep = jnp.where(mine, SCALE, 0.0).astype(B16)
    keep_value = jnp.where(mine, 1.0, 0.0).astype(B16)
    for i in range(seq // QB):
        n = (i + 1) * QB
        q = qkv_ref[i * QB : n, :w] * keep
        d = d_ref[swapped(i), :] * keep_value
        s = dot_nt(q, qkv_ref[:n, w : 2 * w])
        lane = lax.broadcasted_iota(jnp.int32, (QB, 128), 1)
        lse = jnp.sum(jnp.where(lane == h, lse_ref[i * QB : n, :], 0.0), axis=1, keepdims=True)
        tri = lax.broadcasted_iota(jnp.int32, (QB, QB), 0) >= lax.broadcasted_iota(
            jnp.int32, (QB, QB), 1
        )
        last = jnp.where(tri, s[:, n - QB :], NEG)
        s = last if i == 0 else jnp.concatenate([s[:, : n - QB], last], axis=1)
        p = jnp.exp(s - lse)
        dp = dot_nt(d, qkv_ref[:n, 2 * w :])
        inner = jnp.sum(p * dp, axis=1, keepdims=True)
        ds = (p * (dp - inner)).astype(B16)
        dq_ref[i * QB : n, :] += dot_nn(ds, qkv_ref[:n, w : 2 * w] * keep)
        dk_ref[:n, :] += dot_tn(ds, q)
        dv_ref[:n, :] += dot_tn(p.astype(B16), d)

    @pl.when(h == heads - 1)
    def _():
        bias_ref[...] = jnp.zeros_like(bias_ref)

        @pl.loop(0, seq // QB)
        def _(r):
            rows = pl.ds(pl.multiple_of(r * QB, QB), QB)
            qk = jnp.concatenate([dq_ref[rows, :], dk_ref[rows, :]], axis=1)
            qk = rope(qk, cos_ref[rows, :], lo_ref[rows, :], hi_ref[rows, :], -1).astype(B16)
            v = dv_ref[rows, :].astype(B16)
            out_ref[swapped(r), : 2 * w] = qk
            out_ref[swapped(r), 2 * w :] = v
            bias_ref[:, : 2 * w] += jnp.sum(qk.astype(F32), axis=0, keepdims=True)
            bias_ref[:, 2 * w :] += jnp.sum(v.astype(F32), axis=0, keepdims=True)


def attend_backward(qkv, d_context, lse, tables):
    seq = qkv.shape[0]
    w = qkv.shape[1] // 3
    heads = w // HEAD
    table = tables[0].shape
    return pl.pallas_call(
        functools.partial(attend_backward_kernel, w, seq),
        grid=(heads,),
        in_specs=[
            whole((seq, 3 * w)),
            whole((seq, w)),
            whole((seq, 128)),
            whole(table),
            whole(table),
            whole(table),
        ],
        out_specs=[whole((seq, 3 * w)), whole((1, 3 * w))],
        out_shape=[
            jax.ShapeDtypeStruct((seq, 3 * w), B16),
            jax.ShapeDtypeStruct((1, 3 * w), F32),
        ],
        scratch_shapes=[pltpu.VMEM((seq, w), F32)] * 3,
        compiler_params=pltpu.CompilerParams(
            vmem_limit_bytes=40 * MIB, dimension_semantics=("arbitrary",)
        ),
        cost_estimate=pl.CostEstimate(
            flops=10 * seq * seq * 256 * heads,
            bytes_accessed=16 * seq * w,
            transcendentals=seq * seq * heads // 2,
        ),
        name="attend_backward",
    )(qkv, d_context, lse, *tables)


def normal_parts(u):
    x = jnp.abs(u) * (0.5**0.5)
    t = 1.0 / (1.0 + 0.3275911 * x)
    bell = jnp.exp(-0.5 * u * u)
    poly = t * (
        0.254829592
        + t * (-0.284496736 + t * (1.421413741 + t * (-1.453152027 + t * 1.061405429)))
    )
    half_tail = 0.5 * poly * bell
    return jnp.where(u >= 0.0, 1.0 - half_tail, half_tail), bell


def gelu(u):
    return u * normal_parts(u)[0]


def gelu_slope(u):
    share, bell = normal_parts(u)
    return share + u * bell * ((2.0 * math.pi) ** -0.5)


def standardize(x):
    average = jnp.mean(x, axis=-1, keepdims=True)
    centred = x - average
    variance = jnp.mean(centred * centred, axis=-1, keepdims=True)
    inverse = lax.rsqrt(variance + EPS)
    return centred * inverse, inverse


def swap(x, axis, bit):
    size = lax.axis_size(axis)
    return lax.ppermute(x, axis, [(i, i ^ bit) for i in range(size)])


def all_bits(size):
    bits = []
    bit = 1
    while bit < size:
        bits.append(bit)
        bit *= 2
    return bits


def after(x, *others):
    return lax.optimization_barrier((x,) + others)[0]


def on_device(
    tokens,
    cotangent,
    qkv_weight,
    qkv_bias,
    out_weight,
    out_bias,
    up_weight,
    up_bias,
    down_weight,
    down_bias,
    norm_gain,
    norm_shift,
):
    rows, features = tokens.shape
    tensor = lax.axis_size("tensor")
    dp = lax.axis_size("dp")
    chips = tensor // 2
    dp_index = lax.axis_index("dp")
    core = lax.axis_index("tensor") % 2
    w = qkv_weight.shape[2] // 3
    ff = up_weight.shape[2]
    heads = w // HEAD
    tables = rope_tables(SEQ_LEN, min(128, 2 * w))
    streams = range(chips)
    chip_bits = all_bits(chips)
    dp_bits = all_bits(dp)

    def core_gather(half):
        return jnp.concatenate([half, swap(half, "tensor", 1)], axis=0)

    def chip_gather(half):
        found = [half]
        for bit in chip_bits:
            found = found + [swap(item, "tensor", 2 * bit) for item in found]
        return found

    def chip_scatter(parts):
        for bit in reversed(chip_bits):
            sent = [swap(part.astype(B16), "tensor", 2 * bit) for part in parts[bit:]]
            parts = [part + got.astype(F32) for part, got in zip(parts[:bit], sent)]
        return parts[0]

    def chip_reduce(parts):
        for bit in chip_bits:
            low = [part.astype(B16) for part in parts]
            sent = [swap(part, "tensor", 2 * bit) for part in low]
            parts = [low[k].astype(F32) + sent[k ^ bit].astype(F32) for k in range(len(parts))]
        return parts

    def core_product(left, right, dot):
        got = swap(dot(left[rows:], right), "tensor", 1)
        return dot(left[:rows], right) + got

    def regroup(columns, back):
        lead = columns.shape[:-1]
        order = (3, heads, HEAD) if back else (heads, 3, HEAD)
        return jnp.swapaxes(columns.reshape(lead + order), -3, -2).reshape(columns.shape)

    qkv_w = [regroup(qkv_weight[l], False) for l in range(LAYERS)]
    qkv_b = [regroup(qkv_bias[l].astype(F32), False)[None] for l in range(LAYERS)]

    share = out_weight.shape[1] // dp
    piece = lax.dynamic_slice_in_dim(out_weight, dp_index * share, share, axis=1)
    near = [out_weight]
    for j in range(1, chips):
        near.append(lax.all_gather(swap(piece, "tensor", 2 * j), "dp", axis=1, tiled=True))
    far = [swap(item, "tensor", 1) for item in near]
    out_all = jnp.concatenate([x for pair in zip(near, far) for x in pair], axis=1)

    x_half = [t.astype(F32) for t in chip_gather(tokens)]
    stored = []
    stat_terms = []
    tick = tokens
    for l in range(LAYERS):
        final = l == LAYERS - 1
        gains = norm_gain[l].astype(F32)
        shifts = norm_shift[l].astype(F32)
        order = list(streams) if l == 0 else list(reversed(streams))
        na, nb, pre, hidden, ffn, qkv, ctx, lse, near = ([None] * chips for _ in range(9))
        up_b = up_bias[l].astype(F32)

        def feed(k):
            u = dot_nn(nb[k], up_weight[l]) + up_b
            pre[k] = u
            hidden[k] = gelu(u).astype(B16)
            ffn[k] = core_product(hidden[k], down_weight[l], dot_nn)

        def attend(k):
            qkv[k], ctx[k], lse[k] = attend_forward(na[k], qkv_w[l], qkv_b[l], tables)
            got = swap(ctx[k][rows:], "tensor", 1)
            near[k] = jnp.concatenate([ctx[k][:rows], got], axis=1)

        for k in order:
            z, _ = standardize(x_half[k])
            na[k] = core_gather((z * gains[0] + shifts[0]).astype(B16))
            nb[k] = core_gather((z * gains[1] + shifts[1]).astype(B16))
        if l == 0:
            for k in order:
                nb[k] = after(nb[k], tick)
                feed(k)
                na[k] = after(na[k], hidden[k])
                attend(k)
                tick = ctx[k]
        else:
            for k in order:
                nb[k] = after(nb[k], tick)
                feed(k)
                tick = hidden[k]
            for k in order:
                na[k] = after(na[k], tick)
                attend(k)
                tick = ctx[k]
        if final:
            ffn = [chip_scatter(ffn)]
        else:
            ffn = chip_reduce(ffn)
        x_next = []
        for k in streams if not final else range(1):
            blocks = [near[k]] + [swap(near[k ^ j], "tensor", 2 * j) for j in range(1, chips)]
            attn = dot_nn(jnp.concatenate(blocks, axis=1), out_all[l]) + out_bias[l].astype(F32)
            ffn_out = ffn[k] + down_bias[l].astype(F32)
            x_next.append(x_half[k] + attn + ffn_out)
            if k == 0:
                stat_terms.append(
                    jnp.stack(
                        [
                            jnp.sum(x_next[0] * x_next[0]),
                            jnp.sum(attn * attn),
                            jnp.sum(ffn_out * ffn_out),
                        ]
                    )
                )
        stored.append((x_half, na, nb, pre, hidden, qkv, ctx, lse))
        if l == 0:
            grad_low_half = chip_gather(after(cotangent, x_next[0]))
        x_half = x_next
    output = x_half[0]

    grad = cotangent.astype(F32)
    big = [None] * LAYERS
    small_all = [None] * LAYERS
    small_dp = [None] * LAYERS
    summed = None
    for l in reversed(range(LAYERS)):
        x_half, na, nb, pre, hidden, qkv, ctx, lse = stored[l]
        gains = norm_gain[l].astype(F32)
        low = grad.astype(B16)
        if l < LAYERS - 1:
            grad_low_half = chip_gather(low)
        g = [core_gather(item) for item in grad_low_half]
        g[0] = after(g[0], tick)
        d_pre, d_qkv, d_z = [None] * chips, [None] * chips, [None] * chips
        down_g = sum(dot_tn(hidden[k], g[k]) for k in streams)
        up_bias_g = jnp.zeros((ff,), F32)
        qkv_bias_g = jnp.zeros((1, 3 * w), F32)
        sums = 0.0
        for k in streams:
            d_pre[k] = (dot_nt(g[k], down_weight[l]) * gelu_slope(pre[k])).astype(B16)
            up_bias_g = up_bias_g + jnp.sum(d_pre[k], axis=0, dtype=F32)
        up_g = sum(dot_tn(nb[k], d_pre[k]) for k in streams)
        first = (down_g.astype(B16), up_g.astype(B16))
        if summed is not None:
            first = lax.optimization_barrier(first + summed[:1])[:2]
        first = lax.psum(first, "dp")
        tick = up_g
        for k in reversed(streams):
            d_ctx = dot_nt(g[k], out_weight[l]).astype(B16)
            d_qkv[k], bias_k = attend_backward(qkv[k], after(d_ctx, tick), lse[k], tables)
            tick = d_qkv[k]
            qkv_bias_g = qkv_bias_g + bias_k
            d_na = core_product(d_qkv[k], qkv_w[l], dot_nt)
            d_nb = core_product(d_pre[k], up_weight[l], dot_nt)
            z, inverse = standardize(x_half[k])
            sums = sums + jnp.stack(
                [
                    jnp.sum(d_na * z, axis=0),
                    jnp.sum(d_nb * z, axis=0),
                    jnp.sum(d_na, axis=0),
                    jnp.sum(d_nb, axis=0),
                ]
            )
            d_z[k] = d_na * gains[0] + d_nb * gains[1]
        total = chip_scatter(d_z)
        slope = total - jnp.mean(total, axis=-1, keepdims=True)
        slope = slope - z * jnp.mean(total * z, axis=-1, keepdims=True)
        bias_g = jnp.sum(low, axis=0, dtype=F32)
        grad = grad + slope * inverse
        out_g = sum(dot_tn(ctx[k], g[k]) for k in streams)
        qkv_g = sum(dot_tn(na[k], d_qkv[k]) for k in streams)
        second = (qkv_g.astype(B16), out_g.astype(B16))
        second = lax.optimization_barrier(second + first[:1])[:2]
        second = lax.psum(second, "dp")
        small_all[l] = jnp.concatenate(
            [sums, bias_g[None], jnp.pad(stat_terms[l], (0, features - 3))[None]], axis=0
        )
        small_dp[l] = jnp.concatenate([up_bias_g, qkv_bias_g[0]])
        big[l] = first + second
        summed = second
    small = jnp.stack(small_all)
    for bit in all_bits(tensor):
        small = small + swap(small, "tensor", bit)
    vector = jnp.stack(small_dp)
    for bit in dp_bits:
        small = small + swap(small, "dp", bit)
        vector = vector + swap(vector, "dp", bit)
    down_all = jnp.stack([item[0] for item in big]).astype(F32)
    up_all = jnp.stack([item[1] for item in big]).astype(F32)
    qkv_all = jnp.stack([regroup(item[2], True) for item in big]).astype(F32)
    out_w_all = jnp.stack([item[3] for item in big]).astype(F32)
    layer_stats = jnp.sqrt(small[:, 5, :3] / (rows * dp * tensor * features))
    bias_all = small[:, 4]
    return (
        output,
        grad,
        qkv_all,
        regroup(vector[:, ff:], True),
        out_w_all,
        bias_all,
        up_all,
        vector[:, :ff],
        down_all,
        bias_all,
        small[:, 0:2],
        small[:, 2:4],
        layer_stats,
    )


MESH = pl.DeviceIdType.MESH
ANY = pl.BlockSpec(memory_space=pl.ANY)
VMEM = pl.BlockSpec(memory_space=pltpu.VMEM)
DMA = pltpu.SemaphoreType.DMA


def partners():
    me = lax.axis_index("tensor")
    return me + 1 - 2 * lax.rem(me, 2), lax.rem(me + 2, 4)


def greet(others, more=0):
    barrier = pltpu.get_barrier_semaphore()
    for other in others:
        pl.semaphore_signal(barrier, inc=1, device_id={"tensor": other}, device_id_type=MESH)
    pl.semaphore_wait(barrier, len(others) + more)


def remote(src, dst, sems, index, target):
    return pltpu.make_async_remote_copy(
        src_ref=src,
        dst_ref=dst,
        send_sem=sems[0].at[index],
        recv_sem=sems[1].at[index],
        device_id={"tensor": target},
        device_id_type=MESH,
    )


def block(i, size=QB):
    return pl.ds(pl.multiple_of(i * size, size), size)


def loader(sems, **pairs):
    waiting = {}
    for i, (name, (src, dst)) in enumerate(pairs.items()):
        waiting[name] = pltpu.make_async_copy(src, dst, sems.at[i])
        waiting[name].start()

    def need(*names):
        for name in names:
            if name in waiting:
                waiting.pop(name).wait()

    return need


def by_kind(rows, heads):
    return jnp.concatenate(
        [
            rows[:, (3 * h + j) * HEAD : (3 * h + j + 1) * HEAD]
            for j in range(3)
            for h in range(heads)
        ],
        axis=1,
    )


def by_head(rows, heads):
    return jnp.concatenate(
        [
            rows[:, (heads * j + h) * HEAD : (heads * j + h + 1) * HEAD]
            for h in range(heads)
            for j in range(3)
        ],
        axis=1,
    )


def causal(s, n):
    tri = lax.broadcasted_iota(jnp.int32, (QB, QB), 0) >= lax.broadcasted_iota(
        jnp.int32, (QB, QB), 1
    )
    last = jnp.where(tri, s[:, n - QB :], NEG)
    return last if n == QB else jnp.concatenate([s[:, : n - QB], last], axis=1)


def forward_layer_kernel(l, first, final, rows, w, *refs):
    it = iter(refs)
    x_ref, up_h, down_h, qkvw_h, out_h, cos_h, lo_h, hi_h = (next(it) for _ in range(8))
    upb_h, qkvb_h, ob_h, db_h, gain_h, shift_h = (next(it) for _ in range(6))
    cot_ref = next(it) if final else None
    na_o, nb_o, u_o, hid_o, qkv_o, ctx_o, lse_o, x_o = (next(it) for _ in range(8))
    far_o = next(it) if first or final else None
    na_s, nb_s, u_s, hid_s, psend, precv, ysend, yrecv = (next(it) for _ in range(8))
    qkv_s, ctx_s, lse_s = (next(it) for _ in range(3))
    far_s = next(it) if first or final else None
    mine_s = next(it)
    up_ref, down_ref, qkvw_ref, out_ref, cos_ref, lo_ref, hi_ref = (next(it) for _ in range(7))
    upb_ref, qkvb_ref, ob_ref, gain_ref, shift_ref = (next(it) for _ in range(5))
    send, recv, local, u_sem, load_sem = (next(it) for _ in range(5))
    sems = (send, recv)
    need = loader(
        load_sem,
        up=(up_h.at[l], up_ref),
        qkvw=(qkvw_h.at[l], qkvw_ref),
        cos=(cos_h, cos_ref),
        lo=(lo_h, lo_ref),
        hi=(hi_h, hi_ref),
        down=(down_h.at[l], down_ref),
        out=(out_h.at[l], out_ref),
    )

    seq = 2 * rows
    heads = w // HEAD
    blocks = seq // QB
    half_blocks = rows // QB
    shift = lax.rem(lax.axis_index("tensor"), 2) * half_blocks
    core, far = partners()
    upb_ref[...] = upb_h[l : l + 1, :].astype(F32)
    qkvb_ref[...] = qkvb_h[l : l + 1, :].astype(F32)
    ob_ref[...] = ob_h[l : l + 1, :].astype(F32) + db_h[l : l + 1, :].astype(F32)
    gain_ref[...] = gain_h[l].astype(F32)
    shift_ref[...] = shift_h[l].astype(F32)
    greet((core, far))
    outs = []

    def keep(src, dst, index):
        copy = pltpu.make_async_copy(src, dst, local.at[index])
        copy.start()
        outs.append(copy)

    far_copy = None
    if first or final:
        far_copy = remote(x_ref if first else cot_ref, far_s, sems, 0, far)
        far_copy.start()

    def x_rows(k, r):
        if not first:
            return x_ref[block(r + k * half_blocks), :]
        return (far_s if k else x_ref)[block(r), :].astype(F32)

    gathers = {}

    def norms(k):
        @pl.loop(0, half_blocks)
        def _(r):
            z, _ = standardize(x_rows(k, r))
            na_s[k, block(r), :] = (z * gain_ref[0:1, :] + shift_ref[0:1, :]).astype(B16)
            nb_s[k, block(r), :] = (z * gain_ref[1:2, :] + shift_ref[1:2, :]).astype(B16)

        gathers[k] = []
        for at, buf in ((0, nb_s), (1, na_s)):
            copy = remote(
                buf.at[k, pl.ds(0, rows), :],
                buf.at[k, pl.ds(rows, rows), :],
                sems,
                1 + 2 * k + at,
                core,
            )
            copy.start()
            gathers[k].append(copy)

    products = {}
    u_out = []

    def feed(k):
        gathers[k][0].wait()
        need("up")
        keep(nb_s.at[k], nb_o.at[pl.ds(k * seq, seq), :], 2 * k)
        for h in (1, 0):
            for copy in u_out:
                copy.wait()
            u_out.clear()

            @pl.loop(0, half_blocks)
            def _(r):
                at = block(r + h * half_blocks)
                u = dot_nn(nb_s[k, at, :], up_ref[...]) + upb_ref[...]
                u_s[r] = u
                hid_s[k, at, :] = gelu(u).astype(B16)

            for r in range(half_blocks):
                copy = pltpu.make_async_copy(
                    u_s.at[r], u_o.at[pl.ds(k * seq + h * rows + r * QB, QB), :], u_sem.at[r]
                )
                copy.start()
                u_out.append(copy)
        keep(hid_s.at[k], hid_o.at[pl.ds(k * seq, seq), :], 2 * k + 1)

    def join(k):
        need("down", "out")

        @pl.loop(0, half_blocks)
        def _(r):
            at = block(r + half_blocks)
            psend[k, block(r), :] = dot_nn(hid_s[k, at, :], down_ref[...]) + dot_nn(
                ctx_s[k, at, :], out_ref[...]
            )

        product = remote(psend.at[k], precv.at[k], sems, 5 + k, core)
        product.start()
        products[k] = product

        @pl.loop(0, half_blocks)
        def _(r):
            at = block(r)
            mine_s[at, :] = dot_nn(hid_s[k, at, :], down_ref[...]) + dot_nn(
                ctx_s[k, at, :], out_ref[...]
            )

        product.wait_recv()

        @pl.loop(0, half_blocks)
        def _(r):
            at = block(r)
            total = precv[k, at, :] + mine_s[at, :]
            precv[k, at, :] = total
            if not (final and k == 0):
                ysend[k, at, :] = total.astype(B16)

        if not (final and k == 0):
            sums[k] = remote(ysend.at[k], yrecv.at[1 - k], sems, 7 + k, far)
            sums[k].start()

    sums = {}

    def attend(k):
        gathers[k][1].wait()
        need("qkvw", "cos", "lo", "hi")
        keep(na_s.at[k], na_o.at[pl.ds(k * seq, seq), :], 4 + 2 * k)
        swapped = lambda i: block(lax.rem(i + shift, blocks))

        @pl.loop(0, blocks)
        def _(r):
            acc = dot_nn(na_s[k, swapped(r), :], qkvw_ref[...]) + qkvb_ref[...]
            acc = by_kind(acc, heads)
            turned = rope(
                acc[:, : 2 * w], cos_ref[block(r), :], lo_ref[block(r), :], hi_ref[block(r), :], 1
            )
            qkv_s[k, block(r), : 2 * w] = turned.astype(B16)
            qkv_s[k, block(r), 2 * w :] = acc[:, 2 * w :].astype(B16)
            ctx_s[k, block(r), :] = jnp.zeros((QB, w), B16)
            lse_s[k, block(r), :] = jnp.zeros((QB, 128), F32)

        @pl.loop(0, heads)
        def _(h):
            mine = (lax.broadcasted_iota(jnp.int32, (1, w), 1) // HEAD) == h
            scale = jnp.where(mine, SCALE, 0.0).astype(B16)
            lane = lax.broadcasted_iota(jnp.int32, (QB, 128), 1)
            for i in range(blocks):
                n = (i + 1) * QB
                q = qkv_s[k, i * QB : n, :w] * scale
                s = causal(dot_nt(q, qkv_s[k, :n, w : 2 * w]), n)
                top = jnp.max(s, axis=1, keepdims=True)
                p = jnp.exp(s - top)
                total = jnp.sum(p, axis=1, keepdims=True)
                low = (p * (1.0 / total)).astype(B16)
                c = dot_nn(low, qkv_s[k, :n, 2 * w :])
                old = ctx_s[k, swapped(i), :]
                ctx_s[k, swapped(i), :] = jnp.where(mine, c, old.astype(F32)).astype(B16)
                lse_s[k, i * QB : n, :] = jnp.where(
                    lane == h, top + jnp.log(total), lse_s[k, i * QB : n, :]
                )

        keep(qkv_s.at[k], qkv_o.at[pl.ds(k * seq, seq), :], 5 + 2 * k)
        keep(ctx_s.at[k], ctx_o.at[pl.ds(k * seq, seq), :], 8 + 2 * k)
        keep(lse_s.at[k], lse_o.at[pl.ds(k * seq, seq), :], 9 + 2 * k)

    def finish(k):
        sums[1 - k].wait_recv()

        @pl.loop(0, half_blocks)
        def _(r):
            at = block(r)
            both = precv[k, at, :] + yrecv[k, at, :].astype(F32)
            precv[k, at, :] = x_rows(k, r) + (both + ob_ref[...])

        keep(precv.at[k], x_o.at[pl.ds(k * rows, rows), :], 12 + k)

    if first:
        norms(0)
        feed(0)
        attend(0)
        join(0)
        far_copy.wait_recv()
        norms(1)
        feed(1)
        attend(1)
        join(1)
    else:
        norms(1)
        norms(0)
        feed(1)
        attend(1)
        join(1)
        feed(0)
        attend(0)
        join(0)
    if final and not first:
        far_copy.wait_recv()
    if first or final:
        keep(far_s, far_o, 14)
    finish(0)
    if not final:
        finish(1)

    if first or final:
        far_copy.wait_send()
    for copy in u_out + outs:
        copy.wait()
    for copy in products.values():
        copy.wait_send()
    for copy in sums.values():
        copy.wait_send()


def forward_layer(
    l, layers, x, up, down, qkvw, out, tables, upb, qkvb, ob, db, gains, shifts, cot
):
    first, final = l == 0, l == layers - 1
    features = x.shape[1]
    rows = x.shape[0] if first else x.shape[0] // 2
    seq = 2 * rows
    w = qkvw.shape[2] // 3
    ff = up.shape[2]
    shape = jax.ShapeDtypeStruct
    out_shape = [
        shape((2 * seq, features), B16),
        shape((2 * seq, features), B16),
        shape((2 * seq, ff), F32),
        shape((2 * seq, ff), B16),
        shape((2 * seq, 3 * w), B16),
        shape((2 * seq, w), B16),
        shape((2 * seq, 128), F32),
        shape((rows if final else 2 * rows, features), F32),
    ]
    if first or final:
        out_shape.append(shape((rows, features), B16))
    args = [x, up, down, qkvw, out, *tables, upb, qkvb, ob, db, gains, shifts]
    if final:
        args.append(cot)
    scratch = [
        pltpu.VMEM((2, seq, features), B16),
        pltpu.VMEM((2, seq, features), B16),
        pltpu.VMEM((rows // QB, QB, ff), F32),
        pltpu.VMEM((2, seq, ff), B16),
        pltpu.VMEM((2, rows, features), F32),
        pltpu.VMEM((2, rows, features), F32),
        pltpu.VMEM((2, rows, features), B16),
        pltpu.VMEM((2, rows, features), B16),
        pltpu.VMEM((2, seq, 3 * w), B16),
        pltpu.VMEM((2, seq, w), B16),
        pltpu.VMEM((2, seq, 128), F32),
    ]
    if first or final:
        scratch.append(pltpu.VMEM((rows, features), B16))
    scratch.append(pltpu.VMEM((rows, features), F32))
    scratch += [pltpu.VMEM(item.shape[1:], B16) for item in (up, down, qkvw, out)]
    scratch += [pltpu.VMEM(item.shape, F32) for item in tables]
    scratch += [pltpu.VMEM((1, width), F32) for width in (ff, 3 * w, features)]
    scratch += [pltpu.VMEM((2, features), F32)] * 2
    scratch += [DMA((9,)), DMA((9,)), DMA((15,)), DMA((rows // QB,)), DMA((7,))]
    return pl.pallas_call(
        functools.partial(forward_layer_kernel, l, first, final, rows, w),
        in_specs=[VMEM] + [ANY] * 7 + [VMEM] * (len(args) - 8),
        out_specs=[ANY] * len(out_shape),
        out_shape=out_shape,
        scratch_shapes=scratch,
        compiler_params=pltpu.CompilerParams(
            vmem_limit_bytes=63 * MIB, collective_id=l, has_side_effects=True
        ),
        cost_estimate=pl.CostEstimate(
            flops=2 * 2 * seq * features * (3 * w + 2 * ff + w) * 2,
            bytes_accessed=40 * MIB,
            transcendentals=4 * seq * seq * w // HEAD,
        ),
        name="forward_layer",
    )(*args)


def ring_place(index, size):
    side = lax.rem(index, 2)
    level = index // 2
    return level * (1 - side) + (size - 1 - level) * side


def ring_device(place, size):
    side = place // (size // 2)
    return (1 - side) * 2 * place + side * (2 * (size - 1 - place) + 1)


class Ring:
    def __init__(self, n):
        self.n = n
        self.place = ring_place(lax.axis_index("dp"), n)
        self.targets = (
            ring_device(lax.rem(self.place + 1, n), n),
            ring_device(lax.rem(self.place + n - 1, n), n),
        )
        self.steps = n // 2

    def greet(self):
        barrier = pltpu.get_barrier_semaphore()
        for other in self.targets:
            pl.semaphore_signal(barrier, inc=1, device_id={"dp": other}, device_id_type=MESH)

    def rows(self, array, offset):
        size = array.shape[0] // self.n
        chunk = lax.rem(self.place + offset + 2 * self.n, self.n)
        return pl.ds(pl.multiple_of(chunk * size, size), size)

    def copy(self, src, dst, sems, at, way):
        return pltpu.make_async_remote_copy(
            src_ref=src,
            dst_ref=dst,
            send_sem=sems[0].at[at],
            recv_sem=sems[1].at[at],
            device_id={"dp": self.targets[way]},
            device_id_type=MESH,
        )


class Scatter:
    def __init__(self, ring, ins, turns, chunk, it):
        self.ring, self.ins, self.turns, self.chunk = ring, ins, turns, chunk
        self.slots = [next(it) for _ in ins]
        self.mine = [next(it) for _ in ins]
        self.sems = (next(it), next(it))
        self.load = next(it)
        self.parts = [(a, way) for a in range(len(ins)) for way in (0, 1)]

    @staticmethod
    def scratch(n, shapes, dtypes=None):
        count = len(shapes)
        kinds = [(a, b, B16) for a, b in shapes]
        if dtypes:
            kinds = [(a, b, dtype) for (a, b), dtype in zip(shapes, dtypes)]
        return (
            [pltpu.VMEM((2, n // 2, a // n, b), dtype) for a, b, dtype in kinds]
            + [pltpu.VMEM((2, a // n, b), dtype) for a, b, dtype in kinds]
            + [DMA((count, 2, n // 2)), DMA((count, 2, n // 2)), DMA((count, 2))]
        )

    def steps(self, a, way):
        return self.ring.steps - (way ^ self.turns[a])

    def rows(self, a, way, offset):
        return self.ring.rows(self.ins[a], -offset if way else offset)

    def sent(self, a, way, step):
        if step:
            src = self.slots[a].at[way, step - 1]
        else:
            src = self.ins[a].at[self.rows(a, way, self.steps(a, way)), :]
        return self.ring.copy(src, self.slots[a].at[way, step], self.sems, (a, way, step), way)

    def fetch(self, a, way, step):
        at = self.rows(a, way, self.steps(a, way) - step - 1)
        return pltpu.make_async_copy(
            self.ins[a].at[at, :], self.mine[a].at[way], self.load.at[a, way]
        )

    def start(self):
        for part in self.parts:
            self.sent(*part, 0).start()
        for part in self.parts:
            self.fetch(*part, 0).start()

    def step(self, step):
        for a, way in self.parts:
            steps = self.steps(a, way)
            if step >= steps:
                continue
            self.sent(a, way, step).wait_recv()
            if step + 1 < steps:
                self.fetch(a, way, step).wait()
                total = self.slots[a][way, step].astype(F32) + self.mine[a][way].astype(F32)
                self.slots[a][way, step] = total.astype(self.slots[a].dtype)
                self.sent(a, way, step + 1).start()
                if way == 0 or step + 2 < steps:
                    self.fetch(a, way, step + 1).start()
        if step == self.ring.steps - 1:
            for a in range(len(self.ins)):
                self.fetch(a, 0, self.steps(a, 0) - 1).wait()
                total = self.mine[a][0].astype(F32)
                for way in (0, 1):
                    total = total + self.slots[a][way, self.steps(a, way) - 1].astype(F32)
                self.chunk[a][...] = total.astype(self.chunk[a].dtype)

    def finish(self):
        for part in self.parts:
            for step in range(self.steps(*part)):
                self.sent(*part, step).wait_send()


class Gather:
    def __init__(self, ring, chunk, turns, done, it):
        self.ring, self.chunk, self.turns, self.done = ring, chunk, turns, done
        self.sems = (next(it), next(it))
        self.local = next(it)
        self.parts = [(a, way) for a in range(len(chunk)) for way in (0, 1)]

    @staticmethod
    def scratch(n, count):
        return [DMA((count, 2, n // 2)), DMA((count, 2, n // 2)), DMA((count,))]

    steps = Scatter.steps

    def sent(self, a, way, step):
        at = self.ring.rows(self.done[a], step if way else -step)
        src = self.done[a].at[at, :] if step else self.chunk[a]
        return self.ring.copy(src, self.done[a].at[at, :], self.sems, (a, way, step), way)

    def own(self, a):
        at = self.ring.rows(self.done[a], 0)
        return pltpu.make_async_copy(self.chunk[a], self.done[a].at[at, :], self.local.at[a])

    def start(self):
        for part in self.parts:
            self.sent(*part, 0).start()
        for a in range(len(self.chunk)):
            self.own(a).start()

    def step(self, step):
        for a, way in self.parts:
            steps = self.steps(a, way)
            if step < steps:
                self.sent(a, way, step).wait_recv()
                if step + 1 < steps:
                    self.sent(a, way, step + 1).start()

    def finish(self):
        for part in self.parts:
            for step in range(self.steps(*part)):
                self.sent(*part, step).wait_send()
        for a in range(len(self.chunk)):
            self.own(a).wait()


class Total:
    def __init__(self, scatter, gather):
        self.phases = [item for item in (scatter, gather) if item is not None]
        self.steps = self.phases[0].ring.steps
        self.at = 0

    def start(self):
        self.phases[0].start()

    def step(self):
        which, step = divmod(self.at, self.steps)
        self.phases[which].step(step)
        self.at += 1
        if step == self.steps - 1 and which + 1 < len(self.phases):
            self.phases[which + 1].start()

    def finish(self):
        while self.at < len(self.phases) * self.steps:
            self.step()
        for item in self.phases:
            item.finish()


def halves(ref):
    width = ref.shape[1] // 2
    return [ref.at[:, pl.ds(0, width)], ref.at[:, pl.ds(width, width)]]


def half_shapes(shape):
    return [(shape[0], shape[1] // 2)] * 2


def chunk_scratch(n, shapes):
    return [pltpu.VMEM((a // n, b), B16) for a, b in shapes]


def last_sums_kernel(n, count, *refs):
    it = iter(refs)
    ins = [item for _ in range(count) for item in halves(next(it))]
    small_in = next(it)
    done = [item for _ in range(count) for item in halves(next(it))]
    small_out = next(it)
    small_s, small_d = next(it), next(it)
    ring = Ring(n)
    turns = (0, 1) * count + (0,)
    ins.append(small_s)
    done.append(small_d)
    chunk = [next(it) for _ in ins]
    total = Total(Scatter(ring, ins, turns, chunk, it), Gather(ring, chunk, turns, done, it))
    ring.greet()
    rows, width = small_in.shape[0], small_in.shape[1] // 2
    small_s[:rows, :] = small_in[:, :width]
    small_s[rows:, :] = small_in[:, width:]
    pl.semaphore_wait(pltpu.get_barrier_semaphore(), 2)
    total.start()
    total.finish()
    small_out[:, :width] = small_d[:rows, :]
    small_out[:, width:] = small_d[rows:, :]


def last_sums(arrays, small, collective_id):
    n = lax.axis_size("dp")
    shape = jax.ShapeDtypeStruct
    count = len(arrays)
    folded = (2 * small.shape[0], small.shape[1] // 2)
    shapes = [half for item in arrays for half in half_shapes(item.shape)] + [folded]
    dtypes = [B16] * (2 * count) + [F32]
    return pl.pallas_call(
        functools.partial(last_sums_kernel, n, count),
        in_specs=[ANY] * count + [VMEM],
        out_specs=[ANY] * count + [VMEM],
        out_shape=[shape(item.shape, B16) for item in arrays] + [shape(small.shape, F32)],
        scratch_shapes=[pltpu.VMEM(folded, F32)] * 2
        + [pltpu.VMEM((a // n, b), dtype) for (a, b), dtype in zip(shapes, dtypes)]
        + Scatter.scratch(n, shapes, dtypes)
        + Gather.scratch(n, len(shapes)),
        compiler_params=pltpu.CompilerParams(
            vmem_limit_bytes=40 * MIB, collective_id=collective_id, has_side_effects=True
        ),
        cost_estimate=pl.CostEstimate(
            flops=arrays[0].size, bytes_accessed=200 * MIB, transcendentals=0
        ),
        name="last_sums",
    )(*arrays, small)


def backward_layer_kernel(l, first, final, rows, w, n, *refs):
    it = iter(refs)
    grad_ref, u_ref, down_h, up_h, ow_h, qkvw_h = (next(it) for _ in range(6))
    cos_h, lo_h, hi_h = (next(it) for _ in range(3))
    qkv_h, lse_h, ctx_ref, xn_h, x_ref = (next(it) for _ in range(5))
    far_ref = next(it) if first else None
    farg_ref = next(it) if final else None
    gain_h, ob_h = (next(it) for _ in range(2))
    hid_h, nb_h, na_h = (next(it) for _ in range(3))
    chunk_in, ready = (next(it), next(it)) if first else (None, None)
    dx_o, small_ref = (next(it) for _ in range(2))
    down_g, out_g, up_g, qkv_g, down_done, out_done = (next(it) for _ in range(6))
    up_chunk = None if first else next(it)
    up_done, ready_done = (next(it), next(it)) if first else (None, None)
    g_s, dpre_s, dqkv_s, dq_s, dk_s, dv_s, dctx_s = (next(it) for _ in range(7))
    u_s, osend, brecv, arecv, ysend, yrecv = (next(it) for _ in range(6))
    cfull, got_s = (next(it) for _ in range(2))
    down_ref, up_ref, ow_ref, qkvw_ref, outall_ref = (next(it) for _ in range(5))
    cos_ref, lo_ref, hi_ref, qkv_ref, lse_ref = (next(it) for _ in range(5))
    gain_ref, ob_ref = (next(it) for _ in range(2))
    send, recv, local, u_sem, load_sem = (next(it) for _ in range(5))
    sems = (send, recv)
    a_s, o_s, a_sem, o_sem = (next(it) for _ in range(4))
    ring = Ring(n)
    sums = {}
    turns = (0, 1, 0)
    chunk = [next(it) for _ in range(3)]
    sums["a"] = Total(
        Scatter(ring, halves(down_g) + [out_g], turns, chunk, it),
        Gather(ring, chunk, turns, halves(down_done) + [out_done], it),
    )
    if not first:
        sums["b"] = Total(Scatter(ring, halves(up_g), turns, halves(up_chunk), it), None)
    else:
        chunk = [next(it) for _ in range(2)]
        sums["c"] = Total(
            Scatter(ring, halves(ready), turns, chunk, it),
            Gather(ring, chunk, turns, halves(ready_done), it),
        )
        sums["d"] = Total(None, Gather(ring, halves(chunk_in), turns, halves(up_done), it))
    need = loader(
        load_sem,
        down=(down_h.at[l], down_ref),
        up=(up_h.at[l], up_ref),
        ow=(ow_h.at[l], ow_ref),
        qkv=(qkv_h, qkv_ref),
        lse=(lse_h, lse_ref),
        cos=(cos_h, cos_ref),
        lo=(lo_h, lo_ref),
        hi=(hi_h, hi_ref),
        qkvw=(qkvw_h.at[l], qkvw_ref),
    )

    seq = 2 * rows
    ff = up_ref.shape[1]
    heads = w // HEAD
    blocks = seq // QB
    half_blocks = rows // QB
    shift = lax.rem(lax.axis_index("tensor"), 2) * half_blocks
    swapped = lambda i: block(lax.rem(i + shift, blocks))
    core, far = partners()
    diag = lax.rem(core + 2, 4)
    ring.greet()
    greet((core, far, diag), 2)
    def load_u(k, i):
        return pltpu.make_async_copy(
            u_ref.at[pl.ds(k * seq + i * QB, QB), :], u_s.at[i % 2], u_sem.at[i % 2]
        )

    small_ref[...] = jnp.zeros_like(small_ref)
    gain_ref[...] = gain_h[l].astype(F32)
    ob_ref[...] = ob_h[l : l + 1, :].astype(F32)
    load_u(0, 0).start()
    load_u(0, 1).start()

    @pl.loop(0, half_blocks)
    def _(r):
        low = grad_ref[block(r), :].astype(B16)
        g_s[0, block(r), :] = low
        small_ref[4:5, :] += jnp.sum(low.astype(F32), axis=0, keepdims=True)

    own_half = lambda buf, k: buf.at[k, pl.ds(0, rows), :]
    other_half = lambda buf, k: buf.at[k, pl.ds(rows, rows), :]
    if final:
        g_s[1, :rows, :] = farg_ref[...]
    else:
        across = remote(own_half(g_s, 0), own_half(g_s, 1), sems, 0, far)
        across.start()
    near0 = remote(own_half(g_s, 0), other_half(g_s, 0), sems, 1, core)
    near0.start()
    if first:
        sums["c"].start()
        sums["d"].start()
    cfull[:, :w] = ctx_ref[:rows, :]
    contexts = [
        remote(ctx_ref.at[pl.ds(rows, rows), :], cfull.at[:, pl.ds(w, w)], sems, 8, core),
        remote(ctx_ref.at[pl.ds(seq, rows), :], cfull.at[:, pl.ds(2 * w, w)], sems, 9, far),
        remote(ctx_ref.at[pl.ds(seq + rows, rows), :], cfull.at[:, pl.ds(3 * w, w)], sems, 10, diag),
    ]
    need("ow")
    outall_ref[:w, :] = ow_ref[...]
    for i, other in enumerate((core, far, diag)):
        contexts.append(
            remote(ow_ref, outall_ref.at[pl.ds((i + 1) * w, w), :], sems, 13 + i, other)
        )
    for copy in contexts:
        copy.start()

    swaps = {}
    latest = []

    def feed(k):
        need("down")
        for i in range(blocks):
            load_u(k, i).wait()
            at = pl.ds(i * QB, QB)
            d_hidden = dot_nt(g_s[k, at, :], down_ref[...])
            d_pre = (d_hidden * gelu_slope(u_s[i % 2])).astype(B16)
            dpre_s[k, at, :] = d_pre
            small_ref[8:9, :ff] += jnp.sum(d_pre.astype(F32), axis=0, keepdims=True)
            if i + 2 < blocks:
                load_u(k, i + 2).start()
            elif k == 0:
                load_u(1, i + 2 - blocks).start()
            if 2 * (i + 1) == blocks:
                pump("feed%d half" % k)

        need("up")
        if latest:
            latest.pop().wait_send()

        @pl.loop(0, half_blocks)
        def _(r):
            osend[block(r), :] = dot_nt(dpre_s[k, block(r + half_blocks), :], up_ref[...])

        swaps[k] = [remote(osend, brecv.at[k], sems, 3 + 2 * k, core)]
        swaps[k][0].start()
        latest.append(swaps[k][0])

    def attend(k, pump):
        need("ow", "qkv", "lse", "cos", "lo", "hi", "qkvw")

        @pl.loop(0, blocks)
        def _(r):
            dctx_s[block(r), :] = dot_nt(g_s[k, swapped(r), :], ow_ref[...]).astype(B16)
            dq_s[block(r), :] = jnp.zeros((QB, w), F32)
            dk_s[block(r), :] = jnp.zeros((QB, w), F32)
            dv_s[block(r), :] = jnp.zeros((QB, w), F32)

        base = k * seq

        @pl.loop(0, heads)
        def _(h):
            mine = (lax.broadcasted_iota(jnp.int32, (1, w), 1) // HEAD) == h
            scale = jnp.where(mine, SCALE, 0.0).astype(B16)
            only = jnp.where(mine, 1.0, 0.0).astype(B16)
            lane = lax.broadcasted_iota(jnp.int32, (QB, 128), 1)
            for i in range(blocks):
                n = (i + 1) * QB
                q = qkv_ref[base + i * QB : base + n, :w] * scale
                d = dctx_s[i * QB : n, :] * only
                s = causal(dot_nt(q, qkv_ref[base : base + n, w : 2 * w]), n)
                lse = jnp.sum(
                    jnp.where(lane == h, lse_ref[base + i * QB : base + n, :], 0.0),
                    axis=1,
                    keepdims=True,
                )
                p = jnp.exp(s - lse)
                dp = dot_nt(d, qkv_ref[base : base + n, 2 * w :])
                inner = jnp.sum(p * dp, axis=1, keepdims=True)
                ds = (p * (dp - inner)).astype(B16)
                dq_s[i * QB : n, :] += dot_nn(ds, qkv_ref[base : base + n, w : 2 * w] * scale)
                dk_s[:n, :] += dot_tn(ds, q)
                dv_s[:n, :] += dot_tn(p.astype(B16), d)
            pump(h)

        @pl.loop(0, blocks)
        def _(r):
            at = block(r)
            qk = jnp.concatenate([dq_s[at, :], dk_s[at, :]], axis=1)
            qk = rope(qk, cos_ref[at, :], lo_ref[at, :], hi_ref[at, :], -1)
            low = by_head(jnp.concatenate([qk, dv_s[at, :]], axis=1), heads).astype(B16)
            dqkv_s[k, swapped(r), :] = low
            small_ref[9:10, : 3 * w] += jnp.sum(low.astype(F32), axis=0, keepdims=True)

        latest.pop().wait_send()

        @pl.loop(0, half_blocks)
        def _(r):
            osend[block(r), :] = dot_nt(dqkv_s[k, block(r + half_blocks), :], qkvw_ref[...])

        swaps[k].append(remote(osend, arecv.at[k], sems, 4 + 2 * k, core))
        swaps[k][1].start()
        latest.append(swaps[k][1])

    def x_rows(k, r):
        if not first:
            return x_ref[block(r + k * half_blocks), :]
        return (far_ref if k else x_ref)[block(r), :].astype(F32)

    def fold(k):
        for copy in swaps[k]:
            copy.wait_recv()

        @pl.loop(0, half_blocks)
        def _(r):
            at = block(r)
            d_na = dot_nt(dqkv_s[k, at, :], qkvw_ref[...]) + arecv[k, at, :]
            d_nb = dot_nt(dpre_s[k, at, :], up_ref[...]) + brecv[k, at, :]
            z, _ = standardize(x_rows(k, r))
            small_ref[0:1, :] += jnp.sum(d_na * z, axis=0, keepdims=True)
            small_ref[1:2, :] += jnp.sum(d_nb * z, axis=0, keepdims=True)
            small_ref[2:3, :] += jnp.sum(d_na, axis=0, keepdims=True)
            small_ref[3:4, :] += jnp.sum(d_nb, axis=0, keepdims=True)
            d_z = d_na * gain_ref[0:1, :] + d_nb * gain_ref[1:2, :]
            if k == 0:
                arecv[0, at, :] = d_z
            else:
                ysend[at, :] = d_z.astype(B16)

    def weight_grad(left, right, out):
        tiles = left.shape[1] // QB
        width = out.shape[1]

        def load(i):
            slot = lax.rem(i, 2)
            return pltpu.make_async_copy(left.at[:, block(i)], a_s.at[slot], a_sem.at[slot])

        def store(i):
            slot = lax.rem(i, 2)
            return pltpu.make_async_copy(
                o_s.at[slot, :, pl.ds(0, width)], out.at[block(i), :], o_sem.at[slot]
            )

        load(0).start()

        @pl.loop(0, tiles)
        def _(i):
            slot = lax.rem(i, 2)
            load(i).wait()

            @pl.when(i + 1 < tiles)
            def _():
                load(i + 1).start()

            @pl.when(i >= 2)
            def _():
                store(i - 2).wait()

            total = dot_tn(a_s[slot, :seq, :], right[0]) + dot_tn(a_s[slot, seq:, :], right[1])
            o_s[slot, :, :width] = total.astype(B16)
            store(i).start()

        for i in range(max(tiles - 2, 0), tiles):
            store(i).wait()

    if first:
        plan = {
            "feed0": "cd",
            "attend0 2": "cd",
            "near": "cd",
            "hid": "cd",
            "feed1 half": "c",
            "feed1": "ca",
            "nb": "a",
            "attend1 0": "c",
            "attend1 1": "a",
            "attend1 2": "c",
            "attend1 3": "a",
            "fold1": "a",
            "na": "a",
            "stats": "a",
        }
    else:
        plan = {
            "feed0": "a",
            "feed1 half": "a",
            "feed1": "a",
            "nb": "a",
            "attend1 3": "ab",
            "attend0 1": "ab",
            "fold0": "ab",
            "stats": "ab",
        }

    def pump(point):
        for name in plan.get(point, ""):
            sums[name].step()

    def at_heads(k):
        def at_head(h):
            for i in range(heads):
                if "attend%d %d" % (k, i) in plan:

                    @pl.when(h == i)
                    def _():
                        pump("attend%d %d" % (k, i))

        return at_head

    def early_grads():
        weight_grad(hid_h, g_s, down_g)
        pump("hid")
        weight_grad(ctx_ref, g_s, out_g)
        sums["a"].start()
        pump("ctx")

    near0.wait()
    if first:
        feed(0)
        pump("feed0")
        attend(0, at_heads(0))
        across.wait()
    near1 = remote(own_half(g_s, 1), other_half(g_s, 1), sems, 2, core)
    near1.start()
    pump("near")
    near1.wait()
    early_grads()
    if not first:
        feed(0)
        pump("feed0")
    feed(1)
    pump("feed1")
    weight_grad(nb_h, dpre_s, up_g)
    if not first:
        sums["b"].start()
    pump("nb")
    attend(1, at_heads(1))
    fold(1)
    back = remote(ysend, yrecv, sems, 7, far)
    back.start()
    next_rows = pltpu.make_async_copy(xn_h.at[pl.ds(0, rows), :], arecv.at[1], local.at[0])
    next_rows.start()
    pump("fold1")
    if not first:
        attend(0, at_heads(0))
    fold(0)
    pump("fold0")
    weight_grad(na_h, dqkv_s, qkv_g)
    pump("na")
    next_rows.wait()
    for copy in contexts:
        copy.wait()

    @pl.loop(0, half_blocks)
    def _(r):
        at = block(r)
        attn = dot_nn(cfull[at, :], outall_ref[...]) + ob_ref[...]
        x_next = arecv[1, at, :]
        feed_out = x_next - x_rows(0, r) - attn
        small_ref[5:6, :] += jnp.sum(x_next * x_next, axis=0, keepdims=True)
        small_ref[6:7, :] += jnp.sum(attn * attn, axis=0, keepdims=True)
        small_ref[7:8, :] += jnp.sum(feed_out * feed_out, axis=0, keepdims=True)

    for at, other in ((0, core), (1, far)):
        copy = remote(small_ref.at[pl.ds(0, 8), :], got_s.at[at], sems, 11 + at, other)
        copy.start()
        copy.wait()
        small_ref[0:8, :] += got_s[at]
    pump("stats")
    back.wait()

    @pl.loop(0, half_blocks)
    def _(r):
        at = block(r)
        total = arecv[0, at, :] + yrecv[at, :].astype(F32)
        z, inverse = standardize(x_rows(0, r))
        slope = total - jnp.mean(total, axis=-1, keepdims=True)
        slope = slope - z * jnp.mean(total * z, axis=-1, keepdims=True)
        arecv[0, at, :] = grad_ref[at, :].astype(F32) + slope * inverse

    grad_out = pltpu.make_async_copy(arecv.at[0], dx_o, local.at[1])
    grad_out.start()
    latest.pop().wait_send()
    pump("end")
    for item in sums.values():
        item.finish()
    grad_out.wait()


def backward_layer(
    l,
    layers,
    grad,
    u,
    down,
    up,
    out_w,
    qkvw,
    tables,
    qkv,
    lse,
    ctx,
    xn,
    x,
    far_x,
    far_g,
    gains,
    ob,
    hidden,
    nb,
    na,
    ready,
):
    first, final = l == 0, l == layers - 1
    rows, features = grad.shape
    seq = 2 * rows
    w = qkvw.shape[2] // 3
    ff = up.shape[2]
    n = lax.axis_size("dp")
    down_shape, out_w_shape, up_shape, qkv_shape = (
        (ff, features),
        (w, features),
        (features, ff),
        (features, 3 * w),
    )
    shape = jax.ShapeDtypeStruct
    args = [grad, u, down, up, out_w, qkvw, *tables, qkv, lse, ctx, xn, x]
    in_specs = [VMEM] + [ANY] * 10 + [VMEM, ANY, VMEM]
    if first:
        args.append(far_x)
        in_specs.append(VMEM)
    if final:
        args.append(far_g)
        in_specs.append(VMEM)
    args += [gains, ob, hidden, nb, na, *ready]
    in_specs += [VMEM] * 2 + [ANY] * 3
    if first:
        in_specs += [VMEM, ANY]
    low = lambda shapes: [shape(item, B16) for item in shapes]
    out_shape = [shape((rows, features), F32), shape((16, features), F32)]
    out_shape += low([down_shape, out_w_shape, up_shape, qkv_shape, down_shape, out_w_shape])
    out_specs = [ANY, VMEM] + [ANY] * 6
    if first:
        out_shape += low([up_shape, qkv_shape])
        out_specs += [ANY] * 2
    else:
        out_shape += low([(features // n, ff)])
        out_specs += [VMEM]
    scratch = [
        pltpu.VMEM((2, seq, features), B16),
        pltpu.VMEM((2, seq, ff), B16),
        pltpu.VMEM((2, seq, 3 * w), B16),
        pltpu.VMEM((seq, w), F32),
        pltpu.VMEM((seq, w), F32),
        pltpu.VMEM((seq, w), F32),
        pltpu.VMEM((seq, w), B16),
        pltpu.VMEM((2, QB, ff), F32),
        pltpu.VMEM((rows, features), F32),
        pltpu.VMEM((2, rows, features), F32),
        pltpu.VMEM((2, rows, features), F32),
        pltpu.VMEM((rows, features), B16),
        pltpu.VMEM((rows, features), B16),
        pltpu.VMEM((rows, 4 * w), B16),
        pltpu.VMEM((2, 8, features), F32),
    ]
    scratch += [pltpu.VMEM(item.shape[1:], B16) for item in (down, up, out_w, qkvw)]
    scratch += [pltpu.VMEM((4 * w, features), B16)]
    scratch += [pltpu.VMEM(item.shape, F32) for item in tables]
    scratch += [pltpu.VMEM(qkv.shape, B16), pltpu.VMEM(lse.shape, F32)]
    scratch += [pltpu.VMEM((2, features), F32), pltpu.VMEM((1, features), F32)]
    scratch += [DMA((16,)), DMA((16,)), DMA((2,)), DMA((2,)), DMA((9,))]
    scratch += [pltpu.VMEM((2, 2 * seq, QB), B16), pltpu.VMEM((2, QB, features), B16)]
    scratch += [DMA((2,)), DMA((2,))]
    shapes = half_shapes(down_shape) + [out_w_shape]
    scratch += chunk_scratch(n, shapes) + Scatter.scratch(n, shapes) + Gather.scratch(n, 3)
    if not first:
        scratch += Scatter.scratch(n, half_shapes(up_shape))
    else:
        shapes = half_shapes(qkv_shape)
        scratch += chunk_scratch(n, shapes) + Scatter.scratch(n, shapes)
        scratch += Gather.scratch(n, 2) * 2
    return pl.pallas_call(
        functools.partial(backward_layer_kernel, l, first, final, rows, w, n),
        in_specs=in_specs,
        out_specs=out_specs,
        out_shape=out_shape,
        scratch_shapes=scratch,
        compiler_params=pltpu.CompilerParams(
            vmem_limit_bytes=63 * MIB, collective_id=layers + l, has_side_effects=True
        ),
        cost_estimate=pl.CostEstimate(
            flops=2 * 2 * seq * features * (3 * w + 2 * ff + w) * 2,
            bytes_accessed=40 * MIB,
            transcendentals=4 * seq * seq * w // HEAD,
        ),
        name="backward_layer",
    )(*args)


def on_group(
    tokens,
    cotangent,
    qkv_weight,
    qkv_bias,
    out_weight,
    out_bias,
    up_weight,
    up_bias,
    down_weight,
    down_bias,
    norm_gain,
    norm_shift,
):
    rows, features = tokens.shape
    tensor = lax.axis_size("tensor")
    dp = lax.axis_size("dp")
    w = qkv_weight.shape[2] // 3
    ff = up_weight.shape[2]
    tables = rope_tables(SEQ_LEN, 128)

    x = tokens
    stored = []
    far_x = None
    for l in range(LAYERS):
        got = forward_layer(
            l,
            LAYERS,
            x,
            up_weight,
            down_weight,
            qkv_weight,
            out_weight,
            tables,
            up_bias,
            qkv_bias,
            out_bias,
            down_bias,
            norm_gain,
            norm_shift,
            cotangent,
        )
        na, nb, u, hidden, qkv, ctx, lse, x_next = got[:8]
        if l == 0:
            far_x = got[8]
        if l == LAYERS - 1:
            far_g = got[8]
        stored.append((x, na, nb, u, hidden, qkv, ctx, lse, x_next))
        x = x_next
    output = x

    grad = cotangent
    down_sums, out_sums, up_sums, qkv_sums = ([None] * LAYERS for _ in range(4))
    ready = ()
    small = [None] * LAYERS
    for l in reversed(range(LAYERS)):
        x, na, nb, u, hidden, qkv, ctx, lse, x_next = stored[l]
        grad, small[l], *found = backward_layer(
            l,
            LAYERS,
            grad,
            u,
            down_weight,
            up_weight,
            out_weight,
            qkv_weight,
            tables,
            qkv,
            lse,
            ctx,
            x_next,
            x,
            far_x,
            far_g,
            norm_gain,
            out_bias,
            hidden,
            nb,
            na,
            ready,
        )
        down_sums[l], out_sums[l] = found[4:6]
        if l < LAYERS - 1:
            up_sums[l + 1], qkv_sums[l + 1] = found[6:]
        else:
            ready = (found[6], found[3])
    up_sums[0], qkv_sums[0], small = last_sums(found[2:4], jnp.concatenate(small), 2 * LAYERS)
    small = small.reshape(LAYERS, 16, features)
    down_all, up_all, qkv_all, out_w_all = (
        jnp.stack(item).astype(F32) for item in (down_sums, up_sums, qkv_sums, out_sums)
    )
    layer_stats = jnp.sqrt(jnp.sum(small[:, 5:8], axis=2) / (rows * dp * tensor * features))
    bias_all = small[:, 4]
    return (
        output,
        grad,
        qkv_all,
        small[:, 9, : 3 * w],
        out_w_all,
        bias_all,
        up_all,
        small[:, 8, :ff],
        down_all,
        bias_all,
        small[:, 0:2],
        small[:, 2:4],
        layer_stats,
    )


def solution(mesh):
    in_specs = (
        P(("dp", "tensor"), None),
        P(("dp", "tensor"), None),
        P(None, None, "tensor"),
        P(None, "tensor"),
        P(None, "tensor", None),
        P(),
        P(None, None, "tensor"),
        P(None, "tensor"),
        P(None, "tensor", None),
        P(),
        P(),
        P(),
    )
    out_specs = (
        P(("dp", "tensor"), None),
        P(("dp", "tensor"), None),
        P(None, None, "tensor"),
        P(None, "tensor"),
        P(None, "tensor", None),
        P(),
        P(None, None, "tensor"),
        P(None, "tensor"),
        P(None, "tensor", None),
        P(),
        P(),
        P(),
        P(),
    )
    small = mesh.shape["tensor"] == 4 and mesh.shape["dp"] == 8
    return jax.shard_map(
        on_group if small else on_device,
        mesh=mesh, in_specs=in_specs, out_specs=out_specs, check_vma=False
    )
```

```python
import functools
import math

import jax
import jax.numpy as jnp
import numpy as np
from jax import lax
from jax.experimental import pallas as pl
from jax.experimental.pallas import tpu as pltpu
from jax.sharding import PartitionSpec as P

HEAD = 64
ROT = 16
LAYERS = 2
SEQ_LEN = 1024
QB = 256
SCALE = HEAD ** (-0.5)

EPS = 1e-05
NEG = -1e30
F32 = jnp.float32
B16 = jnp.bfloat16
MIB = 1024 * 1024


def dot_nn(left, right):
    return lax.dot_general(left, right, (((1,), (0,)), ((), ())), preferred_element_type=F32)


def dot_nt(left, right):
    return lax.dot_general(left, right, (((1,), (1,)), ((), ())), preferred_element_type=F32)


def dot_tn(left, right):
    return lax.dot_general(left, right, (((0,), (0,)), ((), ())), preferred_element_type=F32)


def rope_tables(seq, width):
    positions = np.arange(seq, dtype=np.float32)
    inverse = np.exp(np.arange(ROT // 2, dtype=np.float32) * (-2.0 * math.log(10000.0) / ROT))
    angles = (positions[:, None] * inverse.astype(np.float32)[None, :]).astype(np.float64)
    cosine, sine = np.cos(angles), np.sin(angles)
    zero = np.zeros_like(sine)
    rest = np.zeros((seq, HEAD - ROT))
    repeat = lambda parts: jnp.asarray(
        np.tile(np.concatenate(parts, axis=1), (1, width // HEAD)).astype(np.float32)
    )
    return (
        repeat([cosine, cosine, rest + 1.0]),
        repeat([-sine, zero, rest]),
        repeat([zero, sine, rest]),
    )


def rope(rows, cos, sin_lo, sin_hi, sign):
    width = cos.shape[1]
    parts = []
    for j in range(rows.shape[1] // width):
        part = rows[:, j * width : (j + 1) * width]
        turned = (
            pltpu.roll(part, width - ROT // 2, 1) * sin_lo + pltpu.roll(part, ROT // 2, 1) * sin_hi
        )
        parts.append(part * cos + turned if sign > 0 else part * cos - turned)
    return parts[0] if len(parts) == 1 else jnp.concatenate(parts, axis=1)


def attend_forward_kernel(
    w, seq, x_ref, w_ref, b_ref, cos_ref, lo_ref, hi_ref, qkv_ref, ctx_ref, lse_ref
):
    h = pl.program_id(0)
    blocks = seq // QB
    shift = (lax.axis_index("tensor") % 2) * (blocks // 2)
    swapped = lambda i: pl.ds(pl.multiple_of(lax.rem(i + shift, blocks) * QB, QB), QB)

    @pl.when(h == 0)
    def _():
        lse_ref[...] = jnp.zeros_like(lse_ref)
        ctx_ref[...] = jnp.zeros_like(ctx_ref)

        @pl.loop(0, seq // QB)
        def _(r):
            rows = pl.ds(pl.multiple_of(r * QB, QB), QB)
            acc = dot_nn(x_ref[swapped(r), :], w_ref[...]) + b_ref[...]
            turned = rope(acc[:, : 2 * w], cos_ref[rows, :], lo_ref[rows, :], hi_ref[rows, :], 1)
            qkv_ref[rows, : 2 * w] = turned.astype(B16)
            qkv_ref[rows, 2 * w :] = acc[:, 2 * w :].astype(B16)

    mine = (lax.broadcasted_iota(jnp.int32, (1, w), 1) // HEAD) == h
    keep = jnp.where(mine, SCALE, 0.0).astype(B16)
    for i in range(seq // QB):
        n = (i + 1) * QB
        q = qkv_ref[i * QB : n, :w] * keep
        s = dot_nt(q, qkv_ref[:n, w : 2 * w])
        tri = lax.broadcasted_iota(jnp.int32, (QB, QB), 0) >= lax.broadcasted_iota(
            jnp.int32, (QB, QB), 1
        )
        last = jnp.where(tri, s[:, n - QB :], NEG)
        s = last if i == 0 else jnp.concatenate([s[:, : n - QB], last], axis=1)
        top = jnp.max(s, axis=1, keepdims=True)
        p = jnp.exp(s - top)
        total = jnp.sum(p, axis=1, keepdims=True)
        low = (p * (1.0 / total)).astype(B16)
        c = dot_nn(low, qkv_ref[:n, 2 * w :])
        old = ctx_ref[swapped(i), :]
        ctx_ref[swapped(i), :] = jnp.where(mine, c, old.astype(F32)).astype(B16)
        lane = lax.broadcasted_iota(jnp.int32, (QB, 128), 1)
        lse_ref[i * QB : n, :] = jnp.where(lane == h, top + jnp.log(total), lse_ref[i * QB : n, :])


def whole(shape):
    return pl.BlockSpec(shape, lambda h: (0,) * len(shape))


def attend_forward(x, weight, bias, tables):
    seq, features = x.shape
    w = weight.shape[1] // 3
    heads = w // HEAD
    table = tables[0].shape
    return pl.pallas_call(
        functools.partial(attend_forward_kernel, w, seq),
        grid=(heads,),
        in_specs=[
            whole((seq, features)),
            whole((features, 3 * w)),
            whole((1, 3 * w)),
            whole(table),
            whole(table),
            whole(table),
        ],
        out_specs=[whole((seq, 3 * w)), whole((seq, w)), whole((seq, 128))],
        out_shape=[
            jax.ShapeDtypeStruct((seq, 3 * w), B16),
            jax.ShapeDtypeStruct((seq, w), B16),
            jax.ShapeDtypeStruct((seq, 128), F32),
        ],
        compiler_params=pltpu.CompilerParams(
            vmem_limit_bytes=40 * MIB, dimension_semantics=("arbitrary",)
        ),
        cost_estimate=pl.CostEstimate(
            flops=2 * seq * features * 3 * w + 4 * seq * seq * 256 * heads,
            bytes_accessed=2 * seq * features + 6 * features * w + 8 * seq * w,
            transcendentals=seq * seq * heads // 2,
        ),
        name="attend_forward",
    )(x, weight, bias, *tables)


def attend_backward_kernel(
    w,
    seq,
    qkv_ref,
    d_ref,
    lse_ref,
    cos_ref,
    lo_ref,
    hi_ref,
    out_ref,
    bias_ref,
    dq_ref,
    dk_ref,
    dv_ref,
):
    h = pl.program_id(0)
    heads = w // HEAD
    blocks = seq // QB
    shift = (lax.axis_index("tensor") % 2) * (blocks // 2)
    swapped = lambda i: pl.ds(pl.multiple_of(lax.rem(i + shift, blocks) * QB, QB), QB)

    @pl.when(h == 0)
    def _():
        dq_ref[...] = jnp.zeros_like(dq_ref)
        dk_ref[...] = jnp.zeros_like(dk_ref)
        dv_ref[...] = jnp.zeros_like(dv_ref)

    mine = (lax.broadcasted_iota(jnp.int32, (1, w), 1) // HEAD) == h
    keep = jnp.where(mine, SCALE, 0.0).astype(B16)
    keep_value = jnp.where(mine, 1.0, 0.0).astype(B16)
    for i in range(seq // QB):
        n = (i + 1) * QB
        q = qkv_ref[i * QB : n, :w] * keep
        d = d_ref[swapped(i), :] * keep_value
        s = dot_nt(q, qkv_ref[:n, w : 2 * w])
        lane = lax.broadcasted_iota(jnp.int32, (QB, 128), 1)
        lse = jnp.sum(jnp.where(lane == h, lse_ref[i * QB : n, :], 0.0), axis=1, keepdims=True)
        tri = lax.broadcasted_iota(jnp.int32, (QB, QB), 0) >= lax.broadcasted_iota(
            jnp.int32, (QB, QB), 1
        )
        last = jnp.where(tri, s[:, n - QB :], NEG)
        s = last if i == 0 else jnp.concatenate([s[:, : n - QB], last], axis=1)
        p = jnp.exp(s - lse)
        dp = dot_nt(d, qkv_ref[:n, 2 * w :])
        inner = jnp.sum(p * dp, axis=1, keepdims=True)
        ds = (p * (dp - inner)).astype(B16)
        dq_ref[i * QB : n, :] += dot_nn(ds, qkv_ref[:n, w : 2 * w] * keep)
        dk_ref[:n, :] += dot_tn(ds, q)
        dv_ref[:n, :] += dot_tn(p.astype(B16), d)

    @pl.when(h == heads - 1)
    def _():
        bias_ref[...] = jnp.zeros_like(bias_ref)

        @pl.loop(0, seq // QB)
        def _(r):
            rows = pl.ds(pl.multiple_of(r * QB, QB), QB)
            qk = jnp.concatenate([dq_ref[rows, :], dk_ref[rows, :]], axis=1)
            qk = rope(qk, cos_ref[rows, :], lo_ref[rows, :], hi_ref[rows, :], -1).astype(B16)
            v = dv_ref[rows, :].astype(B16)
            out_ref[swapped(r), : 2 * w] = qk
            out_ref[swapped(r), 2 * w :] = v
            bias_ref[:, : 2 * w] += jnp.sum(qk.astype(F32), axis=0, keepdims=True)
            bias_ref[:, 2 * w :] += jnp.sum(v.astype(F32), axis=0, keepdims=True)


def attend_backward(qkv, d_context, lse, tables):
    seq = qkv.shape[0]
    w = qkv.shape[1] // 3
    heads = w // HEAD
    table = tables[0].shape
    return pl.pallas_call(
        functools.partial(attend_backward_kernel, w, seq),
        grid=(heads,),
        in_specs=[
            whole((seq, 3 * w)),
            whole((seq, w)),
            whole((seq, 128)),
            whole(table),
            whole(table),
            whole(table),
        ],
        out_specs=[whole((seq, 3 * w)), whole((1, 3 * w))],
        out_shape=[
            jax.ShapeDtypeStruct((seq, 3 * w), B16),
            jax.ShapeDtypeStruct((1, 3 * w), F32),
        ],
        scratch_shapes=[pltpu.VMEM((seq, w), F32)] * 3,
        compiler_params=pltpu.CompilerParams(
            vmem_limit_bytes=40 * MIB, dimension_semantics=("arbitrary",)
        ),
        cost_estimate=pl.CostEstimate(
            flops=10 * seq * seq * 256 * heads,
            bytes_accessed=16 * seq * w,
            transcendentals=seq * seq * heads // 2,
        ),
        name="attend_backward",
    )(qkv, d_context, lse, *tables)


def normal_parts(u):
    x = jnp.abs(u) * (0.5**0.5)
    t = 1.0 / (1.0 + 0.3275911 * x)
    bell = jnp.exp(-0.5 * u * u)
    poly = t * (
        0.254829592
        + t * (-0.284496736 + t * (1.421413741 + t * (-1.453152027 + t * 1.061405429)))
    )
    half_tail = 0.5 * poly * bell
    return jnp.where(u >= 0.0, 1.0 - half_tail, half_tail), bell


def gelu(u):
    return u * normal_parts(u)[0]


def gelu_slope(u):
    share, bell = normal_parts(u)
    return share + u * bell * ((2.0 * math.pi) ** -0.5)


def gelu_and_slope(u):
    share, bell = normal_parts(u)
    return u * share, share + u * bell * ((2.0 * math.pi) ** -0.5)


def standardize(x):
    average = jnp.mean(x, axis=-1, keepdims=True)
    centred = x - average
    variance = jnp.mean(centred * centred, axis=-1, keepdims=True)
    inverse = lax.rsqrt(variance + EPS)
    return centred * inverse, inverse


def swap(x, axis, bit):
    size = lax.axis_size(axis)
    return lax.ppermute(x, axis, [(i, i ^ bit) for i in range(size)])


def all_bits(size):
    bits = []
    bit = 1
    while bit < size:
        bits.append(bit)
        bit *= 2
    return bits


def after(x, *others):
    return lax.optimization_barrier((x,) + others)[0]


def on_device(
    tokens,
    cotangent,
    qkv_weight,
    qkv_bias,
    out_weight,
    out_bias,
    up_weight,
    up_bias,
    down_weight,
    down_bias,
    norm_gain,
    norm_shift,
):
    rows, features = tokens.shape
    tensor = lax.axis_size("tensor")
    dp = lax.axis_size("dp")
    chips = tensor // 2
    dp_index = lax.axis_index("dp")
    core = lax.axis_index("tensor") % 2
    w = qkv_weight.shape[2] // 3
    ff = up_weight.shape[2]
    heads = w // HEAD
    tables = rope_tables(SEQ_LEN, min(128, 2 * w))
    streams = range(chips)
    chip_bits = all_bits(chips)
    dp_bits = all_bits(dp)

    def core_gather(half):
        return jnp.concatenate([half, swap(half, "tensor", 1)], axis=0)

    def chip_gather(half):
        found = [half]
        for bit in chip_bits:
            found = found + [swap(item, "tensor", 2 * bit) for item in found]
        return found

    def chip_scatter(parts):
        for bit in reversed(chip_bits):
            sent = [swap(part.astype(B16), "tensor", 2 * bit) for part in parts[bit:]]
            parts = [part + got.astype(F32) for part, got in zip(parts[:bit], sent)]
        return parts[0]

    def chip_reduce(parts):
        for bit in chip_bits:
            low = [part.astype(B16) for part in parts]
            sent = [swap(part, "tensor", 2 * bit) for part in low]
            parts = [low[k].astype(F32) + sent[k ^ bit].astype(F32) for k in range(len(parts))]
        return parts

    def core_product(left, right, dot):
        got = swap(dot(left[rows:], right), "tensor", 1)
        return dot(left[:rows], right) + got

    def regroup(columns, back):
        lead = columns.shape[:-1]
        order = (3, heads, HEAD) if back else (heads, 3, HEAD)
        return jnp.swapaxes(columns.reshape(lead + order), -3, -2).reshape(columns.shape)

    qkv_w = [regroup(qkv_weight[l], False) for l in range(LAYERS)]
    qkv_b = [regroup(qkv_bias[l].astype(F32), False)[None] for l in range(LAYERS)]

    share = out_weight.shape[1] // dp
    piece = lax.dynamic_slice_in_dim(out_weight, dp_index * share, share, axis=1)
    near = [out_weight]
    for j in range(1, chips):
        near.append(lax.all_gather(swap(piece, "tensor", 2 * j), "dp", axis=1, tiled=True))
    far = [swap(item, "tensor", 1) for item in near]
    out_all = jnp.concatenate([x for pair in zip(near, far) for x in pair], axis=1)

    x_half = [t.astype(F32) for t in chip_gather(tokens)]
    stored = []
    stat_terms = []
    tick = tokens
    for l in range(LAYERS):
        final = l == LAYERS - 1
        gains = norm_gain[l].astype(F32)
        shifts = norm_shift[l].astype(F32)
        order = list(streams) if l == 0 else list(reversed(streams))
        na, nb, pre, hidden, ffn, qkv, ctx, lse, near = ([None] * chips for _ in range(9))
        up_b = up_bias[l].astype(F32)

        def feed(k):
            u = dot_nn(nb[k], up_weight[l]) + up_b
            pre[k] = u
            hidden[k] = gelu(u).astype(B16)
            ffn[k] = core_product(hidden[k], down_weight[l], dot_nn)

        def attend(k):
            qkv[k], ctx[k], lse[k] = attend_forward(na[k], qkv_w[l], qkv_b[l], tables)
            got = swap(ctx[k][rows:], "tensor", 1)
            near[k] = jnp.concatenate([ctx[k][:rows], got], axis=1)

        for k in order:
            z, _ = standardize(x_half[k])
            na[k] = core_gather((z * gains[0] + shifts[0]).astype(B16))
            nb[k] = core_gather((z * gains[1] + shifts[1]).astype(B16))
        if l == 0:
            for k in order:
                nb[k] = after(nb[k], tick)
                feed(k)
                na[k] = after(na[k], hidden[k])
                attend(k)
                tick = ctx[k]
        else:
            for k in order:
                nb[k] = after(nb[k], tick)
                feed(k)
                tick = hidden[k]
            for k in order:
                na[k] = after(na[k], tick)
                attend(k)
                tick = ctx[k]
        if final:
            ffn = [chip_scatter(ffn)]
        else:
            ffn = chip_reduce(ffn)
        x_next = []
        for k in streams if not final else range(1):
            blocks = [near[k]] + [swap(near[k ^ j], "tensor", 2 * j) for j in range(1, chips)]
            attn = dot_nn(jnp.concatenate(blocks, axis=1), out_all[l]) + out_bias[l].astype(F32)
            ffn_out = ffn[k] + down_bias[l].astype(F32)
            x_next.append(x_half[k] + attn + ffn_out)
            if k == 0:
                stat_terms.append(
                    jnp.stack(
                        [
                            jnp.sum(x_next[0] * x_next[0]),
                            jnp.sum(attn * attn),
                            jnp.sum(ffn_out * ffn_out),
                        ]
                    )
                )
        stored.append((x_half, na, nb, pre, hidden, qkv, ctx, lse))
        if l == 0:
            grad_low_half = chip_gather(after(cotangent, x_next[0]))
        x_half = x_next
    output = x_half[0]

    grad = cotangent.astype(F32)
    big = [None] * LAYERS
    small_all = [None] * LAYERS
    small_dp = [None] * LAYERS
    summed = None
    for l in reversed(range(LAYERS)):
        x_half, na, nb, pre, hidden, qkv, ctx, lse = stored[l]
        gains = norm_gain[l].astype(F32)
        low = grad.astype(B16)
        if l < LAYERS - 1:
            grad_low_half = chip_gather(low)
        g = [core_gather(item) for item in grad_low_half]
        g[0] = after(g[0], tick)
        d_pre, d_qkv, d_z = [None] * chips, [None] * chips, [None] * chips
        down_g = sum(dot_tn(hidden[k], g[k]) for k in streams)
        up_bias_g = jnp.zeros((ff,), F32)
        qkv_bias_g = jnp.zeros((1, 3 * w), F32)
        sums = 0.0
        for k in streams:
            d_pre[k] = (dot_nt(g[k], down_weight[l]) * gelu_slope(pre[k])).astype(B16)
            up_bias_g = up_bias_g + jnp.sum(d_pre[k], axis=0, dtype=F32)
        up_g = sum(dot_tn(nb[k], d_pre[k]) for k in streams)
        first = (down_g.astype(B16), up_g.astype(B16))
        if summed is not None:
            first = lax.optimization_barrier(first + summed[:1])[:2]
        first = lax.psum(first, "dp")
        tick = up_g
        for k in reversed(streams):
            d_ctx = dot_nt(g[k], out_weight[l]).astype(B16)
            d_qkv[k], bias_k = attend_backward(qkv[k], after(d_ctx, tick), lse[k], tables)
            tick = d_qkv[k]
            qkv_bias_g = qkv_bias_g + bias_k
            d_na = core_product(d_qkv[k], qkv_w[l], dot_nt)
            d_nb = core_product(d_pre[k], up_weight[l], dot_nt)
            z, inverse = standardize(x_half[k])
            sums = sums + jnp.stack(
                [
                    jnp.sum(d_na * z, axis=0),
                    jnp.sum(d_nb * z, axis=0),
                    jnp.sum(d_na, axis=0),
                    jnp.sum(d_nb, axis=0),
                ]
            )
            d_z[k] = d_na * gains[0] + d_nb * gains[1]
        total = chip_scatter(d_z)
        slope = total - jnp.mean(total, axis=-1, keepdims=True)
        slope = slope - z * jnp.mean(total * z, axis=-1, keepdims=True)
        bias_g = jnp.sum(low, axis=0, dtype=F32)
        grad = grad + slope * inverse
        out_g = sum(dot_tn(ctx[k], g[k]) for k in streams)
        qkv_g = sum(dot_tn(na[k], d_qkv[k]) for k in streams)
        second = (qkv_g.astype(B16), out_g.astype(B16))
        second = lax.optimization_barrier(second + first[:1])[:2]
        second = lax.psum(second, "dp")
        small_all[l] = jnp.concatenate(
            [sums, bias_g[None], jnp.pad(stat_terms[l], (0, features - 3))[None]], axis=0
        )
        small_dp[l] = jnp.concatenate([up_bias_g, qkv_bias_g[0]])
        big[l] = first + second
        summed = second
    small = jnp.stack(small_all)
    for bit in all_bits(tensor):
        small = small + swap(small, "tensor", bit)
    vector = jnp.stack(small_dp)
    for bit in dp_bits:
        small = small + swap(small, "dp", bit)
        vector = vector + swap(vector, "dp", bit)
    down_all = jnp.stack([item[0] for item in big]).astype(F32)
    up_all = jnp.stack([item[1] for item in big]).astype(F32)
    qkv_all = jnp.stack([regroup(item[2], True) for item in big]).astype(F32)
    out_w_all = jnp.stack([item[3] for item in big]).astype(F32)
    layer_stats = jnp.sqrt(small[:, 5, :3] / (rows * dp * tensor * features))
    bias_all = small[:, 4]
    return (
        output,
        grad,
        qkv_all,
        regroup(vector[:, ff:], True),
        out_w_all,
        bias_all,
        up_all,
        vector[:, :ff],
        down_all,
        bias_all,
        small[:, 0:2],
        small[:, 2:4],
        layer_stats,
    )


MESH = pl.DeviceIdType.MESH
ANY = pl.BlockSpec(memory_space=pl.ANY)
VMEM = pl.BlockSpec(memory_space=pltpu.VMEM)
DMA = pltpu.SemaphoreType.DMA


def partners():
    me = lax.axis_index("tensor")
    return me + 1 - 2 * lax.rem(me, 2), lax.rem(me + 2, 4)


def greet(others, more=0):
    barrier = pltpu.get_barrier_semaphore()
    for other in others:
        pl.semaphore_signal(barrier, inc=1, device_id={"tensor": other}, device_id_type=MESH)
    pl.semaphore_wait(barrier, len(others) + more)


def remote(src, dst, sems, index, target):
    return pltpu.make_async_remote_copy(
        src_ref=src,
        dst_ref=dst,
        send_sem=sems[0].at[index],
        recv_sem=sems[1].at[index],
        device_id={"tensor": target},
        device_id_type=MESH,
    )


def block(i, size=QB):
    return pl.ds(pl.multiple_of(i * size, size), size)


def loader(sems, **pairs):
    waiting = {}
    for i, (name, (src, dst)) in enumerate(pairs.items()):
        waiting[name] = pltpu.make_async_copy(src, dst, sems.at[i])
        waiting[name].start()

    def need(*names):
        for name in names:
            if name in waiting:
                waiting.pop(name).wait()

    return need


def by_kind(rows, heads):
    return jnp.concatenate(
        [
            rows[:, (3 * h + j) * HEAD : (3 * h + j + 1) * HEAD]
            for j in range(3)
            for h in range(heads)
        ],
        axis=1,
    )


def by_head(rows, heads):
    return jnp.concatenate(
        [
            rows[:, (heads * j + h) * HEAD : (heads * j + h + 1) * HEAD]
            for h in range(heads)
            for j in range(3)
        ],
        axis=1,
    )


def causal(s, n):
    tri = lax.broadcasted_iota(jnp.int32, (QB, QB), 0) >= lax.broadcasted_iota(
        jnp.int32, (QB, QB), 1
    )
    last = jnp.where(tri, s[:, n - QB :], NEG)
    return last if n == QB else jnp.concatenate([s[:, : n - QB], last], axis=1)


def forward_layer_kernel(l, first, final, rows, w, *refs):
    it = iter(refs)
    x_ref, up_h, down_h, qkvw_h, out_h, cos_h, lo_h, hi_h = (next(it) for _ in range(8))
    upb_h, qkvb_h, ob_h, db_h, gain_h, shift_h = (next(it) for _ in range(6))
    cot_ref = next(it) if final else None
    na_o, nb_o, u_o, hid_o, qkv_o, ctx_o, lse_o, x_o = (next(it) for _ in range(8))
    far_o = next(it) if first or final else None
    na_s, nb_s, u_s, hid_s, psend, precv, ysend, yrecv = (next(it) for _ in range(8))
    qkv_s, ctx_s, lse_s = (next(it) for _ in range(3))
    far_s = next(it) if first or final else None
    mine_s = next(it)
    up_ref, down_ref, qkvw_ref, out_ref, cos_ref, lo_ref, hi_ref = (next(it) for _ in range(7))
    upb_ref, qkvb_ref, ob_ref, gain_ref, shift_ref = (next(it) for _ in range(5))
    send, recv, local, u_sem, load_sem = (next(it) for _ in range(5))
    sems = (send, recv)
    need = loader(
        load_sem,
        up=(up_h.at[l], up_ref),
        qkvw=(qkvw_h.at[l], qkvw_ref),
        cos=(cos_h, cos_ref),
        lo=(lo_h, lo_ref),
        hi=(hi_h, hi_ref),
        down=(down_h.at[l], down_ref),
        out=(out_h.at[l], out_ref),
    )

    seq = 2 * rows
    heads = w // HEAD
    blocks = seq // QB
    half_blocks = rows // QB
    shift = lax.rem(lax.axis_index("tensor"), 2) * half_blocks
    core, far = partners()
    upb_ref[...] = upb_h[l : l + 1, :].astype(F32)
    qkvb_ref[...] = qkvb_h[l : l + 1, :].astype(F32)
    ob_ref[...] = ob_h[l : l + 1, :].astype(F32) + db_h[l : l + 1, :].astype(F32)
    gain_ref[...] = gain_h[l].astype(F32)
    shift_ref[...] = shift_h[l].astype(F32)
    greet((core, far))
    outs = []

    def keep(src, dst, index):
        copy = pltpu.make_async_copy(src, dst, local.at[index])
        copy.start()
        outs.append(copy)

    far_copy = None
    if first or final:
        far_copy = remote(x_ref if first else cot_ref, far_s, sems, 0, far)
        far_copy.start()

    def x_rows(k, r):
        if not first:
            return x_ref[block(r + k * half_blocks), :]
        return (far_s if k else x_ref)[block(r), :].astype(F32)

    gathers = {}

    def norms(k):
        @pl.loop(0, half_blocks)
        def _(r):
            z, _ = standardize(x_rows(k, r))
            na_s[k, block(r), :] = (z * gain_ref[0:1, :] + shift_ref[0:1, :]).astype(B16)
            nb_s[k, block(r), :] = (z * gain_ref[1:2, :] + shift_ref[1:2, :]).astype(B16)

        gathers[k] = []
        for at, buf in ((0, nb_s), (1, na_s)):
            copy = remote(
                buf.at[k, pl.ds(0, rows), :],
                buf.at[k, pl.ds(rows, rows), :],
                sems,
                1 + 2 * k + at,
                core,
            )
            copy.start()
            gathers[k].append(copy)

    products = {}
    u_out = []

    def feed(k):
        gathers[k][0].wait()
        need("up")
        keep(nb_s.at[k], nb_o.at[pl.ds(k * seq, seq), :], 2 * k)
        for h in (1, 0):
            for copy in u_out:
                copy.wait()
            u_out.clear()

            @pl.loop(0, half_blocks)
            def _(r):
                at = block(r + h * half_blocks)
                u = dot_nn(nb_s[k, at, :], up_ref[...]) + upb_ref[...]
                value, slope = gelu_and_slope(u)
                u_s[r] = slope
                hid_s[k, at, :] = value.astype(B16)

            for r in range(half_blocks):
                copy = pltpu.make_async_copy(
                    u_s.at[r], u_o.at[pl.ds(k * seq + h * rows + r * QB, QB), :], u_sem.at[r]
                )
                copy.start()
                u_out.append(copy)
        keep(hid_s.at[k], hid_o.at[pl.ds(k * seq, seq), :], 2 * k + 1)

    def join(k):
        need("down", "out")

        @pl.loop(0, half_blocks)
        def _(r):
            at = block(r + half_blocks)
            psend[k, block(r), :] = dot_nn(hid_s[k, at, :], down_ref[...]) + dot_nn(
                ctx_s[k, at, :], out_ref[...]
            )

        product = remote(psend.at[k], precv.at[k], sems, 5 + k, core)
        product.start()
        products[k] = product

        @pl.loop(0, half_blocks)
        def _(r):
            at = block(r)
            mine_s[at, :] = dot_nn(hid_s[k, at, :], down_ref[...]) + dot_nn(
                ctx_s[k, at, :], out_ref[...]
            )

        product.wait_recv()

        @pl.loop(0, half_blocks)
        def _(r):
            at = block(r)
            total = precv[k, at, :] + mine_s[at, :]
            precv[k, at, :] = total
            if not (final and k == 0):
                ysend[k, at, :] = total.astype(B16)

        if not (final and k == 0):
            sums[k] = remote(ysend.at[k], yrecv.at[1 - k], sems, 7 + k, far)
            sums[k].start()

    sums = {}

    def attend(k):
        gathers[k][1].wait()
        need("qkvw", "cos", "lo", "hi")
        keep(na_s.at[k], na_o.at[pl.ds(k * seq, seq), :], 4 + 2 * k)
        swapped = lambda i: block(lax.rem(i + shift, blocks))

        @pl.loop(0, blocks)
        def _(r):
            acc = dot_nn(na_s[k, swapped(r), :], qkvw_ref[...]) + qkvb_ref[...]
            acc = by_kind(acc, heads)
            turned = rope(
                acc[:, : 2 * w], cos_ref[block(r), :], lo_ref[block(r), :], hi_ref[block(r), :], 1
            )
            qkv_s[k, block(r), : 2 * w] = turned.astype(B16)
            qkv_s[k, block(r), 2 * w :] = acc[:, 2 * w :].astype(B16)
            ctx_s[k, block(r), :] = jnp.zeros((QB, w), B16)
            lse_s[k, block(r), :] = jnp.zeros((QB, 128), F32)

        @pl.loop(0, heads)
        def _(h):
            mine = (lax.broadcasted_iota(jnp.int32, (1, w), 1) // HEAD) == h
            scale = jnp.where(mine, SCALE, 0.0).astype(B16)
            lane = lax.broadcasted_iota(jnp.int32, (QB, 128), 1)
            for i in range(blocks):
                n = (i + 1) * QB
                q = qkv_s[k, i * QB : n, :w] * scale
                s = causal(dot_nt(q, qkv_s[k, :n, w : 2 * w]), n)
                top = jnp.max(s, axis=1, keepdims=True)
                p = jnp.exp(s - top)
                total = jnp.sum(p, axis=1, keepdims=True)
                low = (p * (1.0 / total)).astype(B16)
                c = dot_nn(low, qkv_s[k, :n, 2 * w :])
                old = ctx_s[k, swapped(i), :]
                ctx_s[k, swapped(i), :] = jnp.where(mine, c, old.astype(F32)).astype(B16)
                lse_s[k, i * QB : n, :] = jnp.where(
                    lane == h, top + jnp.log(total), lse_s[k, i * QB : n, :]
                )

        keep(qkv_s.at[k], qkv_o.at[pl.ds(k * seq, seq), :], 5 + 2 * k)
        keep(ctx_s.at[k], ctx_o.at[pl.ds(k * seq, seq), :], 8 + 2 * k)
        keep(lse_s.at[k], lse_o.at[pl.ds(k * seq, seq), :], 9 + 2 * k)

    def finish(k):
        sums[1 - k].wait_recv()

        @pl.loop(0, half_blocks)
        def _(r):
            at = block(r)
            both = precv[k, at, :] + yrecv[k, at, :].astype(F32)
            precv[k, at, :] = x_rows(k, r) + (both + ob_ref[...])

        keep(precv.at[k], x_o.at[pl.ds(k * rows, rows), :], 12 + k)

    if first:
        norms(0)
        feed(0)
        attend(0)
        join(0)
        far_copy.wait_recv()
        norms(1)
        feed(1)
        attend(1)
        join(1)
    else:
        norms(1)
        norms(0)
        feed(1)
        attend(1)
        join(1)
        feed(0)
        attend(0)
        join(0)
    if final and not first:
        far_copy.wait_recv()
    if first or final:
        keep(far_s, far_o, 14)
    finish(0)
    if not final:
        finish(1)

    if first or final:
        far_copy.wait_send()
    for copy in u_out + outs:
        copy.wait()
    for copy in products.values():
        copy.wait_send()
    for copy in sums.values():
        copy.wait_send()


def forward_layer(
    l, layers, x, up, down, qkvw, out, tables, upb, qkvb, ob, db, gains, shifts, cot
):
    first, final = l == 0, l == layers - 1
    features = x.shape[1]
    rows = x.shape[0] if first else x.shape[0] // 2
    seq = 2 * rows
    w = qkvw.shape[2] // 3
    ff = up.shape[2]
    shape = jax.ShapeDtypeStruct
    out_shape = [
        shape((2 * seq, features), B16),
        shape((2 * seq, features), B16),
        shape((2 * seq, ff), F32),
        shape((2 * seq, ff), B16),
        shape((2 * seq, 3 * w), B16),
        shape((2 * seq, w), B16),
        shape((2 * seq, 128), F32),
        shape((rows if final else 2 * rows, features), F32),
    ]
    if first or final:
        out_shape.append(shape((rows, features), B16))
    args = [x, up, down, qkvw, out, *tables, upb, qkvb, ob, db, gains, shifts]
    if final:
        args.append(cot)
    scratch = [
        pltpu.VMEM((2, seq, features), B16),
        pltpu.VMEM((2, seq, features), B16),
        pltpu.VMEM((rows // QB, QB, ff), F32),
        pltpu.VMEM((2, seq, ff), B16),
        pltpu.VMEM((2, rows, features), F32),
        pltpu.VMEM((2, rows, features), F32),
        pltpu.VMEM((2, rows, features), B16),
        pltpu.VMEM((2, rows, features), B16),
        pltpu.VMEM((2, seq, 3 * w), B16),
        pltpu.VMEM((2, seq, w), B16),
        pltpu.VMEM((2, seq, 128), F32),
    ]
    if first or final:
        scratch.append(pltpu.VMEM((rows, features), B16))
    scratch.append(pltpu.VMEM((rows, features), F32))
    scratch += [pltpu.VMEM(item.shape[1:], B16) for item in (up, down, qkvw, out)]
    scratch += [pltpu.VMEM(item.shape, F32) for item in tables]
    scratch += [pltpu.VMEM((1, width), F32) for width in (ff, 3 * w, features)]
    scratch += [pltpu.VMEM((2, features), F32)] * 2
    scratch += [DMA((9,)), DMA((9,)), DMA((15,)), DMA((rows // QB,)), DMA((7,))]
    return pl.pallas_call(
        functools.partial(forward_layer_kernel, l, first, final, rows, w),
        in_specs=[VMEM] + [ANY] * 7 + [VMEM] * (len(args) - 8),
        out_specs=[ANY] * len(out_shape),
        out_shape=out_shape,
        scratch_shapes=scratch,
        compiler_params=pltpu.CompilerParams(
            vmem_limit_bytes=63 * MIB, collective_id=l, has_side_effects=True
        ),
        cost_estimate=pl.CostEstimate(
            flops=2 * 2 * seq * features * (3 * w + 2 * ff + w) * 2,
            bytes_accessed=40 * MIB,
            transcendentals=4 * seq * seq * w // HEAD,
        ),
        name="forward_layer",
    )(*args)


def ring_place(index, size):
    side = lax.rem(index, 2)
    level = index // 2
    return level * (1 - side) + (size - 1 - level) * side


def ring_device(place, size):
    side = place // (size // 2)
    return (1 - side) * 2 * place + side * (2 * (size - 1 - place) + 1)


class Ring:
    def __init__(self, n):
        self.n = n
        self.place = ring_place(lax.axis_index("dp"), n)
        self.targets = (
            ring_device(lax.rem(self.place + 1, n), n),
            ring_device(lax.rem(self.place + n - 1, n), n),
        )
        self.steps = n // 2

    def greet(self):
        barrier = pltpu.get_barrier_semaphore()
        for other in self.targets:
            pl.semaphore_signal(barrier, inc=1, device_id={"dp": other}, device_id_type=MESH)

    def rows(self, array, offset):
        size = array.shape[0] // self.n
        chunk = lax.rem(self.place + offset + 2 * self.n, self.n)
        return pl.ds(pl.multiple_of(chunk * size, size), size)

    def copy(self, src, dst, sems, at, way):
        return pltpu.make_async_remote_copy(
            src_ref=src,
            dst_ref=dst,
            send_sem=sems[0].at[at],
            recv_sem=sems[1].at[at],
            device_id={"dp": self.targets[way]},
            device_id_type=MESH,
        )


class Scatter:
    def __init__(self, ring, ins, turns, chunk, it):
        self.ring, self.ins, self.turns, self.chunk = ring, ins, turns, chunk
        self.slots = [next(it) for _ in ins]
        self.mine = [next(it) for _ in ins]
        self.sems = (next(it), next(it))
        self.load = next(it)
        self.parts = [(a, way) for a in range(len(ins)) for way in (0, 1)]

    @staticmethod
    def scratch(n, shapes, dtypes=None):
        count = len(shapes)
        kinds = [(a, b, B16) for a, b in shapes]
        if dtypes:
            kinds = [(a, b, dtype) for (a, b), dtype in zip(shapes, dtypes)]
        return (
            [pltpu.VMEM((2, n // 2, a // n, b), dtype) for a, b, dtype in kinds]
            + [pltpu.VMEM((2, a // n, b), dtype) for a, b, dtype in kinds]
            + [DMA((count, 2, n // 2)), DMA((count, 2, n // 2)), DMA((count, 2))]
        )

    def steps(self, a, way):
        return self.ring.steps - (way ^ self.turns[a])

    def rows(self, a, way, offset):
        return self.ring.rows(self.ins[a], -offset if way else offset)

    def sent(self, a, way, step):
        if step:
            src = self.slots[a].at[way, step - 1]
        else:
            src = self.ins[a].at[self.rows(a, way, self.steps(a, way)), :]
        return self.ring.copy(src, self.slots[a].at[way, step], self.sems, (a, way, step), way)

    def fetch(self, a, way, step):
        at = self.rows(a, way, self.steps(a, way) - step - 1)
        return pltpu.make_async_copy(
            self.ins[a].at[at, :], self.mine[a].at[way], self.load.at[a, way]
        )

    def start(self):
        for part in self.parts:
            self.sent(*part, 0).start()
        for part in self.parts:
            self.fetch(*part, 0).start()

    def step(self, step):
        for a, way in self.parts:
            steps = self.steps(a, way)
            if step >= steps:
                continue
            self.sent(a, way, step).wait_recv()
            if step + 1 < steps:
                self.fetch(a, way, step).wait()
                total = self.slots[a][way, step].astype(F32) + self.mine[a][way].astype(F32)
                self.slots[a][way, step] = total.astype(self.slots[a].dtype)
                self.sent(a, way, step + 1).start()
                if way == 0 or step + 2 < steps:
                    self.fetch(a, way, step + 1).start()
        if step == self.ring.steps - 1:
            for a in range(len(self.ins)):
                self.fetch(a, 0, self.steps(a, 0) - 1).wait()
                total = self.mine[a][0].astype(F32)
                for way in (0, 1):
                    total = total + self.slots[a][way, self.steps(a, way) - 1].astype(F32)
                self.chunk[a][...] = total.astype(self.chunk[a].dtype)

    def finish(self):
        for part in self.parts:
            for step in range(self.steps(*part)):
                self.sent(*part, step).wait_send()


class Gather:
    def __init__(self, ring, chunk, turns, done, it):
        self.ring, self.chunk, self.turns, self.done = ring, chunk, turns, done
        self.sems = (next(it), next(it))
        self.local = next(it)
        self.parts = [(a, way) for a in range(len(chunk)) for way in (0, 1)]

    @staticmethod
    def scratch(n, count):
        return [DMA((count, 2, n // 2)), DMA((count, 2, n // 2)), DMA((count,))]

    steps = Scatter.steps

    def sent(self, a, way, step):
        at = self.ring.rows(self.done[a], step if way else -step)
        src = self.done[a].at[at, :] if step else self.chunk[a]
        return self.ring.copy(src, self.done[a].at[at, :], self.sems, (a, way, step), way)

    def own(self, a):
        at = self.ring.rows(self.done[a], 0)
        return pltpu.make_async_copy(self.chunk[a], self.done[a].at[at, :], self.local.at[a])

    def start(self):
        for part in self.parts:
            self.sent(*part, 0).start()
        for a in range(len(self.chunk)):
            self.own(a).start()

    def step(self, step):
        for a, way in self.parts:
            steps = self.steps(a, way)
            if step < steps:
                self.sent(a, way, step).wait_recv()
                if step + 1 < steps:
                    self.sent(a, way, step + 1).start()

    def finish(self):
        for part in self.parts:
            for step in range(self.steps(*part)):
                self.sent(*part, step).wait_send()
        for a in range(len(self.chunk)):
            self.own(a).wait()


class Total:
    def __init__(self, scatter, gather):
        self.phases = [item for item in (scatter, gather) if item is not None]
        self.steps = self.phases[0].ring.steps
        self.at = 0

    def start(self):
        self.phases[0].start()

    def step(self):
        which, step = divmod(self.at, self.steps)
        self.phases[which].step(step)
        self.at += 1
        if step == self.steps - 1 and which + 1 < len(self.phases):
            self.phases[which + 1].start()

    def finish(self):
        while self.at < len(self.phases) * self.steps:
            self.step()
        for item in self.phases:
            item.finish()


def halves(ref):
    width = ref.shape[1] // 2
    return [ref.at[:, pl.ds(0, width)], ref.at[:, pl.ds(width, width)]]


def half_shapes(shape):
    return [(shape[0], shape[1] // 2)] * 2


def chunk_scratch(n, shapes):
    return [pltpu.VMEM((a // n, b), B16) for a, b in shapes]


def last_sums_kernel(n, count, *refs):
    it = iter(refs)
    ins = [item for _ in range(count) for item in halves(next(it))]
    small_in = next(it)
    done = [item for _ in range(count) for item in halves(next(it))]
    small_out = next(it)
    small_s, small_d = next(it), next(it)
    ring = Ring(n)
    turns = (0, 1) * count + (0,)
    ins.append(small_s)
    done.append(small_d)
    chunk = [next(it) for _ in ins]
    total = Total(Scatter(ring, ins, turns, chunk, it), Gather(ring, chunk, turns, done, it))
    ring.greet()
    rows, width = small_in.shape[0], small_in.shape[1] // 2
    small_s[:rows, :] = small_in[:, :width]
    small_s[rows:, :] = small_in[:, width:]
    pl.semaphore_wait(pltpu.get_barrier_semaphore(), 2)
    total.start()
    total.finish()
    small_out[:, :width] = small_d[:rows, :]
    small_out[:, width:] = small_d[rows:, :]


def last_sums(arrays, small, collective_id):
    n = lax.axis_size("dp")
    shape = jax.ShapeDtypeStruct
    count = len(arrays)
    folded = (2 * small.shape[0], small.shape[1] // 2)
    shapes = [half for item in arrays for half in half_shapes(item.shape)] + [folded]
    dtypes = [B16] * (2 * count) + [F32]
    return pl.pallas_call(
        functools.partial(last_sums_kernel, n, count),
        in_specs=[ANY] * count + [VMEM],
        out_specs=[ANY] * count + [VMEM],
        out_shape=[shape(item.shape, B16) for item in arrays] + [shape(small.shape, F32)],
        scratch_shapes=[pltpu.VMEM(folded, F32)] * 2
        + [pltpu.VMEM((a // n, b), dtype) for (a, b), dtype in zip(shapes, dtypes)]
        + Scatter.scratch(n, shapes, dtypes)
        + Gather.scratch(n, len(shapes)),
        compiler_params=pltpu.CompilerParams(
            vmem_limit_bytes=40 * MIB, collective_id=collective_id, has_side_effects=True
        ),
        cost_estimate=pl.CostEstimate(
            flops=arrays[0].size, bytes_accessed=200 * MIB, transcendentals=0
        ),
        name="last_sums",
    )(*arrays, small)


def backward_layer_kernel(l, first, final, rows, w, n, *refs):
    it = iter(refs)
    grad_ref, u_ref, down_h, up_h, ow_h, qkvw_h = (next(it) for _ in range(6))
    cos_h, lo_h, hi_h = (next(it) for _ in range(3))
    qkv_h, lse_h, ctx_ref, xn_h, x_ref = (next(it) for _ in range(5))
    far_ref = next(it) if first else None
    farg_ref = next(it) if final else None
    gain_h, ob_h = (next(it) for _ in range(2))
    hid_h, nb_h, na_h = (next(it) for _ in range(3))
    chunk_in, ready = (next(it), next(it)) if first else (None, None)
    dx_o, small_ref = (next(it) for _ in range(2))
    down_g, out_g, up_g, qkv_g, down_done, out_done = (next(it) for _ in range(6))
    up_chunk = None if first else next(it)
    up_done, ready_done = (next(it), next(it)) if first else (None, None)
    g_s, dpre_s, dqkv_s, dq_s, dk_s, dv_s, dctx_s = (next(it) for _ in range(7))
    u_s, osend, brecv, arecv, ysend, yrecv = (next(it) for _ in range(6))
    cfull, got_s = (next(it) for _ in range(2))
    down_ref, up_ref, ow_ref, qkvw_ref, outall_ref = (next(it) for _ in range(5))
    cos_ref, lo_ref, hi_ref, qkv_ref, lse_ref = (next(it) for _ in range(5))
    gain_ref, ob_ref = (next(it) for _ in range(2))
    send, recv, local, u_sem, load_sem = (next(it) for _ in range(5))
    sems = (send, recv)
    a_s, o_s, a_sem, o_sem = (next(it) for _ in range(4))
    ring = Ring(n)
    sums = {}
    turns = (0, 1, 0)
    chunk = [next(it) for _ in range(3)]
    sums["a"] = Total(
        Scatter(ring, halves(down_g) + [out_g], turns, chunk, it),
        Gather(ring, chunk, turns, halves(down_done) + [out_done], it),
    )
    if not first:
        sums["b"] = Total(Scatter(ring, halves(up_g), turns, halves(up_chunk), it), None)
    else:
        chunk = [next(it) for _ in range(2)]
        sums["c"] = Total(
            Scatter(ring, halves(ready), turns, chunk, it),
            Gather(ring, chunk, turns, halves(ready_done), it),
        )
        sums["d"] = Total(None, Gather(ring, halves(chunk_in), turns, halves(up_done), it))
    need = loader(
        load_sem,
        down=(down_h.at[l], down_ref),
        up=(up_h.at[l], up_ref),
        ow=(ow_h.at[l], ow_ref),
        qkv=(qkv_h, qkv_ref),
        lse=(lse_h, lse_ref),
        cos=(cos_h, cos_ref),
        lo=(lo_h, lo_ref),
        hi=(hi_h, hi_ref),
        qkvw=(qkvw_h.at[l], qkvw_ref),
    )

    seq = 2 * rows
    ff = up_ref.shape[1]
    heads = w // HEAD
    blocks = seq // QB
    half_blocks = rows // QB
    shift = lax.rem(lax.axis_index("tensor"), 2) * half_blocks
    swapped = lambda i: block(lax.rem(i + shift, blocks))
    core, far = partners()
    diag = lax.rem(core + 2, 4)
    ring.greet()
    greet((core, far, diag), 2)
    def load_u(k, i):
        return pltpu.make_async_copy(
            u_ref.at[pl.ds(k * seq + i * QB, QB), :], u_s.at[i % 2], u_sem.at[i % 2]
        )

    small_ref[...] = jnp.zeros_like(small_ref)
    gain_ref[...] = gain_h[l].astype(F32)
    ob_ref[...] = ob_h[l : l + 1, :].astype(F32)
    load_u(0, 0).start()
    load_u(0, 1).start()

    @pl.loop(0, half_blocks)
    def _(r):
        low = grad_ref[block(r), :].astype(B16)
        g_s[0, block(r), :] = low
        small_ref[4:5, :] += jnp.sum(low.astype(F32), axis=0, keepdims=True)

    own_half = lambda buf, k: buf.at[k, pl.ds(0, rows), :]
    other_half = lambda buf, k: buf.at[k, pl.ds(rows, rows), :]
    if final:
        g_s[1, :rows, :] = farg_ref[...]
    else:
        across = remote(own_half(g_s, 0), own_half(g_s, 1), sems, 0, far)
        across.start()
    near0 = remote(own_half(g_s, 0), other_half(g_s, 0), sems, 1, core)
    near0.start()
    if first:
        sums["c"].start()
        sums["d"].start()
    cfull[:, :w] = ctx_ref[:rows, :]
    contexts = [
        remote(ctx_ref.at[pl.ds(rows, rows), :], cfull.at[:, pl.ds(w, w)], sems, 8, core),
        remote(ctx_ref.at[pl.ds(seq, rows), :], cfull.at[:, pl.ds(2 * w, w)], sems, 9, far),
        remote(ctx_ref.at[pl.ds(seq + rows, rows), :], cfull.at[:, pl.ds(3 * w, w)], sems, 10, diag),
    ]
    need("ow")
    outall_ref[:w, :] = ow_ref[...]
    for i, other in enumerate((core, far, diag)):
        contexts.append(
            remote(ow_ref, outall_ref.at[pl.ds((i + 1) * w, w), :], sems, 13 + i, other)
        )
    for copy in contexts:
        copy.start()

    swaps = {}
    latest = []

    def feed(k):
        need("down")
        for i in range(blocks):
            load_u(k, i).wait()
            at = pl.ds(i * QB, QB)
            d_hidden = dot_nt(g_s[k, at, :], down_ref[...])
            d_pre = (d_hidden * u_s[i % 2]).astype(B16)
            dpre_s[k, at, :] = d_pre
            small_ref[8:9, :ff] += jnp.sum(d_pre.astype(F32), axis=0, keepdims=True)
            if i + 2 < blocks:
                load_u(k, i + 2).start()
            elif k == 0:
                load_u(1, i + 2 - blocks).start()
            if 2 * (i + 1) == blocks:
                pump("feed%d half" % k)

        need("up")
        for copy in latest:
            copy.wait_send()
        latest.clear()

        @pl.loop(0, half_blocks)
        def _(r):
            osend[block(r), :] = dot_nt(dpre_s[k, block(r + half_blocks), :], up_ref[...])

        swaps[k] = [remote(osend, brecv.at[k], sems, 3 + 2 * k, core)]
        swaps[k][0].start()
        latest.append(swaps[k][0])

    def attend(k, pump):
        need("ow", "qkv", "lse", "cos", "lo", "hi", "qkvw")

        @pl.loop(0, blocks)
        def _(r):
            dctx_s[block(r), :] = dot_nt(g_s[k, swapped(r), :], ow_ref[...]).astype(B16)
            dq_s[block(r), :] = jnp.zeros((QB, w), F32)
            dk_s[block(r), :] = jnp.zeros((QB, w), F32)
            dv_s[block(r), :] = jnp.zeros((QB, w), F32)

        base = k * seq

        @pl.loop(0, heads)
        def _(h):
            mine = (lax.broadcasted_iota(jnp.int32, (1, w), 1) // HEAD) == h
            scale = jnp.where(mine, SCALE, 0.0).astype(B16)
            only = jnp.where(mine, 1.0, 0.0).astype(B16)
            lane = lax.broadcasted_iota(jnp.int32, (QB, 128), 1)
            for i in range(blocks):
                n = (i + 1) * QB
                q = qkv_ref[base + i * QB : base + n, :w] * scale
                d = dctx_s[i * QB : n, :] * only
                s = causal(dot_nt(q, qkv_ref[base : base + n, w : 2 * w]), n)
                lse = jnp.sum(
                    jnp.where(lane == h, lse_ref[base + i * QB : base + n, :], 0.0),
                    axis=1,
                    keepdims=True,
                )
                p = jnp.exp(s - lse)
                dp = dot_nt(d, qkv_ref[base : base + n, 2 * w :])
                inner = jnp.sum(p * dp, axis=1, keepdims=True)
                ds = (p * (dp - inner)).astype(B16)
                dq_s[i * QB : n, :] += dot_nn(ds, qkv_ref[base : base + n, w : 2 * w] * scale)
                dk_s[:n, :] += dot_tn(ds, q)
                dv_s[:n, :] += dot_tn(p.astype(B16), d)
            pump(h)

        @pl.loop(0, blocks)
        def _(r):
            at = block(r)
            qk = jnp.concatenate([dq_s[at, :], dk_s[at, :]], axis=1)
            qk = rope(qk, cos_ref[at, :], lo_ref[at, :], hi_ref[at, :], -1)
            low = by_head(jnp.concatenate([qk, dv_s[at, :]], axis=1), heads).astype(B16)
            dqkv_s[k, swapped(r), :] = low
            small_ref[9:10, : 3 * w] += jnp.sum(low.astype(F32), axis=0, keepdims=True)

        for copy in latest:
            copy.wait_send()
        latest.clear()

        @pl.loop(0, half_blocks)
        def _(r):
            osend[block(r), :] = dot_nt(dqkv_s[k, block(r + half_blocks), :], qkvw_ref[...])
            piece(k, r).start()

        latest.extend(piece(k, r) for r in range(half_blocks))

    def piece(k, r):
        at = block(r)
        index = 16 + k * half_blocks + r
        return remote(osend.at[at, :], arecv.at[k, at, :], sems, index, core)

    def x_rows(k, r):
        if not first:
            return x_ref[block(r + k * half_blocks), :]
        return (far_ref if k else x_ref)[block(r), :].astype(F32)

    def fold(k):
        swaps[k][0].wait_recv()

        @pl.loop(0, half_blocks)
        def _(r):
            piece(k, r).wait_recv()
            at = block(r)
            d_na = dot_nt(dqkv_s[k, at, :], qkvw_ref[...]) + arecv[k, at, :]
            d_nb = dot_nt(dpre_s[k, at, :], up_ref[...]) + brecv[k, at, :]
            z, _ = standardize(x_rows(k, r))
            small_ref[0:1, :] += jnp.sum(d_na * z, axis=0, keepdims=True)
            small_ref[1:2, :] += jnp.sum(d_nb * z, axis=0, keepdims=True)
            small_ref[2:3, :] += jnp.sum(d_na, axis=0, keepdims=True)
            small_ref[3:4, :] += jnp.sum(d_nb, axis=0, keepdims=True)
            d_z = d_na * gain_ref[0:1, :] + d_nb * gain_ref[1:2, :]
            if k == 0:
                arecv[0, at, :] = d_z
            else:
                ysend[at, :] = d_z.astype(B16)

    def weight_grad(left, right, out):
        tiles = left.shape[1] // QB
        width = out.shape[1]

        def load(i):
            slot = lax.rem(i, 2)
            return pltpu.make_async_copy(left.at[:, block(i)], a_s.at[slot], a_sem.at[slot])

        def store(i):
            slot = lax.rem(i, 2)
            return pltpu.make_async_copy(
                o_s.at[slot, :, pl.ds(0, width)], out.at[block(i), :], o_sem.at[slot]
            )

        load(0).start()

        @pl.loop(0, tiles)
        def _(i):
            slot = lax.rem(i, 2)
            load(i).wait()

            @pl.when(i + 1 < tiles)
            def _():
                load(i + 1).start()

            @pl.when(i >= 2)
            def _():
                store(i - 2).wait()

            total = dot_tn(a_s[slot, :seq, :], right[0]) + dot_tn(a_s[slot, seq:, :], right[1])
            o_s[slot, :, :width] = total.astype(B16)
            store(i).start()

        for i in range(max(tiles - 2, 0), tiles):
            store(i).wait()

    if first:
        plan = {
            "feed0": "cd",
            "attend0 2": "cd",
            "near": "cd",
            "hid": "cd",
            "feed1 half": "c",
            "feed1": "ca",
            "nb": "a",
            "attend1 0": "c",
            "attend1 1": "a",
            "attend1 2": "c",
            "attend1 3": "a",
            "fold1": "a",
            "stats": "a",
            "na": "a",
        }
    else:
        plan = {
            "feed0": "a",
            "feed1": "a",
            "nb": "a",
            "attend1 0": "a",
            "attend1 3": "ab",
            "attend0 1": "ab",
            "fold0": "ab",
            "stats": "ab",
        }

    def pump(point):
        for name in plan.get(point, ""):
            sums[name].step()

    def at_heads(k):
        def at_head(h):
            for i in range(heads):
                if "attend%d %d" % (k, i) in plan:

                    @pl.when(h == i)
                    def _():
                        pump("attend%d %d" % (k, i))

        return at_head

    def early_grads():
        weight_grad(hid_h, g_s, down_g)
        pump("hid")
        weight_grad(ctx_ref, g_s, out_g)
        sums["a"].start()
        pump("ctx")

    near0.wait()
    if first:
        feed(0)
        pump("feed0")
        attend(0, at_heads(0))
        across.wait()
    near1 = remote(own_half(g_s, 1), other_half(g_s, 1), sems, 2, core)
    near1.start()
    pump("near")
    near1.wait()
    early_grads()
    if not first:
        feed(0)
        pump("feed0")
    feed(1)
    pump("feed1")
    weight_grad(nb_h, dpre_s, up_g)
    if not first:
        sums["b"].start()
    pump("nb")
    attend(1, at_heads(1))
    fold(1)
    back = remote(ysend, yrecv, sems, 7, far)
    back.start()
    next_rows = pltpu.make_async_copy(xn_h.at[pl.ds(0, rows), :], arecv.at[1], local.at[0])
    next_rows.start()
    pump("fold1")
    if not first:
        attend(0, at_heads(0))
    fold(0)
    pump("fold0")
    next_rows.wait()
    for copy in contexts:
        copy.wait()

    @pl.loop(0, half_blocks)
    def _(r):
        at = block(r)
        attn = dot_nn(cfull[at, :], outall_ref[...]) + ob_ref[...]
        x_next = arecv[1, at, :]
        feed_out = x_next - x_rows(0, r) - attn
        small_ref[5:6, :] += jnp.sum(x_next * x_next, axis=0, keepdims=True)
        small_ref[6:7, :] += jnp.sum(attn * attn, axis=0, keepdims=True)
        small_ref[7:8, :] += jnp.sum(feed_out * feed_out, axis=0, keepdims=True)

    pump("stats")
    near_sums = remote(small_ref.at[pl.ds(0, 8), :], got_s.at[0], sems, 11, core)
    near_sums.start()
    weight_grad(na_h, dqkv_s, qkv_g)
    near_sums.wait()
    small_ref[0:8, :] += got_s[0]
    far_sums = remote(small_ref.at[pl.ds(0, 8), :], got_s.at[1], sems, 12, far)
    far_sums.start()
    pump("na")
    back.wait()

    @pl.loop(0, half_blocks)
    def _(r):
        at = block(r)
        total = arecv[0, at, :] + yrecv[at, :].astype(F32)
        z, inverse = standardize(x_rows(0, r))
        slope = total - jnp.mean(total, axis=-1, keepdims=True)
        slope = slope - z * jnp.mean(total * z, axis=-1, keepdims=True)
        arecv[0, at, :] = grad_ref[at, :].astype(F32) + slope * inverse

    grad_out = pltpu.make_async_copy(arecv.at[0], dx_o, local.at[1])
    grad_out.start()
    far_sums.wait()
    small_ref[0:8, :] += got_s[1]
    for copy in latest:
        copy.wait_send()
    pump("end")
    for item in sums.values():
        item.finish()
    grad_out.wait()


def backward_layer(
    l,
    layers,
    grad,
    u,
    down,
    up,
    out_w,
    qkvw,
    tables,
    qkv,
    lse,
    ctx,
    xn,
    x,
    far_x,
    far_g,
    gains,
    ob,
    hidden,
    nb,
    na,
    ready,
):
    first, final = l == 0, l == layers - 1
    rows, features = grad.shape
    seq = 2 * rows
    w = qkvw.shape[2] // 3
    ff = up.shape[2]
    n = lax.axis_size("dp")
    down_shape, out_w_shape, up_shape, qkv_shape = (
        (ff, features),
        (w, features),
        (features, ff),
        (features, 3 * w),
    )
    shape = jax.ShapeDtypeStruct
    args = [grad, u, down, up, out_w, qkvw, *tables, qkv, lse, ctx, xn, x]
    in_specs = [VMEM] + [ANY] * 10 + [VMEM, ANY, VMEM]
    if first:
        args.append(far_x)
        in_specs.append(VMEM)
    if final:
        args.append(far_g)
        in_specs.append(VMEM)
    args += [gains, ob, hidden, nb, na, *ready]
    in_specs += [VMEM] * 2 + [ANY] * 3
    if first:
        in_specs += [VMEM, ANY]
    low = lambda shapes: [shape(item, B16) for item in shapes]
    out_shape = [shape((rows, features), F32), shape((16, features), F32)]
    out_shape += low([down_shape, out_w_shape, up_shape, qkv_shape, down_shape, out_w_shape])
    out_specs = [ANY, VMEM] + [ANY] * 6
    if first:
        out_shape += low([up_shape, qkv_shape])
        out_specs += [ANY] * 2
    else:
        out_shape += low([(features // n, ff)])
        out_specs += [VMEM]
    scratch = [
        pltpu.VMEM((2, seq, features), B16),
        pltpu.VMEM((2, seq, ff), B16),
        pltpu.VMEM((2, seq, 3 * w), B16),
        pltpu.VMEM((seq, w), F32),
        pltpu.VMEM((seq, w), F32),
        pltpu.VMEM((seq, w), F32),
        pltpu.VMEM((seq, w), B16),
        pltpu.VMEM((2, QB, ff), F32),
        pltpu.VMEM((rows, features), F32),
        pltpu.VMEM((2, rows, features), F32),
        pltpu.VMEM((2, rows, features), F32),
        pltpu.VMEM((rows, features), B16),
        pltpu.VMEM((rows, features), B16),
        pltpu.VMEM((rows, 4 * w), B16),
        pltpu.VMEM((2, 8, features), F32),
    ]
    scratch += [pltpu.VMEM(item.shape[1:], B16) for item in (down, up, out_w, qkvw)]
    scratch += [pltpu.VMEM((4 * w, features), B16)]
    scratch += [pltpu.VMEM(item.shape, F32) for item in tables]
    scratch += [pltpu.VMEM(qkv.shape, B16), pltpu.VMEM(lse.shape, F32)]
    scratch += [pltpu.VMEM((2, features), F32), pltpu.VMEM((1, features), F32)]
    sems = 16 + 2 * (rows // QB)
    scratch += [DMA((sems,)), DMA((sems,)), DMA((2,)), DMA((2,)), DMA((9,))]
    scratch += [pltpu.VMEM((2, 2 * seq, QB), B16), pltpu.VMEM((2, QB, features), B16)]
    scratch += [DMA((2,)), DMA((2,))]
    shapes = half_shapes(down_shape) + [out_w_shape]
    scratch += chunk_scratch(n, shapes) + Scatter.scratch(n, shapes) + Gather.scratch(n, 3)
    if not first:
        scratch += Scatter.scratch(n, half_shapes(up_shape))
    else:
        shapes = half_shapes(qkv_shape)
        scratch += chunk_scratch(n, shapes) + Scatter.scratch(n, shapes)
        scratch += Gather.scratch(n, 2) * 2
    return pl.pallas_call(
        functools.partial(backward_layer_kernel, l, first, final, rows, w, n),
        in_specs=in_specs,
        out_specs=out_specs,
        out_shape=out_shape,
        scratch_shapes=scratch,
        compiler_params=pltpu.CompilerParams(
            vmem_limit_bytes=63 * MIB, collective_id=layers + l, has_side_effects=True
        ),
        cost_estimate=pl.CostEstimate(
            flops=2 * 2 * seq * features * (3 * w + 2 * ff + w) * 2,
            bytes_accessed=40 * MIB,
            transcendentals=4 * seq * seq * w // HEAD,
        ),
        name="backward_layer",
    )(*args)


def on_group(
    tokens,
    cotangent,
    qkv_weight,
    qkv_bias,
    out_weight,
    out_bias,
    up_weight,
    up_bias,
    down_weight,
    down_bias,
    norm_gain,
    norm_shift,
):
    rows, features = tokens.shape
    tensor = lax.axis_size("tensor")
    dp = lax.axis_size("dp")
    w = qkv_weight.shape[2] // 3
    ff = up_weight.shape[2]
    tables = rope_tables(SEQ_LEN, 128)

    x = tokens
    stored = []
    far_x = None
    for l in range(LAYERS):
        got = forward_layer(
            l,
            LAYERS,
            x,
            up_weight,
            down_weight,
            qkv_weight,
            out_weight,
            tables,
            up_bias,
            qkv_bias,
            out_bias,
            down_bias,
            norm_gain,
            norm_shift,
            cotangent,
        )
        na, nb, u, hidden, qkv, ctx, lse, x_next = got[:8]
        if l == 0:
            far_x = got[8]
        if l == LAYERS - 1:
            far_g = got[8]
        stored.append((x, na, nb, u, hidden, qkv, ctx, lse, x_next))
        x = x_next
    output = x

    grad = cotangent
    down_sums, out_sums, up_sums, qkv_sums = ([None] * LAYERS for _ in range(4))
    ready = ()
    small = [None] * LAYERS
    for l in reversed(range(LAYERS)):
        x, na, nb, u, hidden, qkv, ctx, lse, x_next = stored[l]
        grad, small[l], *found = backward_layer(
            l,
            LAYERS,
            grad,
            u,
            down_weight,
            up_weight,
            out_weight,
            qkv_weight,
            tables,
            qkv,
            lse,
            ctx,
            x_next,
            x,
            far_x,
            far_g,
            norm_gain,
            out_bias,
            hidden,
            nb,
            na,
            ready,
        )
        down_sums[l], out_sums[l] = found[4:6]
        if l < LAYERS - 1:
            up_sums[l + 1], qkv_sums[l + 1] = found[6:]
        else:
            ready = (found[6], found[3])
    up_sums[0], qkv_sums[0], small = last_sums(found[2:4], jnp.concatenate(small), 2 * LAYERS)
    small = small.reshape(LAYERS, 16, features)
    down_all, up_all, qkv_all, out_w_all = (
        jnp.stack(item).astype(F32) for item in (down_sums, up_sums, qkv_sums, out_sums)
    )
    layer_stats = jnp.sqrt(jnp.sum(small[:, 5:8], axis=2) / (rows * dp * tensor * features))
    bias_all = small[:, 4]
    return (
        output,
        grad,
        qkv_all,
        small[:, 9, : 3 * w],
        out_w_all,
        bias_all,
        up_all,
        small[:, 8, :ff],
        down_all,
        bias_all,
        small[:, 0:2],
        small[:, 2:4],
        layer_stats,
    )


def solution(mesh):
    in_specs = (
        P(("dp", "tensor"), None),
        P(("dp", "tensor"), None),
        P(None, None, "tensor"),
        P(None, "tensor"),
        P(None, "tensor", None),
        P(),
        P(None, None, "tensor"),
        P(None, "tensor"),
        P(None, "tensor", None),
        P(),
        P(),
        P(),
    )
    out_specs = (
        P(("dp", "tensor"), None),
        P(("dp", "tensor"), None),
        P(None, None, "tensor"),
        P(None, "tensor"),
        P(None, "tensor", None),
        P(),
        P(None, None, "tensor"),
        P(None, "tensor"),
        P(None, "tensor", None),
        P(),
        P(),
        P(),
        P(),
    )
    small = mesh.shape["tensor"] == 4 and mesh.shape["dp"] == 8
    return jax.shard_map(
        on_group if small else on_device,
        mesh=mesh, in_specs=in_specs, out_specs=out_specs, check_vma=False
    )
```

```python
import functools
import math

import jax
import jax.numpy as jnp
import numpy as np
from jax import lax
from jax.experimental import pallas as pl
from jax.experimental.pallas import tpu as pltpu
from jax.sharding import PartitionSpec as P

HEAD = 64
ROT = 16
LAYERS = 2
SEQ_LEN = 1024
QB = 256
SCALE = HEAD ** (-0.5)

EPS = 1e-05
NEG = -1e30
F32 = jnp.float32
B16 = jnp.bfloat16
MIB = 1024 * 1024


def dot_nn(left, right):
    return lax.dot_general(left, right, (((1,), (0,)), ((), ())), preferred_element_type=F32)


def dot_nt(left, right):
    return lax.dot_general(left, right, (((1,), (1,)), ((), ())), preferred_element_type=F32)


def dot_tn(left, right):
    return lax.dot_general(left, right, (((0,), (0,)), ((), ())), preferred_element_type=F32)


def rope_tables(seq, width):
    positions = np.arange(seq, dtype=np.float32)
    inverse = np.exp(np.arange(ROT // 2, dtype=np.float32) * (-2.0 * math.log(10000.0) / ROT))
    angles = (positions[:, None] * inverse.astype(np.float32)[None, :]).astype(np.float64)
    cosine, sine = np.cos(angles), np.sin(angles)
    zero = np.zeros_like(sine)
    rest = np.zeros((seq, HEAD - ROT))
    repeat = lambda parts: jnp.asarray(
        np.tile(np.concatenate(parts, axis=1), (1, width // HEAD)).astype(np.float32)
    )
    return (
        repeat([cosine, cosine, rest + 1.0]),
        repeat([-sine, zero, rest]),
        repeat([zero, sine, rest]),
    )


def rope(rows, cos, sin_lo, sin_hi, sign):
    width = cos.shape[1]
    parts = []
    for j in range(rows.shape[1] // width):
        part = rows[:, j * width : (j + 1) * width]
        turned = (
            pltpu.roll(part, width - ROT // 2, 1) * sin_lo + pltpu.roll(part, ROT // 2, 1) * sin_hi
        )
        parts.append(part * cos + turned if sign > 0 else part * cos - turned)
    return parts[0] if len(parts) == 1 else jnp.concatenate(parts, axis=1)


def attend_forward_kernel(
    w, seq, x_ref, w_ref, b_ref, cos_ref, lo_ref, hi_ref, qkv_ref, ctx_ref, lse_ref
):
    h = pl.program_id(0)
    blocks = seq // QB
    shift = (lax.axis_index("tensor") % 2) * (blocks // 2)
    swapped = lambda i: pl.ds(pl.multiple_of(lax.rem(i + shift, blocks) * QB, QB), QB)

    @pl.when(h == 0)
    def _():
        lse_ref[...] = jnp.zeros_like(lse_ref)
        ctx_ref[...] = jnp.zeros_like(ctx_ref)

        @pl.loop(0, seq // QB)
        def _(r):
            rows = pl.ds(pl.multiple_of(r * QB, QB), QB)
            acc = dot_nn(x_ref[swapped(r), :], w_ref[...]) + b_ref[...]
            turned = rope(acc[:, : 2 * w], cos_ref[rows, :], lo_ref[rows, :], hi_ref[rows, :], 1)
            qkv_ref[rows, : 2 * w] = turned.astype(B16)
            qkv_ref[rows, 2 * w :] = acc[:, 2 * w :].astype(B16)

    mine = (lax.broadcasted_iota(jnp.int32, (1, w), 1) // HEAD) == h
    keep = jnp.where(mine, SCALE, 0.0).astype(B16)
    for i in range(seq // QB):
        n = (i + 1) * QB
        q = qkv_ref[i * QB : n, :w] * keep
        s = dot_nt(q, qkv_ref[:n, w : 2 * w])
        tri = lax.broadcasted_iota(jnp.int32, (QB, QB), 0) >= lax.broadcasted_iota(
            jnp.int32, (QB, QB), 1
        )
        last = jnp.where(tri, s[:, n - QB :], NEG)
        s = last if i == 0 else jnp.concatenate([s[:, : n - QB], last], axis=1)
        top = jnp.max(s, axis=1, keepdims=True)
        p = jnp.exp(s - top)
        total = jnp.sum(p, axis=1, keepdims=True)
        low = (p * (1.0 / total)).astype(B16)
        c = dot_nn(low, qkv_ref[:n, 2 * w :])
        old = ctx_ref[swapped(i), :]
        ctx_ref[swapped(i), :] = jnp.where(mine, c, old.astype(F32)).astype(B16)
        lane = lax.broadcasted_iota(jnp.int32, (QB, 128), 1)
        lse_ref[i * QB : n, :] = jnp.where(lane == h, top + jnp.log(total), lse_ref[i * QB : n, :])


def whole(shape):
    return pl.BlockSpec(shape, lambda h: (0,) * len(shape))


def attend_forward(x, weight, bias, tables):
    seq, features = x.shape
    w = weight.shape[1] // 3
    heads = w // HEAD
    table = tables[0].shape
    return pl.pallas_call(
        functools.partial(attend_forward_kernel, w, seq),
        grid=(heads,),
        in_specs=[
            whole((seq, features)),
            whole((features, 3 * w)),
            whole((1, 3 * w)),
            whole(table),
            whole(table),
            whole(table),
        ],
        out_specs=[whole((seq, 3 * w)), whole((seq, w)), whole((seq, 128))],
        out_shape=[
            jax.ShapeDtypeStruct((seq, 3 * w), B16),
            jax.ShapeDtypeStruct((seq, w), B16),
            jax.ShapeDtypeStruct((seq, 128), F32),
        ],
        compiler_params=pltpu.CompilerParams(
            vmem_limit_bytes=40 * MIB, dimension_semantics=("arbitrary",)
        ),
        cost_estimate=pl.CostEstimate(
            flops=2 * seq * features * 3 * w + 4 * seq * seq * 256 * heads,
            bytes_accessed=2 * seq * features + 6 * features * w + 8 * seq * w,
            transcendentals=seq * seq * heads // 2,
        ),
        name="attend_forward",
    )(x, weight, bias, *tables)


def attend_backward_kernel(
    w,
    seq,
    qkv_ref,
    d_ref,
    lse_ref,
    cos_ref,
    lo_ref,
    hi_ref,
    out_ref,
    bias_ref,
    dq_ref,
    dk_ref,
    dv_ref,
):
    h = pl.program_id(0)
    heads = w // HEAD
    blocks = seq // QB
    shift = (lax.axis_index("tensor") % 2) * (blocks // 2)
    swapped = lambda i: pl.ds(pl.multiple_of(lax.rem(i + shift, blocks) * QB, QB), QB)

    @pl.when(h == 0)
    def _():
        dq_ref[...] = jnp.zeros_like(dq_ref)
        dk_ref[...] = jnp.zeros_like(dk_ref)
        dv_ref[...] = jnp.zeros_like(dv_ref)

    mine = (lax.broadcasted_iota(jnp.int32, (1, w), 1) // HEAD) == h
    keep = jnp.where(mine, SCALE, 0.0).astype(B16)
    keep_value = jnp.where(mine, 1.0, 0.0).astype(B16)
    for i in range(seq // QB):
        n = (i + 1) * QB
        q = qkv_ref[i * QB : n, :w] * keep
        d = d_ref[swapped(i), :] * keep_value
        s = dot_nt(q, qkv_ref[:n, w : 2 * w])
        lane = lax.broadcasted_iota(jnp.int32, (QB, 128), 1)
        lse = jnp.sum(jnp.where(lane == h, lse_ref[i * QB : n, :], 0.0), axis=1, keepdims=True)
        tri = lax.broadcasted_iota(jnp.int32, (QB, QB), 0) >= lax.broadcasted_iota(
            jnp.int32, (QB, QB), 1
        )
        last = jnp.where(tri, s[:, n - QB :], NEG)
        s = last if i == 0 else jnp.concatenate([s[:, : n - QB], last], axis=1)
        p = jnp.exp(s - lse)
        dp = dot_nt(d, qkv_ref[:n, 2 * w :])
        inner = jnp.sum(p * dp, axis=1, keepdims=True)
        ds = (p * (dp - inner)).astype(B16)
        dq_ref[i * QB : n, :] += dot_nn(ds, qkv_ref[:n, w : 2 * w] * keep)
        dk_ref[:n, :] += dot_tn(ds, q)
        dv_ref[:n, :] += dot_tn(p.astype(B16), d)

    @pl.when(h == heads - 1)
    def _():
        bias_ref[...] = jnp.zeros_like(bias_ref)

        @pl.loop(0, seq // QB)
        def _(r):
            rows = pl.ds(pl.multiple_of(r * QB, QB), QB)
            qk = jnp.concatenate([dq_ref[rows, :], dk_ref[rows, :]], axis=1)
            qk = rope(qk, cos_ref[rows, :], lo_ref[rows, :], hi_ref[rows, :], -1).astype(B16)
            v = dv_ref[rows, :].astype(B16)
            out_ref[swapped(r), : 2 * w] = qk
            out_ref[swapped(r), 2 * w :] = v
            bias_ref[:, : 2 * w] += jnp.sum(qk.astype(F32), axis=0, keepdims=True)
            bias_ref[:, 2 * w :] += jnp.sum(v.astype(F32), axis=0, keepdims=True)


def attend_backward(qkv, d_context, lse, tables):
    seq = qkv.shape[0]
    w = qkv.shape[1] // 3
    heads = w // HEAD
    table = tables[0].shape
    return pl.pallas_call(
        functools.partial(attend_backward_kernel, w, seq),
        grid=(heads,),
        in_specs=[
            whole((seq, 3 * w)),
            whole((seq, w)),
            whole((seq, 128)),
            whole(table),
            whole(table),
            whole(table),
        ],
        out_specs=[whole((seq, 3 * w)), whole((1, 3 * w))],
        out_shape=[
            jax.ShapeDtypeStruct((seq, 3 * w), B16),
            jax.ShapeDtypeStruct((1, 3 * w), F32),
        ],
        scratch_shapes=[pltpu.VMEM((seq, w), F32)] * 3,
        compiler_params=pltpu.CompilerParams(
            vmem_limit_bytes=40 * MIB, dimension_semantics=("arbitrary",)
        ),
        cost_estimate=pl.CostEstimate(
            flops=10 * seq * seq * 256 * heads,
            bytes_accessed=16 * seq * w,
            transcendentals=seq * seq * heads // 2,
        ),
        name="attend_backward",
    )(qkv, d_context, lse, *tables)


def normal_parts(u):
    x = jnp.abs(u) * (0.5**0.5)
    t = 1.0 / (1.0 + 0.3275911 * x)
    bell = jnp.exp(-0.5 * u * u)
    poly = t * (
        0.254829592
        + t * (-0.284496736 + t * (1.421413741 + t * (-1.453152027 + t * 1.061405429)))
    )
    half_tail = 0.5 * poly * bell
    return jnp.where(u >= 0.0, 1.0 - half_tail, half_tail), bell


def gelu(u):
    return u * normal_parts(u)[0]


def gelu_slope(u):
    share, bell = normal_parts(u)
    return share + u * bell * ((2.0 * math.pi) ** -0.5)


def gelu_and_slope(u):
    share, bell = normal_parts(u)
    return u * share, share + u * bell * ((2.0 * math.pi) ** -0.5)


def standardize(x):
    average = jnp.mean(x, axis=-1, keepdims=True)
    centred = x - average
    variance = jnp.mean(centred * centred, axis=-1, keepdims=True)
    inverse = lax.rsqrt(variance + EPS)
    return centred * inverse, inverse


def swap(x, axis, bit):
    size = lax.axis_size(axis)
    return lax.ppermute(x, axis, [(i, i ^ bit) for i in range(size)])


def all_bits(size):
    bits = []
    bit = 1
    while bit < size:
        bits.append(bit)
        bit *= 2
    return bits


def after(x, *others):
    return lax.optimization_barrier((x,) + others)[0]


def on_device(
    tokens,
    cotangent,
    qkv_weight,
    qkv_bias,
    out_weight,
    out_bias,
    up_weight,
    up_bias,
    down_weight,
    down_bias,
    norm_gain,
    norm_shift,
):
    rows, features = tokens.shape
    tensor = lax.axis_size("tensor")
    dp = lax.axis_size("dp")
    chips = tensor // 2
    dp_index = lax.axis_index("dp")
    core = lax.axis_index("tensor") % 2
    w = qkv_weight.shape[2] // 3
    ff = up_weight.shape[2]
    heads = w // HEAD
    tables = rope_tables(SEQ_LEN, min(128, 2 * w))
    streams = range(chips)
    chip_bits = all_bits(chips)
    dp_bits = all_bits(dp)

    def core_gather(half):
        return jnp.concatenate([half, swap(half, "tensor", 1)], axis=0)

    def chip_gather(half):
        found = [half]
        for bit in chip_bits:
            found = found + [swap(item, "tensor", 2 * bit) for item in found]
        return found

    def chip_scatter(parts):
        for bit in reversed(chip_bits):
            sent = [swap(part.astype(B16), "tensor", 2 * bit) for part in parts[bit:]]
            parts = [part + got.astype(F32) for part, got in zip(parts[:bit], sent)]
        return parts[0]

    def chip_reduce(parts):
        for bit in chip_bits:
            low = [part.astype(B16) for part in parts]
            sent = [swap(part, "tensor", 2 * bit) for part in low]
            parts = [low[k].astype(F32) + sent[k ^ bit].astype(F32) for k in range(len(parts))]
        return parts

    def core_product(left, right, dot):
        got = swap(dot(left[rows:], right), "tensor", 1)
        return dot(left[:rows], right) + got

    def regroup(columns, back):
        lead = columns.shape[:-1]
        order = (3, heads, HEAD) if back else (heads, 3, HEAD)
        return jnp.swapaxes(columns.reshape(lead + order), -3, -2).reshape(columns.shape)

    qkv_w = [regroup(qkv_weight[l], False) for l in range(LAYERS)]
    qkv_b = [regroup(qkv_bias[l].astype(F32), False)[None] for l in range(LAYERS)]

    share = out_weight.shape[1] // dp
    piece = lax.dynamic_slice_in_dim(out_weight, dp_index * share, share, axis=1)
    near = [out_weight]
    for j in range(1, chips):
        near.append(lax.all_gather(swap(piece, "tensor", 2 * j), "dp", axis=1, tiled=True))
    far = [swap(item, "tensor", 1) for item in near]
    out_all = jnp.concatenate([x for pair in zip(near, far) for x in pair], axis=1)

    x_half = [t.astype(F32) for t in chip_gather(tokens)]
    stored = []
    stat_terms = []
    tick = tokens
    for l in range(LAYERS):
        final = l == LAYERS - 1
        gains = norm_gain[l].astype(F32)
        shifts = norm_shift[l].astype(F32)
        order = list(streams) if l == 0 else list(reversed(streams))
        na, nb, pre, hidden, ffn, qkv, ctx, lse, near = ([None] * chips for _ in range(9))
        up_b = up_bias[l].astype(F32)

        def feed(k):
            u = dot_nn(nb[k], up_weight[l]) + up_b
            pre[k] = u
            hidden[k] = gelu(u).astype(B16)
            ffn[k] = core_product(hidden[k], down_weight[l], dot_nn)

        def attend(k):
            qkv[k], ctx[k], lse[k] = attend_forward(na[k], qkv_w[l], qkv_b[l], tables)
            got = swap(ctx[k][rows:], "tensor", 1)
            near[k] = jnp.concatenate([ctx[k][:rows], got], axis=1)

        for k in order:
            z, _ = standardize(x_half[k])
            na[k] = core_gather((z * gains[0] + shifts[0]).astype(B16))
            nb[k] = core_gather((z * gains[1] + shifts[1]).astype(B16))
        if l == 0:
            for k in order:
                nb[k] = after(nb[k], tick)
                feed(k)
                na[k] = after(na[k], hidden[k])
                attend(k)
                tick = ctx[k]
        else:
            for k in order:
                nb[k] = after(nb[k], tick)
                feed(k)
                tick = hidden[k]
            for k in order:
                na[k] = after(na[k], tick)
                attend(k)
                tick = ctx[k]
        if final:
            ffn = [chip_scatter(ffn)]
        else:
            ffn = chip_reduce(ffn)
        x_next = []
        for k in streams if not final else range(1):
            blocks = [near[k]] + [swap(near[k ^ j], "tensor", 2 * j) for j in range(1, chips)]
            attn = dot_nn(jnp.concatenate(blocks, axis=1), out_all[l]) + out_bias[l].astype(F32)
            ffn_out = ffn[k] + down_bias[l].astype(F32)
            x_next.append(x_half[k] + attn + ffn_out)
            if k == 0:
                stat_terms.append(
                    jnp.stack(
                        [
                            jnp.sum(x_next[0] * x_next[0]),
                            jnp.sum(attn * attn),
                            jnp.sum(ffn_out * ffn_out),
                        ]
                    )
                )
        stored.append((x_half, na, nb, pre, hidden, qkv, ctx, lse))
        if l == 0:
            grad_low_half = chip_gather(after(cotangent, x_next[0]))
        x_half = x_next
    output = x_half[0]

    grad = cotangent.astype(F32)
    big = [None] * LAYERS
    small_all = [None] * LAYERS
    small_dp = [None] * LAYERS
    summed = None
    for l in reversed(range(LAYERS)):
        x_half, na, nb, pre, hidden, qkv, ctx, lse = stored[l]
        gains = norm_gain[l].astype(F32)
        low = grad.astype(B16)
        if l < LAYERS - 1:
            grad_low_half = chip_gather(low)
        g = [core_gather(item) for item in grad_low_half]
        g[0] = after(g[0], tick)
        d_pre, d_qkv, d_z = [None] * chips, [None] * chips, [None] * chips
        down_g = sum(dot_tn(hidden[k], g[k]) for k in streams)
        up_bias_g = jnp.zeros((ff,), F32)
        qkv_bias_g = jnp.zeros((1, 3 * w), F32)
        sums = 0.0
        for k in streams:
            d_pre[k] = (dot_nt(g[k], down_weight[l]) * gelu_slope(pre[k])).astype(B16)
            up_bias_g = up_bias_g + jnp.sum(d_pre[k], axis=0, dtype=F32)
        up_g = sum(dot_tn(nb[k], d_pre[k]) for k in streams)
        first = (down_g.astype(B16), up_g.astype(B16))
        if summed is not None:
            first = lax.optimization_barrier(first + summed[:1])[:2]
        first = lax.psum(first, "dp")
        tick = up_g
        for k in reversed(streams):
            d_ctx = dot_nt(g[k], out_weight[l]).astype(B16)
            d_qkv[k], bias_k = attend_backward(qkv[k], after(d_ctx, tick), lse[k], tables)
            tick = d_qkv[k]
            qkv_bias_g = qkv_bias_g + bias_k
            d_na = core_product(d_qkv[k], qkv_w[l], dot_nt)
            d_nb = core_product(d_pre[k], up_weight[l], dot_nt)
            z, inverse = standardize(x_half[k])
            sums = sums + jnp.stack(
                [
                    jnp.sum(d_na * z, axis=0),
                    jnp.sum(d_nb * z, axis=0),
                    jnp.sum(d_na, axis=0),
                    jnp.sum(d_nb, axis=0),
                ]
            )
            d_z[k] = d_na * gains[0] + d_nb * gains[1]
        total = chip_scatter(d_z)
        slope = total - jnp.mean(total, axis=-1, keepdims=True)
        slope = slope - z * jnp.mean(total * z, axis=-1, keepdims=True)
        bias_g = jnp.sum(low, axis=0, dtype=F32)
        grad = grad + slope * inverse
        out_g = sum(dot_tn(ctx[k], g[k]) for k in streams)
        qkv_g = sum(dot_tn(na[k], d_qkv[k]) for k in streams)
        second = (qkv_g.astype(B16), out_g.astype(B16))
        second = lax.optimization_barrier(second + first[:1])[:2]
        second = lax.psum(second, "dp")
        small_all[l] = jnp.concatenate(
            [sums, bias_g[None], jnp.pad(stat_terms[l], (0, features - 3))[None]], axis=0
        )
        small_dp[l] = jnp.concatenate([up_bias_g, qkv_bias_g[0]])
        big[l] = first + second
        summed = second
    small = jnp.stack(small_all)
    for bit in all_bits(tensor):
        small = small + swap(small, "tensor", bit)
    vector = jnp.stack(small_dp)
    for bit in dp_bits:
        small = small + swap(small, "dp", bit)
        vector = vector + swap(vector, "dp", bit)
    down_all = jnp.stack([item[0] for item in big]).astype(F32)
    up_all = jnp.stack([item[1] for item in big]).astype(F32)
    qkv_all = jnp.stack([regroup(item[2], True) for item in big]).astype(F32)
    out_w_all = jnp.stack([item[3] for item in big]).astype(F32)
    layer_stats = jnp.sqrt(small[:, 5, :3] / (rows * dp * tensor * features))
    bias_all = small[:, 4]
    return (
        output,
        grad,
        qkv_all,
        regroup(vector[:, ff:], True),
        out_w_all,
        bias_all,
        up_all,
        vector[:, :ff],
        down_all,
        bias_all,
        small[:, 0:2],
        small[:, 2:4],
        layer_stats,
    )


MESH = pl.DeviceIdType.MESH
ANY = pl.BlockSpec(memory_space=pl.ANY)
VMEM = pl.BlockSpec(memory_space=pltpu.VMEM)
DMA = pltpu.SemaphoreType.DMA


def partners():
    me = lax.axis_index("tensor")
    return me + 1 - 2 * lax.rem(me, 2), lax.rem(me + 2, 4)


def greet(others, more=0):
    barrier = pltpu.get_barrier_semaphore()
    for other in others:
        pl.semaphore_signal(barrier, inc=1, device_id={"tensor": other}, device_id_type=MESH)
    pl.semaphore_wait(barrier, len(others) + more)


def remote(src, dst, sems, index, target):
    return pltpu.make_async_remote_copy(
        src_ref=src,
        dst_ref=dst,
        send_sem=sems[0].at[index],
        recv_sem=sems[1].at[index],
        device_id={"tensor": target},
        device_id_type=MESH,
    )


def block(i, size=QB):
    return pl.ds(pl.multiple_of(i * size, size), size)


def loader(sems, **pairs):
    waiting = {}
    for i, (name, (src, dst)) in enumerate(pairs.items()):
        waiting[name] = pltpu.make_async_copy(src, dst, sems.at[i])
        waiting[name].start()

    def need(*names):
        for name in names:
            if name in waiting:
                waiting.pop(name).wait()

    return need


def by_kind(rows, heads):
    return jnp.concatenate(
        [
            rows[:, (3 * h + j) * HEAD : (3 * h + j + 1) * HEAD]
            for j in range(3)
            for h in range(heads)
        ],
        axis=1,
    )


def by_head(rows, heads):
    return jnp.concatenate(
        [
            rows[:, (heads * j + h) * HEAD : (heads * j + h + 1) * HEAD]
            for h in range(heads)
            for j in range(3)
        ],
        axis=1,
    )


def causal(s, n):
    tri = lax.broadcasted_iota(jnp.int32, (QB, QB), 0) >= lax.broadcasted_iota(
        jnp.int32, (QB, QB), 1
    )
    last = jnp.where(tri, s[:, n - QB :], NEG)
    return last if n == QB else jnp.concatenate([s[:, : n - QB], last], axis=1)


def forward_layer_kernel(l, first, final, rows, w, *refs):
    it = iter(refs)
    x_ref, up_h, down_h, qkvw_h, out_h, cos_h, lo_h, hi_h = (next(it) for _ in range(8))
    upb_h, qkvb_h, ob_h, db_h, gain_h, shift_h = (next(it) for _ in range(6))
    cot_ref = next(it) if final else None
    na_o, nb_o, u_o, hid_o, qkv_o, ctx_o, lse_o, x_o = (next(it) for _ in range(8))
    far_o = next(it) if first or final else None
    na_s, nb_s, u_s, hid_s, psend, precv, ysend, yrecv = (next(it) for _ in range(8))
    qkv_s, ctx_s, lse_s = (next(it) for _ in range(3))
    far_s = next(it) if first or final else None
    mine_s = next(it)
    up_ref, down_ref, qkvw_ref, out_ref, cos_ref, lo_ref, hi_ref = (next(it) for _ in range(7))
    upb_ref, qkvb_ref, ob_ref, gain_ref, shift_ref = (next(it) for _ in range(5))
    send, recv, local, u_sem, load_sem = (next(it) for _ in range(5))
    sems = (send, recv)
    need = loader(
        load_sem,
        up=(up_h.at[l], up_ref),
        qkvw=(qkvw_h.at[l], qkvw_ref),
        cos=(cos_h, cos_ref),
        lo=(lo_h, lo_ref),
        hi=(hi_h, hi_ref),
        down=(down_h.at[l], down_ref),
        out=(out_h.at[l], out_ref),
    )

    seq = 2 * rows
    heads = w // HEAD
    blocks = seq // QB
    half_blocks = rows // QB
    shift = lax.rem(lax.axis_index("tensor"), 2) * half_blocks
    core, far = partners()
    upb_ref[...] = upb_h[l : l + 1, :].astype(F32)
    qkvb_ref[...] = qkvb_h[l : l + 1, :].astype(F32)
    ob_ref[...] = ob_h[l : l + 1, :].astype(F32) + db_h[l : l + 1, :].astype(F32)
    gain_ref[...] = gain_h[l].astype(F32)
    shift_ref[...] = shift_h[l].astype(F32)
    greet((core, far))
    outs = []

    def keep(src, dst, index):
        copy = pltpu.make_async_copy(src, dst, local.at[index])
        copy.start()
        outs.append(copy)

    far_copy = None
    if first or final:
        far_copy = remote(x_ref if first else cot_ref, far_s, sems, 0, far)
        far_copy.start()

    def x_rows(k, r):
        if not first:
            return x_ref[block(r + k * half_blocks), :]
        return (far_s if k else x_ref)[block(r), :].astype(F32)

    gathers = {}

    def norms(k):
        @pl.loop(0, half_blocks)
        def _(r):
            z, _ = standardize(x_rows(k, r))
            na_s[k, block(r), :] = (z * gain_ref[0:1, :] + shift_ref[0:1, :]).astype(B16)
            nb_s[k, block(r), :] = (z * gain_ref[1:2, :] + shift_ref[1:2, :]).astype(B16)

        gathers[k] = []
        for at, buf in ((0, nb_s), (1, na_s)):
            copy = remote(
                buf.at[k, pl.ds(0, rows), :],
                buf.at[k, pl.ds(rows, rows), :],
                sems,
                1 + 2 * k + at,
                core,
            )
            copy.start()
            gathers[k].append(copy)

    products = {}
    u_out = []

    def feed(k):
        gathers[k][0].wait()
        need("up")
        keep(nb_s.at[k], nb_o.at[pl.ds(k * seq, seq), :], 2 * k)
        for h in (1, 0):
            for copy in u_out:
                copy.wait()
            u_out.clear()

            @pl.loop(0, half_blocks)
            def _(r):
                at = block(r + h * half_blocks)
                u = dot_nn(nb_s[k, at, :], up_ref[...]) + upb_ref[...]
                value, slope = gelu_and_slope(u)
                u_s[r] = slope
                hid_s[k, at, :] = value.astype(B16)

            for r in range(half_blocks):
                copy = pltpu.make_async_copy(
                    u_s.at[r], u_o.at[pl.ds(k * seq + h * rows + r * QB, QB), :], u_sem.at[r]
                )
                copy.start()
                u_out.append(copy)
        keep(hid_s.at[k], hid_o.at[pl.ds(k * seq, seq), :], 2 * k + 1)

    def join(k):
        need("down", "out")

        @pl.loop(0, half_blocks)
        def _(r):
            at = block(r + half_blocks)
            psend[k, block(r), :] = dot_nn(hid_s[k, at, :], down_ref[...]) + dot_nn(
                ctx_s[k, at, :], out_ref[...]
            )

        product = remote(psend.at[k], precv.at[k], sems, 5 + k, core)
        product.start()
        products[k] = product

        @pl.loop(0, half_blocks)
        def _(r):
            at = block(r)
            mine_s[at, :] = dot_nn(hid_s[k, at, :], down_ref[...]) + dot_nn(
                ctx_s[k, at, :], out_ref[...]
            )

        product.wait_recv()

        @pl.loop(0, half_blocks)
        def _(r):
            at = block(r)
            total = precv[k, at, :] + mine_s[at, :]
            precv[k, at, :] = total
            if not (final and k == 0):
                ysend[k, at, :] = total.astype(B16)

        if not (final and k == 0):
            sums[k] = remote(ysend.at[k], yrecv.at[1 - k], sems, 7 + k, far)
            sums[k].start()

    sums = {}

    def attend(k):
        gathers[k][1].wait()
        need("qkvw", "cos", "lo", "hi")
        keep(na_s.at[k], na_o.at[pl.ds(k * seq, seq), :], 4 + 2 * k)
        swapped = lambda i: block(lax.rem(i + shift, blocks))

        @pl.loop(0, blocks)
        def _(r):
            acc = dot_nn(na_s[k, swapped(r), :], qkvw_ref[...]) + qkvb_ref[...]
            acc = by_kind(acc, heads)
            turned = rope(
                acc[:, : 2 * w], cos_ref[block(r), :], lo_ref[block(r), :], hi_ref[block(r), :], 1
            )
            qkv_s[k, block(r), : 2 * w] = turned.astype(B16)
            qkv_s[k, block(r), 2 * w :] = acc[:, 2 * w :].astype(B16)
            ctx_s[k, block(r), :] = jnp.zeros((QB, w), B16)
            lse_s[k, block(r), :] = jnp.zeros((QB, 128), F32)

        @pl.loop(0, heads)
        def _(h):
            mine = (lax.broadcasted_iota(jnp.int32, (1, w), 1) // HEAD) == h
            scale = jnp.where(mine, SCALE, 0.0).astype(B16)
            lane = lax.broadcasted_iota(jnp.int32, (QB, 128), 1)
            for i in range(blocks):
                n = (i + 1) * QB
                q = qkv_s[k, i * QB : n, :w] * scale
                s = causal(dot_nt(q, qkv_s[k, :n, w : 2 * w]), n)
                top = jnp.max(s, axis=1, keepdims=True)
                p = jnp.exp(s - top)
                total = jnp.sum(p, axis=1, keepdims=True)
                low = (p * (1.0 / total)).astype(B16)
                c = dot_nn(low, qkv_s[k, :n, 2 * w :])
                old = ctx_s[k, swapped(i), :]
                ctx_s[k, swapped(i), :] = jnp.where(mine, c, old.astype(F32)).astype(B16)
                lse_s[k, i * QB : n, :] = jnp.where(
                    lane == h, top + jnp.log(total), lse_s[k, i * QB : n, :]
                )

        keep(qkv_s.at[k], qkv_o.at[pl.ds(k * seq, seq), :], 5 + 2 * k)
        keep(ctx_s.at[k], ctx_o.at[pl.ds(k * seq, seq), :], 8 + 2 * k)
        keep(lse_s.at[k], lse_o.at[pl.ds(k * seq, seq), :], 9 + 2 * k)

    def finish(k):
        sums[1 - k].wait_recv()

        @pl.loop(0, half_blocks)
        def _(r):
            at = block(r)
            both = precv[k, at, :] + yrecv[k, at, :].astype(F32)
            precv[k, at, :] = x_rows(k, r) + (both + ob_ref[...])

        keep(precv.at[k], x_o.at[pl.ds(k * rows, rows), :], 12 + k)

    if first:
        norms(0)
        feed(0)
        attend(0)
        join(0)
        far_copy.wait_recv()
        norms(1)
        feed(1)
        attend(1)
        join(1)
    else:
        norms(1)
        norms(0)
        feed(1)
        attend(1)
        join(1)
        feed(0)
        attend(0)
        join(0)
    if final and not first:
        far_copy.wait_recv()
    if first or final:
        keep(far_s, far_o, 14)
    finish(0)
    if not final:
        finish(1)

    if first or final:
        far_copy.wait_send()
    for copy in u_out + outs:
        copy.wait()
    for copy in products.values():
        copy.wait_send()
    for copy in sums.values():
        copy.wait_send()


def forward_layer(
    l, layers, x, up, down, qkvw, out, tables, upb, qkvb, ob, db, gains, shifts, cot
):
    first, final = l == 0, l == layers - 1
    features = x.shape[1]
    rows = x.shape[0] if first else x.shape[0] // 2
    seq = 2 * rows
    w = qkvw.shape[2] // 3
    ff = up.shape[2]
    shape = jax.ShapeDtypeStruct
    out_shape = [
        shape((2 * seq, features), B16),
        shape((2 * seq, features), B16),
        shape((2 * seq, ff), F32),
        shape((2 * seq, ff), B16),
        shape((2 * seq, 3 * w), B16),
        shape((2 * seq, w), B16),
        shape((2 * seq, 128), F32),
        shape((rows if final else 2 * rows, features), F32),
    ]
    if first or final:
        out_shape.append(shape((rows, features), B16))
    args = [x, up, down, qkvw, out, *tables, upb, qkvb, ob, db, gains, shifts]
    if final:
        args.append(cot)
    scratch = [
        pltpu.VMEM((2, seq, features), B16),
        pltpu.VMEM((2, seq, features), B16),
        pltpu.VMEM((rows // QB, QB, ff), F32),
        pltpu.VMEM((2, seq, ff), B16),
        pltpu.VMEM((2, rows, features), F32),
        pltpu.VMEM((2, rows, features), F32),
        pltpu.VMEM((2, rows, features), B16),
        pltpu.VMEM((2, rows, features), B16),
        pltpu.VMEM((2, seq, 3 * w), B16),
        pltpu.VMEM((2, seq, w), B16),
        pltpu.VMEM((2, seq, 128), F32),
    ]
    if first or final:
        scratch.append(pltpu.VMEM((rows, features), B16))
    scratch.append(pltpu.VMEM((rows, features), F32))
    scratch += [pltpu.VMEM(item.shape[1:], B16) for item in (up, down, qkvw, out)]
    scratch += [pltpu.VMEM(item.shape, F32) for item in tables]
    scratch += [pltpu.VMEM((1, width), F32) for width in (ff, 3 * w, features)]
    scratch += [pltpu.VMEM((2, features), F32)] * 2
    scratch += [DMA((9,)), DMA((9,)), DMA((15,)), DMA((rows // QB,)), DMA((7,))]
    return pl.pallas_call(
        functools.partial(forward_layer_kernel, l, first, final, rows, w),
        in_specs=[VMEM] + [ANY] * 7 + [VMEM] * (len(args) - 8),
        out_specs=[ANY] * len(out_shape),
        out_shape=out_shape,
        scratch_shapes=scratch,
        compiler_params=pltpu.CompilerParams(
            vmem_limit_bytes=63 * MIB, collective_id=l, has_side_effects=True
        ),
        cost_estimate=pl.CostEstimate(
            flops=2 * 2 * seq * features * (3 * w + 2 * ff + w) * 2,
            bytes_accessed=40 * MIB,
            transcendentals=4 * seq * seq * w // HEAD,
        ),
        name="forward_layer",
    )(*args)


def ring_place(index, size):
    side = lax.rem(index, 2)
    level = index // 2
    return level * (1 - side) + (size - 1 - level) * side


def ring_device(place, size):
    side = place // (size // 2)
    return (1 - side) * 2 * place + side * (2 * (size - 1 - place) + 1)


class Ring:
    def __init__(self, n):
        self.n = n
        self.place = ring_place(lax.axis_index("dp"), n)
        self.targets = (
            ring_device(lax.rem(self.place + 1, n), n),
            ring_device(lax.rem(self.place + n - 1, n), n),
        )
        self.steps = n // 2

    def greet(self):
        barrier = pltpu.get_barrier_semaphore()
        for other in self.targets:
            pl.semaphore_signal(barrier, inc=1, device_id={"dp": other}, device_id_type=MESH)

    def rows(self, array, offset):
        size = array.shape[0] // self.n
        chunk = lax.rem(self.place + offset + 2 * self.n, self.n)
        return pl.ds(pl.multiple_of(chunk * size, size), size)

    def copy(self, src, dst, sems, at, way):
        return pltpu.make_async_remote_copy(
            src_ref=src,
            dst_ref=dst,
            send_sem=sems[0].at[at],
            recv_sem=sems[1].at[at],
            device_id={"dp": self.targets[way]},
            device_id_type=MESH,
        )


class Scatter:
    def __init__(self, ring, ins, turns, chunk, it):
        self.ring, self.ins, self.turns, self.chunk = ring, ins, turns, chunk
        self.slots = [next(it) for _ in ins]
        self.mine = [next(it) for _ in ins]
        self.sems = (next(it), next(it))
        self.load = next(it)
        self.parts = [(a, way) for a in range(len(ins)) for way in (0, 1)]

    @staticmethod
    def scratch(n, shapes, dtypes=None):
        count = len(shapes)
        kinds = [(a, b, B16) for a, b in shapes]
        if dtypes:
            kinds = [(a, b, dtype) for (a, b), dtype in zip(shapes, dtypes)]
        return (
            [pltpu.VMEM((2, n // 2, a // n, b), dtype) for a, b, dtype in kinds]
            + [pltpu.VMEM((2, a // n, b), dtype) for a, b, dtype in kinds]
            + [DMA((count, 2, n // 2)), DMA((count, 2, n // 2)), DMA((count, 2))]
        )

    def steps(self, a, way):
        return self.ring.steps - (way ^ self.turns[a])

    def rows(self, a, way, offset):
        return self.ring.rows(self.ins[a], -offset if way else offset)

    def sent(self, a, way, step):
        if step:
            src = self.slots[a].at[way, step - 1]
        else:
            src = self.ins[a].at[self.rows(a, way, self.steps(a, way)), :]
        return self.ring.copy(src, self.slots[a].at[way, step], self.sems, (a, way, step), way)

    def fetch(self, a, way, step):
        at = self.rows(a, way, self.steps(a, way) - step - 1)
        return pltpu.make_async_copy(
            self.ins[a].at[at, :], self.mine[a].at[way], self.load.at[a, way]
        )

    def start(self):
        for part in self.parts:
            self.sent(*part, 0).start()
        for part in self.parts:
            self.fetch(*part, 0).start()

    def step(self, step):
        for a, way in self.parts:
            steps = self.steps(a, way)
            if step >= steps:
                continue
            self.sent(a, way, step).wait_recv()
            if step + 1 < steps:
                self.fetch(a, way, step).wait()
                total = self.slots[a][way, step].astype(F32) + self.mine[a][way].astype(F32)
                self.slots[a][way, step] = total.astype(self.slots[a].dtype)
                self.sent(a, way, step + 1).start()
                if way == 0 or step + 2 < steps:
                    self.fetch(a, way, step + 1).start()
        if step == self.ring.steps - 1:
            for a in range(len(self.ins)):
                self.fetch(a, 0, self.steps(a, 0) - 1).wait()
                total = self.mine[a][0].astype(F32)
                for way in (0, 1):
                    total = total + self.slots[a][way, self.steps(a, way) - 1].astype(F32)
                self.chunk[a][...] = total.astype(self.chunk[a].dtype)

    def finish(self):
        for part in self.parts:
            for step in range(self.steps(*part)):
                self.sent(*part, step).wait_send()


class Gather:
    def __init__(self, ring, chunk, turns, done, it):
        self.ring, self.chunk, self.turns, self.done = ring, chunk, turns, done
        self.sems = (next(it), next(it))
        self.local = next(it)
        self.parts = [(a, way) for a in range(len(chunk)) for way in (0, 1)]

    @staticmethod
    def scratch(n, count):
        return [DMA((count, 2, n // 2)), DMA((count, 2, n // 2)), DMA((count,))]

    steps = Scatter.steps

    def sent(self, a, way, step):
        at = self.ring.rows(self.done[a], step if way else -step)
        src = self.done[a].at[at, :] if step else self.chunk[a]
        return self.ring.copy(src, self.done[a].at[at, :], self.sems, (a, way, step), way)

    def own(self, a):
        at = self.ring.rows(self.done[a], 0)
        return pltpu.make_async_copy(self.chunk[a], self.done[a].at[at, :], self.local.at[a])

    def start(self):
        for part in self.parts:
            self.sent(*part, 0).start()
        for a in range(len(self.chunk)):
            self.own(a).start()

    def step(self, step):
        for a, way in self.parts:
            steps = self.steps(a, way)
            if step < steps:
                self.sent(a, way, step).wait_recv()
                if step + 1 < steps:
                    self.sent(a, way, step + 1).start()

    def finish(self):
        for part in self.parts:
            for step in range(self.steps(*part)):
                self.sent(*part, step).wait_send()
        for a in range(len(self.chunk)):
            self.own(a).wait()


class Total:
    def __init__(self, scatter, gather):
        self.phases = [item for item in (scatter, gather) if item is not None]
        self.steps = self.phases[0].ring.steps
        self.at = 0

    def start(self):
        self.phases[0].start()

    def step(self):
        which, step = divmod(self.at, self.steps)
        self.phases[which].step(step)
        self.at += 1
        if step == self.steps - 1 and which + 1 < len(self.phases):
            self.phases[which + 1].start()

    def finish(self):
        while self.at < len(self.phases) * self.steps:
            self.step()
        for item in self.phases:
            item.finish()


def halves(ref):
    width = ref.shape[1] // 2
    return [ref.at[:, pl.ds(0, width)], ref.at[:, pl.ds(width, width)]]


def half_shapes(shape):
    return [(shape[0], shape[1] // 2)] * 2


def chunk_scratch(n, shapes):
    return [pltpu.VMEM((a // n, b), B16) for a, b in shapes]


def last_sums_kernel(n, count, *refs):
    it = iter(refs)
    ins = [item for _ in range(count) for item in halves(next(it))]
    small_in = next(it)
    done = [item for _ in range(count) for item in halves(next(it))]
    small_out = next(it)
    small_s, small_d = next(it), next(it)
    ring = Ring(n)
    turns = (0, 1) * count + (0,)
    ins.append(small_s)
    done.append(small_d)
    chunk = [next(it) for _ in ins]
    total = Total(Scatter(ring, ins, turns, chunk, it), Gather(ring, chunk, turns, done, it))
    ring.greet()
    rows, width = small_in.shape[0], small_in.shape[1] // 2
    small_s[:rows, :] = small_in[:, :width]
    small_s[rows:, :] = small_in[:, width:]
    pl.semaphore_wait(pltpu.get_barrier_semaphore(), 2)
    total.start()
    total.finish()
    small_out[:, :width] = small_d[:rows, :]
    small_out[:, width:] = small_d[rows:, :]


def last_sums(arrays, small, collective_id):
    n = lax.axis_size("dp")
    shape = jax.ShapeDtypeStruct
    count = len(arrays)
    folded = (2 * small.shape[0], small.shape[1] // 2)
    shapes = [half for item in arrays for half in half_shapes(item.shape)] + [folded]
    dtypes = [B16] * (2 * count) + [F32]
    return pl.pallas_call(
        functools.partial(last_sums_kernel, n, count),
        in_specs=[ANY] * count + [VMEM],
        out_specs=[ANY] * count + [VMEM],
        out_shape=[shape(item.shape, B16) for item in arrays] + [shape(small.shape, F32)],
        scratch_shapes=[pltpu.VMEM(folded, F32)] * 2
        + [pltpu.VMEM((a // n, b), dtype) for (a, b), dtype in zip(shapes, dtypes)]
        + Scatter.scratch(n, shapes, dtypes)
        + Gather.scratch(n, len(shapes)),
        compiler_params=pltpu.CompilerParams(
            vmem_limit_bytes=40 * MIB, collective_id=collective_id, has_side_effects=True
        ),
        cost_estimate=pl.CostEstimate(
            flops=arrays[0].size, bytes_accessed=200 * MIB, transcendentals=0
        ),
        name="last_sums",
    )(*arrays, small)


def backward_layer_kernel(l, first, final, rows, w, n, *refs):
    it = iter(refs)
    grad_ref, u_ref, down_h, up_h, ow_h, qkvw_h = (next(it) for _ in range(6))
    cos_h, lo_h, hi_h = (next(it) for _ in range(3))
    qkv_h, lse_h, ctx_ref, xn_h, x_ref = (next(it) for _ in range(5))
    far_ref = next(it) if first else None
    farg_ref = next(it) if final else None
    gain_h, ob_h = (next(it) for _ in range(2))
    hid_h, nb_h, na_h = (next(it) for _ in range(3))
    chunk_in, ready = (next(it), next(it)) if first else (None, None)
    dx_o, small_ref = (next(it) for _ in range(2))
    down_g, out_g, up_g, qkv_g, down_done, out_done = (next(it) for _ in range(6))
    up_chunk = None if first else next(it)
    up_done, ready_done = (next(it), next(it)) if first else (None, None)
    g_s, dpre_s, dqkv_s, dq_s, dk_s, dv_s, dctx_s = (next(it) for _ in range(7))
    u_s, osend, brecv, arecv, ysend, yrecv = (next(it) for _ in range(6))
    cfull, got_s = (next(it) for _ in range(2))
    down_ref, up_ref, ow_ref, qkvw_ref, outall_ref = (next(it) for _ in range(5))
    cos_ref, lo_ref, hi_ref, qkv_ref, lse_ref = (next(it) for _ in range(5))
    gain_ref, ob_ref = (next(it) for _ in range(2))
    send, recv, local, u_sem, load_sem = (next(it) for _ in range(5))
    sems = (send, recv)
    a_s, o_s, a_sem, o_sem = (next(it) for _ in range(4))
    ring = Ring(n)
    sums = {}
    turns = (0, 1, 0)
    chunk = [next(it) for _ in range(3)]
    sums["a"] = Total(
        Scatter(ring, halves(down_g) + [out_g], turns, chunk, it),
        Gather(ring, chunk, turns, halves(down_done) + [out_done], it),
    )
    if not first:
        sums["b"] = Total(Scatter(ring, halves(up_g), turns, halves(up_chunk), it), None)
    else:
        chunk = [next(it) for _ in range(2)]
        sums["c"] = Total(
            Scatter(ring, halves(ready), turns, chunk, it),
            Gather(ring, chunk, turns, halves(ready_done), it),
        )
        sums["d"] = Total(None, Gather(ring, halves(chunk_in), turns, halves(up_done), it))
    need = loader(
        load_sem,
        down=(down_h.at[l], down_ref),
        up=(up_h.at[l], up_ref),
        ow=(ow_h.at[l], ow_ref),
        qkv=(qkv_h, qkv_ref),
        lse=(lse_h, lse_ref),
        cos=(cos_h, cos_ref),
        lo=(lo_h, lo_ref),
        hi=(hi_h, hi_ref),
        qkvw=(qkvw_h.at[l], qkvw_ref),
    )

    seq = 2 * rows
    ff = up_ref.shape[1]
    heads = w // HEAD
    blocks = seq // QB
    half_blocks = rows // QB
    shift = lax.rem(lax.axis_index("tensor"), 2) * half_blocks
    swapped = lambda i: block(lax.rem(i + shift, blocks))
    core, far = partners()
    diag = lax.rem(core + 2, 4)
    ring.greet()
    greet((core, far, diag), 2)
    def load_u(k, i):
        return pltpu.make_async_copy(
            u_ref.at[pl.ds(k * seq + i * QB, QB), :], u_s.at[i % 2], u_sem.at[i % 2]
        )

    small_ref[...] = jnp.zeros_like(small_ref)
    gain_ref[...] = gain_h[l].astype(F32)
    ob_ref[...] = ob_h[l : l + 1, :].astype(F32)
    load_u(0, 0).start()
    load_u(0, 1).start()

    @pl.loop(0, half_blocks)
    def _(r):
        low = grad_ref[block(r), :].astype(B16)
        g_s[0, block(r), :] = low
        small_ref[4:5, :] += jnp.sum(low.astype(F32), axis=0, keepdims=True)

    own_half = lambda buf, k: buf.at[k, pl.ds(0, rows), :]
    other_half = lambda buf, k: buf.at[k, pl.ds(rows, rows), :]
    if final:
        g_s[1, :rows, :] = farg_ref[...]
    else:
        across = remote(own_half(g_s, 0), own_half(g_s, 1), sems, 0, far)
        across.start()
    near0 = remote(own_half(g_s, 0), other_half(g_s, 0), sems, 1, core)
    near0.start()
    if first:
        sums["c"].start()
        sums["d"].start()
    cfull[:, :w] = ctx_ref[:rows, :]
    contexts = [
        remote(ctx_ref.at[pl.ds(rows, rows), :], cfull.at[:, pl.ds(w, w)], sems, 8, core),
        remote(ctx_ref.at[pl.ds(seq, rows), :], cfull.at[:, pl.ds(2 * w, w)], sems, 9, far),
        remote(ctx_ref.at[pl.ds(seq + rows, rows), :], cfull.at[:, pl.ds(3 * w, w)], sems, 10, diag),
    ]
    need("ow")
    outall_ref[:w, :] = ow_ref[...]
    for i, other in enumerate((core, far, diag)):
        contexts.append(
            remote(ow_ref, outall_ref.at[pl.ds((i + 1) * w, w), :], sems, 13 + i, other)
        )
    for copy in contexts:
        copy.start()

    swaps = {}
    latest = []

    def feed(k):
        need("down")
        for i in range(blocks):
            load_u(k, i).wait()
            at = pl.ds(i * QB, QB)
            d_hidden = dot_nt(g_s[k, at, :], down_ref[...])
            d_pre = (d_hidden * u_s[i % 2]).astype(B16)
            dpre_s[k, at, :] = d_pre
            small_ref[8:9, :ff] += jnp.sum(d_pre.astype(F32), axis=0, keepdims=True)
            if i + 2 < blocks:
                load_u(k, i + 2).start()
            elif k == 0:
                load_u(1, i + 2 - blocks).start()
            if 2 * (i + 1) == blocks:
                pump("feed%d half" % k)

        need("up")
        for copy in latest:
            copy.wait_send()
        latest.clear()

        @pl.loop(0, half_blocks)
        def _(r):
            osend[block(r), :] = dot_nt(dpre_s[k, block(r + half_blocks), :], up_ref[...])

        swaps[k] = [remote(osend, brecv.at[k], sems, 3 + 2 * k, core)]
        swaps[k][0].start()
        latest.append(swaps[k][0])

    def attend(k, pump):
        need("ow", "qkv", "lse", "cos", "lo", "hi", "qkvw")

        @pl.loop(0, blocks)
        def _(r):
            dctx_s[block(r), :] = dot_nt(g_s[k, swapped(r), :], ow_ref[...]).astype(B16)
            dq_s[block(r), :] = jnp.zeros((QB, w), F32)
            dk_s[block(r), :] = jnp.zeros((QB, w), F32)
            dv_s[block(r), :] = jnp.zeros((QB, w), F32)

        base = k * seq

        @pl.loop(0, heads)
        def _(h):
            mine = (lax.broadcasted_iota(jnp.int32, (1, w), 1) // HEAD) == h
            scale = jnp.where(mine, SCALE, 0.0).astype(B16)
            only = jnp.where(mine, 1.0, 0.0).astype(B16)
            lane = lax.broadcasted_iota(jnp.int32, (QB, 128), 1)
            for i in range(blocks):
                n = (i + 1) * QB
                q = qkv_ref[base + i * QB : base + n, :w] * scale
                d = dctx_s[i * QB : n, :] * only
                s = causal(dot_nt(q, qkv_ref[base : base + n, w : 2 * w]), n)
                lse = jnp.sum(
                    jnp.where(lane == h, lse_ref[base + i * QB : base + n, :], 0.0),
                    axis=1,
                    keepdims=True,
                )
                p = jnp.exp(s - lse)
                dp = dot_nt(d, qkv_ref[base : base + n, 2 * w :])
                inner = jnp.sum(p * dp, axis=1, keepdims=True)
                ds = (p * (dp - inner)).astype(B16)
                dq_s[i * QB : n, :] += dot_nn(ds, qkv_ref[base : base + n, w : 2 * w] * scale)
                dk_s[:n, :] += dot_tn(ds, q)
                dv_s[:n, :] += dot_tn(p.astype(B16), d)
            pump(h)

        @pl.loop(0, blocks)
        def _(r):
            at = block(r)
            qk = jnp.concatenate([dq_s[at, :], dk_s[at, :]], axis=1)
            qk = rope(qk, cos_ref[at, :], lo_ref[at, :], hi_ref[at, :], -1)
            low = by_head(jnp.concatenate([qk, dv_s[at, :]], axis=1), heads).astype(B16)
            dqkv_s[k, swapped(r), :] = low
            small_ref[9:10, : 3 * w] += jnp.sum(low.astype(F32), axis=0, keepdims=True)

        for copy in latest:
            copy.wait_send()
        latest.clear()

        @pl.loop(0, half_blocks)
        def _(r):
            osend[block(r), :] = dot_nt(dqkv_s[k, block(r + half_blocks), :], qkvw_ref[...])
            piece(k, r).start()

        latest.extend(piece(k, r) for r in range(half_blocks))

    def piece(k, r):
        at = block(r)
        index = 16 + k * half_blocks + r
        return remote(osend.at[at, :], arecv.at[k, at, :], sems, index, core)

    def x_rows(k, r):
        if not first:
            return x_ref[block(r + k * half_blocks), :]
        return (far_ref if k else x_ref)[block(r), :].astype(F32)

    def fold(k):
        swaps[k][0].wait_recv()

        @pl.loop(0, half_blocks)
        def _(r):
            piece(k, r).wait_recv()
            at = block(r)
            d_na = dot_nt(dqkv_s[k, at, :], qkvw_ref[...]) + arecv[k, at, :]
            d_nb = dot_nt(dpre_s[k, at, :], up_ref[...]) + brecv[k, at, :]
            z, _ = standardize(x_rows(k, r))
            small_ref[0:1, :] += jnp.sum(d_na * z, axis=0, keepdims=True)
            small_ref[1:2, :] += jnp.sum(d_nb * z, axis=0, keepdims=True)
            small_ref[2:3, :] += jnp.sum(d_na, axis=0, keepdims=True)
            small_ref[3:4, :] += jnp.sum(d_nb, axis=0, keepdims=True)
            d_z = d_na * gain_ref[0:1, :] + d_nb * gain_ref[1:2, :]
            if k == 0:
                arecv[0, at, :] = d_z
            else:
                ysend[at, :] = d_z.astype(B16)

    def weight_grad(left, right, out):
        tiles = left.shape[1] // QB
        width = out.shape[1]

        def load(i):
            slot = lax.rem(i, 2)
            return pltpu.make_async_copy(left.at[:, block(i)], a_s.at[slot], a_sem.at[slot])

        def store(i):
            slot = lax.rem(i, 2)
            return pltpu.make_async_copy(
                o_s.at[slot, :, pl.ds(0, width)], out.at[block(i), :], o_sem.at[slot]
            )

        load(0).start()

        @pl.loop(0, tiles)
        def _(i):
            slot = lax.rem(i, 2)
            load(i).wait()

            @pl.when(i + 1 < tiles)
            def _():
                load(i + 1).start()

            @pl.when(i >= 2)
            def _():
                store(i - 2).wait()

            total = dot_tn(a_s[slot, :seq, :], right[0]) + dot_tn(a_s[slot, seq:, :], right[1])
            o_s[slot, :, :width] = total.astype(B16)
            store(i).start()

        for i in range(max(tiles - 2, 0), tiles):
            store(i).wait()

    if first:
        plan = {
            "feed0": "cd",
            "attend0 2": "cd",
            "near": "cd",
            "hid": "cd",
            "feed1 half": "c",
            "feed1": "a",
            "nb": "c",
            "attend1 1": "a",
            "attend1 2": "c",
            "after1": "a",
            "fold1": "ac",
            "stats": "a",
            "na": "a",
            "back": "a",
        }
    else:
        plan = {
            "feed0": "a",
            "feed1": "a",
            "attend1 0": "a",
            "attend1 1": "a",
            "attend1 2": "b",
            "after1": "a",
            "attend0 0": "b",
            "attend0 1": "a",
            "attend0 3": "b",
            "fold0": "a",
            "stats": "b",
            "na": "a",
        }

    def pump(point):
        for name in plan.get(point, ""):
            sums[name].step()

    def at_heads(k):
        def at_head(h):
            for i in range(heads):
                if "attend%d %d" % (k, i) in plan:

                    @pl.when(h == i)
                    def _():
                        pump("attend%d %d" % (k, i))

        return at_head

    def early_grads():
        weight_grad(hid_h, g_s, down_g)
        pump("hid")
        weight_grad(ctx_ref, g_s, out_g)
        sums["a"].start()
        pump("ctx")

    near0.wait()
    if first:
        feed(0)
        pump("feed0")
        attend(0, at_heads(0))
        across.wait()
    near1 = remote(own_half(g_s, 1), other_half(g_s, 1), sems, 2, core)
    near1.start()
    pump("near")
    near1.wait()
    early_grads()
    if not first:
        feed(0)
        pump("feed0")
    feed(1)
    pump("feed1")
    weight_grad(nb_h, dpre_s, up_g)
    if not first:
        sums["b"].start()
    pump("nb")
    attend(1, at_heads(1))
    pump("after1")
    fold(1)
    back = remote(ysend, yrecv, sems, 7, far)
    back.start()
    next_rows = pltpu.make_async_copy(xn_h.at[pl.ds(0, rows), :], arecv.at[1], local.at[0])
    next_rows.start()
    pump("fold1")
    if not first:
        attend(0, at_heads(0))
    fold(0)
    pump("fold0")
    next_rows.wait()
    for copy in contexts:
        copy.wait()

    @pl.loop(0, half_blocks)
    def _(r):
        at = block(r)
        attn = dot_nn(cfull[at, :], outall_ref[...]) + ob_ref[...]
        x_next = arecv[1, at, :]
        feed_out = x_next - x_rows(0, r) - attn
        small_ref[5:6, :] += jnp.sum(x_next * x_next, axis=0, keepdims=True)
        small_ref[6:7, :] += jnp.sum(attn * attn, axis=0, keepdims=True)
        small_ref[7:8, :] += jnp.sum(feed_out * feed_out, axis=0, keepdims=True)

    pump("stats")
    near_sums = remote(small_ref.at[pl.ds(0, 8), :], got_s.at[0], sems, 11, core)
    near_sums.start()
    weight_grad(na_h, dqkv_s, qkv_g)
    near_sums.wait()
    small_ref[0:8, :] += got_s[0]
    far_sums = remote(small_ref.at[pl.ds(0, 8), :], got_s.at[1], sems, 12, far)
    far_sums.start()
    pump("na")
    back.wait()
    pump("back")

    @pl.loop(0, half_blocks)
    def _(r):
        at = block(r)
        total = arecv[0, at, :] + yrecv[at, :].astype(F32)
        z, inverse = standardize(x_rows(0, r))
        slope = total - jnp.mean(total, axis=-1, keepdims=True)
        slope = slope - z * jnp.mean(total * z, axis=-1, keepdims=True)
        arecv[0, at, :] = grad_ref[at, :].astype(F32) + slope * inverse

    grad_out = pltpu.make_async_copy(arecv.at[0], dx_o, local.at[1])
    grad_out.start()
    far_sums.wait()
    small_ref[0:8, :] += got_s[1]
    for copy in latest:
        copy.wait_send()
    pump("end")
    for item in sums.values():
        item.finish()
    grad_out.wait()


def backward_layer(
    l,
    layers,
    grad,
    u,
    down,
    up,
    out_w,
    qkvw,
    tables,
    qkv,
    lse,
    ctx,
    xn,
    x,
    far_x,
    far_g,
    gains,
    ob,
    hidden,
    nb,
    na,
    ready,
):
    first, final = l == 0, l == layers - 1
    rows, features = grad.shape
    seq = 2 * rows
    w = qkvw.shape[2] // 3
    ff = up.shape[2]
    n = lax.axis_size("dp")
    down_shape, out_w_shape, up_shape, qkv_shape = (
        (ff, features),
        (w, features),
        (features, ff),
        (features, 3 * w),
    )
    shape = jax.ShapeDtypeStruct
    args = [grad, u, down, up, out_w, qkvw, *tables, qkv, lse, ctx, xn, x]
    in_specs = [VMEM] + [ANY] * 10 + [VMEM, ANY, VMEM]
    if first:
        args.append(far_x)
        in_specs.append(VMEM)
    if final:
        args.append(far_g)
        in_specs.append(VMEM)
    args += [gains, ob, hidden, nb, na, *ready]
    in_specs += [VMEM] * 2 + [ANY] * 3
    if first:
        in_specs += [VMEM, ANY]
    low = lambda shapes: [shape(item, B16) for item in shapes]
    out_shape = [shape((rows, features), F32), shape((16, features), F32)]
    out_shape += low([down_shape, out_w_shape, up_shape, qkv_shape, down_shape, out_w_shape])
    out_specs = [ANY, VMEM] + [ANY] * 6
    if first:
        out_shape += low([up_shape, qkv_shape])
        out_specs += [ANY] * 2
    else:
        out_shape += low([(features // n, ff)])
        out_specs += [VMEM]
    scratch = [
        pltpu.VMEM((2, seq, features), B16),
        pltpu.VMEM((2, seq, ff), B16),
        pltpu.VMEM((2, seq, 3 * w), B16),
        pltpu.VMEM((seq, w), F32),
        pltpu.VMEM((seq, w), F32),
        pltpu.VMEM((seq, w), F32),
        pltpu.VMEM((seq, w), B16),
        pltpu.VMEM((2, QB, ff), F32),
        pltpu.VMEM((rows, features), F32),
        pltpu.VMEM((2, rows, features), F32),
        pltpu.VMEM((2, rows, features), F32),
        pltpu.VMEM((rows, features), B16),
        pltpu.VMEM((rows, features), B16),
        pltpu.VMEM((rows, 4 * w), B16),
        pltpu.VMEM((2, 8, features), F32),
    ]
    scratch += [pltpu.VMEM(item.shape[1:], B16) for item in (down, up, out_w, qkvw)]
    scratch += [pltpu.VMEM((4 * w, features), B16)]
    scratch += [pltpu.VMEM(item.shape, F32) for item in tables]
    scratch += [pltpu.VMEM(qkv.shape, B16), pltpu.VMEM(lse.shape, F32)]
    scratch += [pltpu.VMEM((2, features), F32), pltpu.VMEM((1, features), F32)]
    sems = 16 + 2 * (rows // QB)
    scratch += [DMA((sems,)), DMA((sems,)), DMA((2,)), DMA((2,)), DMA((9,))]
    scratch += [pltpu.VMEM((2, 2 * seq, QB), B16), pltpu.VMEM((2, QB, features), B16)]
    scratch += [DMA((2,)), DMA((2,))]
    shapes = half_shapes(down_shape) + [out_w_shape]
    scratch += chunk_scratch(n, shapes) + Scatter.scratch(n, shapes) + Gather.scratch(n, 3)
    if not first:
        scratch += Scatter.scratch(n, half_shapes(up_shape))
    else:
        shapes = half_shapes(qkv_shape)
        scratch += chunk_scratch(n, shapes) + Scatter.scratch(n, shapes)
        scratch += Gather.scratch(n, 2) * 2
    return pl.pallas_call(
        functools.partial(backward_layer_kernel, l, first, final, rows, w, n),
        in_specs=in_specs,
        out_specs=out_specs,
        out_shape=out_shape,
        scratch_shapes=scratch,
        compiler_params=pltpu.CompilerParams(
            vmem_limit_bytes=63 * MIB, collective_id=layers + l, has_side_effects=True
        ),
        cost_estimate=pl.CostEstimate(
            flops=2 * 2 * seq * features * (3 * w + 2 * ff + w) * 2,
            bytes_accessed=40 * MIB,
            transcendentals=4 * seq * seq * w // HEAD,
        ),
        name="backward_layer",
    )(*args)


def on_group(
    tokens,
    cotangent,
    qkv_weight,
    qkv_bias,
    out_weight,
    out_bias,
    up_weight,
    up_bias,
    down_weight,
    down_bias,
    norm_gain,
    norm_shift,
):
    rows, features = tokens.shape
    tensor = lax.axis_size("tensor")
    dp = lax.axis_size("dp")
    w = qkv_weight.shape[2] // 3
    ff = up_weight.shape[2]
    tables = rope_tables(SEQ_LEN, 128)

    x = tokens
    stored = []
    far_x = None
    for l in range(LAYERS):
        got = forward_layer(
            l,
            LAYERS,
            x,
            up_weight,
            down_weight,
            qkv_weight,
            out_weight,
            tables,
            up_bias,
            qkv_bias,
            out_bias,
            down_bias,
            norm_gain,
            norm_shift,
            cotangent,
        )
        na, nb, u, hidden, qkv, ctx, lse, x_next = got[:8]
        if l == 0:
            far_x = got[8]
        if l == LAYERS - 1:
            far_g = got[8]
        stored.append((x, na, nb, u, hidden, qkv, ctx, lse, x_next))
        x = x_next
    output = x

    grad = cotangent
    down_sums, out_sums, up_sums, qkv_sums = ([None] * LAYERS for _ in range(4))
    ready = ()
    small = [None] * LAYERS
    for l in reversed(range(LAYERS)):
        x, na, nb, u, hidden, qkv, ctx, lse, x_next = stored[l]
        grad, small[l], *found = backward_layer(
            l,
            LAYERS,
            grad,
            u,
            down_weight,
            up_weight,
            out_weight,
            qkv_weight,
            tables,
            qkv,
            lse,
            ctx,
            x_next,
            x,
            far_x,
            far_g,
            norm_gain,
            out_bias,
            hidden,
            nb,
            na,
            ready,
        )
        down_sums[l], out_sums[l] = found[4:6]
        if l < LAYERS - 1:
            up_sums[l + 1], qkv_sums[l + 1] = found[6:]
        else:
            ready = (found[6], found[3])
    up_sums[0], qkv_sums[0], small = last_sums(found[2:4], jnp.concatenate(small), 2 * LAYERS)
    small = small.reshape(LAYERS, 16, features)
    down_all, up_all, qkv_all, out_w_all = (
        jnp.stack(item).astype(F32) for item in (down_sums, up_sums, qkv_sums, out_sums)
    )
    layer_stats = jnp.sqrt(jnp.sum(small[:, 5:8], axis=2) / (rows * dp * tensor * features))
    bias_all = small[:, 4]
    return (
        output,
        grad,
        qkv_all,
        small[:, 9, : 3 * w],
        out_w_all,
        bias_all,
        up_all,
        small[:, 8, :ff],
        down_all,
        bias_all,
        small[:, 0:2],
        small[:, 2:4],
        layer_stats,
    )


def solution(mesh):
    in_specs = (
        P(("dp", "tensor"), None),
        P(("dp", "tensor"), None),
        P(None, None, "tensor"),
        P(None, "tensor"),
        P(None, "tensor", None),
        P(),
        P(None, None, "tensor"),
        P(None, "tensor"),
        P(None, "tensor", None),
        P(),
        P(),
        P(),
    )
    out_specs = (
        P(("dp", "tensor"), None),
        P(("dp", "tensor"), None),
        P(None, None, "tensor"),
        P(None, "tensor"),
        P(None, "tensor", None),
        P(),
        P(None, None, "tensor"),
        P(None, "tensor"),
        P(None, "tensor", None),
        P(),
        P(),
        P(),
        P(),
    )
    small = mesh.shape["tensor"] == 4 and mesh.shape["dp"] == 8
    return jax.shard_map(
        on_group if small else on_device,
        mesh=mesh, in_specs=in_specs, out_specs=out_specs, check_vma=False
    )
```

```python
import functools
import math

import jax
import jax.numpy as jnp
import numpy as np
from jax import lax
from jax.experimental import pallas as pl
from jax.experimental.pallas import tpu as pltpu
from jax.sharding import PartitionSpec as P

HEAD = 64
ROT = 16
LAYERS = 2
SEQ_LEN = 1024
QB = 256
SCALE = HEAD ** (-0.5)

EPS = 1e-05
NEG = -1e30
F32 = jnp.float32
B16 = jnp.bfloat16
MIB = 1024 * 1024


def dot_nn(left, right):
    return lax.dot_general(left, right, (((1,), (0,)), ((), ())), preferred_element_type=F32)


def dot_nt(left, right):
    return lax.dot_general(left, right, (((1,), (1,)), ((), ())), preferred_element_type=F32)


def dot_tn(left, right):
    return lax.dot_general(left, right, (((0,), (0,)), ((), ())), preferred_element_type=F32)


def rope_tables(seq, width):
    positions = np.arange(seq, dtype=np.float32)
    inverse = np.exp(np.arange(ROT // 2, dtype=np.float32) * (-2.0 * math.log(10000.0) / ROT))
    angles = (positions[:, None] * inverse.astype(np.float32)[None, :]).astype(np.float64)
    cosine, sine = np.cos(angles), np.sin(angles)
    zero = np.zeros_like(sine)
    rest = np.zeros((seq, HEAD - ROT))
    repeat = lambda parts: jnp.asarray(
        np.tile(np.concatenate(parts, axis=1), (1, width // HEAD)).astype(np.float32)
    )
    return (
        repeat([cosine, cosine, rest + 1.0]),
        repeat([-sine, zero, rest]),
        repeat([zero, sine, rest]),
    )


def rope(rows, cos, sin_lo, sin_hi, sign):
    width = cos.shape[1]
    parts = []
    for j in range(rows.shape[1] // width):
        part = rows[:, j * width : (j + 1) * width]
        turned = (
            pltpu.roll(part, width - ROT // 2, 1) * sin_lo + pltpu.roll(part, ROT // 2, 1) * sin_hi
        )
        parts.append(part * cos + turned if sign > 0 else part * cos - turned)
    return parts[0] if len(parts) == 1 else jnp.concatenate(parts, axis=1)


def attend_forward_kernel(
    w, seq, x_ref, w_ref, b_ref, cos_ref, lo_ref, hi_ref, qkv_ref, ctx_ref, lse_ref
):
    h = pl.program_id(0)
    blocks = seq // QB
    shift = (lax.axis_index("tensor") % 2) * (blocks // 2)
    swapped = lambda i: pl.ds(pl.multiple_of(lax.rem(i + shift, blocks) * QB, QB), QB)

    @pl.when(h == 0)
    def _():
        lse_ref[...] = jnp.zeros_like(lse_ref)
        ctx_ref[...] = jnp.zeros_like(ctx_ref)

        @pl.loop(0, seq // QB)
        def _(r):
            rows = pl.ds(pl.multiple_of(r * QB, QB), QB)
            acc = dot_nn(x_ref[swapped(r), :], w_ref[...]) + b_ref[...]
            turned = rope(acc[:, : 2 * w], cos_ref[rows, :], lo_ref[rows, :], hi_ref[rows, :], 1)
            qkv_ref[rows, : 2 * w] = turned.astype(B16)
            qkv_ref[rows, 2 * w :] = acc[:, 2 * w :].astype(B16)

    mine = (lax.broadcasted_iota(jnp.int32, (1, w), 1) // HEAD) == h
    keep = jnp.where(mine, SCALE, 0.0).astype(B16)
    for i in range(seq // QB):
        n = (i + 1) * QB
        q = qkv_ref[i * QB : n, :w] * keep
        s = dot_nt(q, qkv_ref[:n, w : 2 * w])
        tri = lax.broadcasted_iota(jnp.int32, (QB, QB), 0) >= lax.broadcasted_iota(
            jnp.int32, (QB, QB), 1
        )
        last = jnp.where(tri, s[:, n - QB :], NEG)
        s = last if i == 0 else jnp.concatenate([s[:, : n - QB], last], axis=1)
        top = jnp.max(s, axis=1, keepdims=True)
        p = jnp.exp(s - top)
        total = jnp.sum(p, axis=1, keepdims=True)
        low = (p * (1.0 / total)).astype(B16)
        c = dot_nn(low, qkv_ref[:n, 2 * w :])
        old = ctx_ref[swapped(i), :]
        ctx_ref[swapped(i), :] = jnp.where(mine, c, old.astype(F32)).astype(B16)
        lane = lax.broadcasted_iota(jnp.int32, (QB, 128), 1)
        lse_ref[i * QB : n, :] = jnp.where(lane == h, top + jnp.log(total), lse_ref[i * QB : n, :])


def whole(shape):
    return pl.BlockSpec(shape, lambda h: (0,) * len(shape))


def attend_forward(x, weight, bias, tables):
    seq, features = x.shape
    w = weight.shape[1] // 3
    heads = w // HEAD
    table = tables[0].shape
    return pl.pallas_call(
        functools.partial(attend_forward_kernel, w, seq),
        grid=(heads,),
        in_specs=[
            whole((seq, features)),
            whole((features, 3 * w)),
            whole((1, 3 * w)),
            whole(table),
            whole(table),
            whole(table),
        ],
        out_specs=[whole((seq, 3 * w)), whole((seq, w)), whole((seq, 128))],
        out_shape=[
            jax.ShapeDtypeStruct((seq, 3 * w), B16),
            jax.ShapeDtypeStruct((seq, w), B16),
            jax.ShapeDtypeStruct((seq, 128), F32),
        ],
        compiler_params=pltpu.CompilerParams(
            vmem_limit_bytes=40 * MIB, dimension_semantics=("arbitrary",)
        ),
        cost_estimate=pl.CostEstimate(
            flops=2 * seq * features * 3 * w + 4 * seq * seq * 256 * heads,
            bytes_accessed=2 * seq * features + 6 * features * w + 8 * seq * w,
            transcendentals=seq * seq * heads // 2,
        ),
        name="attend_forward",
    )(x, weight, bias, *tables)


def attend_backward_kernel(
    w,
    seq,
    qkv_ref,
    d_ref,
    lse_ref,
    cos_ref,
    lo_ref,
    hi_ref,
    out_ref,
    bias_ref,
    dq_ref,
    dk_ref,
    dv_ref,
):
    h = pl.program_id(0)
    heads = w // HEAD
    blocks = seq // QB
    shift = (lax.axis_index("tensor") % 2) * (blocks // 2)
    swapped = lambda i: pl.ds(pl.multiple_of(lax.rem(i + shift, blocks) * QB, QB), QB)

    @pl.when(h == 0)
    def _():
        dq_ref[...] = jnp.zeros_like(dq_ref)
        dk_ref[...] = jnp.zeros_like(dk_ref)
        dv_ref[...] = jnp.zeros_like(dv_ref)

    mine = (lax.broadcasted_iota(jnp.int32, (1, w), 1) // HEAD) == h
    keep = jnp.where(mine, SCALE, 0.0).astype(B16)
    keep_value = jnp.where(mine, 1.0, 0.0).astype(B16)
    for i in range(seq // QB):
        n = (i + 1) * QB
        q = qkv_ref[i * QB : n, :w] * keep
        d = d_ref[swapped(i), :] * keep_value
        s = dot_nt(q, qkv_ref[:n, w : 2 * w])
        lane = lax.broadcasted_iota(jnp.int32, (QB, 128), 1)
        lse = jnp.sum(jnp.where(lane == h, lse_ref[i * QB : n, :], 0.0), axis=1, keepdims=True)
        tri = lax.broadcasted_iota(jnp.int32, (QB, QB), 0) >= lax.broadcasted_iota(
            jnp.int32, (QB, QB), 1
        )
        last = jnp.where(tri, s[:, n - QB :], NEG)
        s = last if i == 0 else jnp.concatenate([s[:, : n - QB], last], axis=1)
        p = jnp.exp(s - lse)
        dp = dot_nt(d, qkv_ref[:n, 2 * w :])
        inner = jnp.sum(p * dp, axis=1, keepdims=True)
        ds = (p * (dp - inner)).astype(B16)
        dq_ref[i * QB : n, :] += dot_nn(ds, qkv_ref[:n, w : 2 * w] * keep)
        dk_ref[:n, :] += dot_tn(ds, q)
        dv_ref[:n, :] += dot_tn(p.astype(B16), d)

    @pl.when(h == heads - 1)
    def _():
        bias_ref[...] = jnp.zeros_like(bias_ref)

        @pl.loop(0, seq // QB)
        def _(r):
            rows = pl.ds(pl.multiple_of(r * QB, QB), QB)
            qk = jnp.concatenate([dq_ref[rows, :], dk_ref[rows, :]], axis=1)
            qk = rope(qk, cos_ref[rows, :], lo_ref[rows, :], hi_ref[rows, :], -1).astype(B16)
            v = dv_ref[rows, :].astype(B16)
            out_ref[swapped(r), : 2 * w] = qk
            out_ref[swapped(r), 2 * w :] = v
            bias_ref[:, : 2 * w] += jnp.sum(qk.astype(F32), axis=0, keepdims=True)
            bias_ref[:, 2 * w :] += jnp.sum(v.astype(F32), axis=0, keepdims=True)


def attend_backward(qkv, d_context, lse, tables):
    seq = qkv.shape[0]
    w = qkv.shape[1] // 3
    heads = w // HEAD
    table = tables[0].shape
    return pl.pallas_call(
        functools.partial(attend_backward_kernel, w, seq),
        grid=(heads,),
        in_specs=[
            whole((seq, 3 * w)),
            whole((seq, w)),
            whole((seq, 128)),
            whole(table),
            whole(table),
            whole(table),
        ],
        out_specs=[whole((seq, 3 * w)), whole((1, 3 * w))],
        out_shape=[
            jax.ShapeDtypeStruct((seq, 3 * w), B16),
            jax.ShapeDtypeStruct((1, 3 * w), F32),
        ],
        scratch_shapes=[pltpu.VMEM((seq, w), F32)] * 3,
        compiler_params=pltpu.CompilerParams(
            vmem_limit_bytes=40 * MIB, dimension_semantics=("arbitrary",)
        ),
        cost_estimate=pl.CostEstimate(
            flops=10 * seq * seq * 256 * heads,
            bytes_accessed=16 * seq * w,
            transcendentals=seq * seq * heads // 2,
        ),
        name="attend_backward",
    )(qkv, d_context, lse, *tables)


def normal_parts(u):
    x = jnp.abs(u) * (0.5**0.5)
    t = 1.0 / (1.0 + 0.3275911 * x)
    bell = jnp.exp(-0.5 * u * u)
    poly = t * (
        0.254829592
        + t * (-0.284496736 + t * (1.421413741 + t * (-1.453152027 + t * 1.061405429)))
    )
    half_tail = 0.5 * poly * bell
    return jnp.where(u >= 0.0, 1.0 - half_tail, half_tail), bell


def gelu(u):
    return u * normal_parts(u)[0]


def gelu_slope(u):
    share, bell = normal_parts(u)
    return share + u * bell * ((2.0 * math.pi) ** -0.5)


def gelu_and_slope(u):
    share, bell = normal_parts(u)
    return u * share, share + u * bell * ((2.0 * math.pi) ** -0.5)


def standardize(x):
    average = jnp.mean(x, axis=-1, keepdims=True)
    centred = x - average
    variance = jnp.mean(centred * centred, axis=-1, keepdims=True)
    inverse = lax.rsqrt(variance + EPS)
    return centred * inverse, inverse


def swap(x, axis, bit):
    size = lax.axis_size(axis)
    return lax.ppermute(x, axis, [(i, i ^ bit) for i in range(size)])


def all_bits(size):
    bits = []
    bit = 1
    while bit < size:
        bits.append(bit)
        bit *= 2
    return bits


def after(x, *others):
    return lax.optimization_barrier((x,) + others)[0]


def on_device(
    tokens,
    cotangent,
    qkv_weight,
    qkv_bias,
    out_weight,
    out_bias,
    up_weight,
    up_bias,
    down_weight,
    down_bias,
    norm_gain,
    norm_shift,
):
    rows, features = tokens.shape
    tensor = lax.axis_size("tensor")
    dp = lax.axis_size("dp")
    chips = tensor // 2
    dp_index = lax.axis_index("dp")
    core = lax.axis_index("tensor") % 2
    w = qkv_weight.shape[2] // 3
    ff = up_weight.shape[2]
    heads = w // HEAD
    tables = rope_tables(SEQ_LEN, min(128, 2 * w))
    streams = range(chips)
    chip_bits = all_bits(chips)
    dp_bits = all_bits(dp)

    def core_gather(half):
        return jnp.concatenate([half, swap(half, "tensor", 1)], axis=0)

    def chip_gather(half):
        found = [half]
        for bit in chip_bits:
            found = found + [swap(item, "tensor", 2 * bit) for item in found]
        return found

    def chip_scatter(parts):
        for bit in reversed(chip_bits):
            sent = [swap(part.astype(B16), "tensor", 2 * bit) for part in parts[bit:]]
            parts = [part + got.astype(F32) for part, got in zip(parts[:bit], sent)]
        return parts[0]

    def chip_reduce(parts):
        for bit in chip_bits:
            low = [part.astype(B16) for part in parts]
            sent = [swap(part, "tensor", 2 * bit) for part in low]
            parts = [low[k].astype(F32) + sent[k ^ bit].astype(F32) for k in range(len(parts))]
        return parts

    def core_product(left, right, dot):
        got = swap(dot(left[rows:], right), "tensor", 1)
        return dot(left[:rows], right) + got

    def regroup(columns, back):
        lead = columns.shape[:-1]
        order = (3, heads, HEAD) if back else (heads, 3, HEAD)
        return jnp.swapaxes(columns.reshape(lead + order), -3, -2).reshape(columns.shape)

    qkv_w = [regroup(qkv_weight[l], False) for l in range(LAYERS)]
    qkv_b = [regroup(qkv_bias[l].astype(F32), False)[None] for l in range(LAYERS)]

    share = out_weight.shape[1] // dp
    piece = lax.dynamic_slice_in_dim(out_weight, dp_index * share, share, axis=1)
    near = [out_weight]
    for j in range(1, chips):
        near.append(lax.all_gather(swap(piece, "tensor", 2 * j), "dp", axis=1, tiled=True))
    far = [swap(item, "tensor", 1) for item in near]
    out_all = jnp.concatenate([x for pair in zip(near, far) for x in pair], axis=1)

    x_half = [t.astype(F32) for t in chip_gather(tokens)]
    stored = []
    stat_terms = []
    tick = tokens
    for l in range(LAYERS):
        final = l == LAYERS - 1
        gains = norm_gain[l].astype(F32)
        shifts = norm_shift[l].astype(F32)
        order = list(streams) if l == 0 else list(reversed(streams))
        na, nb, pre, hidden, ffn, qkv, ctx, lse, near = ([None] * chips for _ in range(9))
        up_b = up_bias[l].astype(F32)

        def feed(k):
            u = dot_nn(nb[k], up_weight[l]) + up_b
            pre[k] = u
            hidden[k] = gelu(u).astype(B16)
            ffn[k] = core_product(hidden[k], down_weight[l], dot_nn)

        def attend(k):
            qkv[k], ctx[k], lse[k] = attend_forward(na[k], qkv_w[l], qkv_b[l], tables)
            got = swap(ctx[k][rows:], "tensor", 1)
            near[k] = jnp.concatenate([ctx[k][:rows], got], axis=1)

        for k in order:
            z, _ = standardize(x_half[k])
            na[k] = core_gather((z * gains[0] + shifts[0]).astype(B16))
            nb[k] = core_gather((z * gains[1] + shifts[1]).astype(B16))
        if l == 0:
            for k in order:
                nb[k] = after(nb[k], tick)
                feed(k)
                na[k] = after(na[k], hidden[k])
                attend(k)
                tick = ctx[k]
        else:
            for k in order:
                nb[k] = after(nb[k], tick)
                feed(k)
                tick = hidden[k]
            for k in order:
                na[k] = after(na[k], tick)
                attend(k)
                tick = ctx[k]
        if final:
            ffn = [chip_scatter(ffn)]
        else:
            ffn = chip_reduce(ffn)
        x_next = []
        for k in streams if not final else range(1):
            blocks = [near[k]] + [swap(near[k ^ j], "tensor", 2 * j) for j in range(1, chips)]
            attn = dot_nn(jnp.concatenate(blocks, axis=1), out_all[l]) + out_bias[l].astype(F32)
            ffn_out = ffn[k] + down_bias[l].astype(F32)
            x_next.append(x_half[k] + attn + ffn_out)
            if k == 0:
                stat_terms.append(
                    jnp.stack(
                        [
                            jnp.sum(x_next[0] * x_next[0]),
                            jnp.sum(attn * attn),
                            jnp.sum(ffn_out * ffn_out),
                        ]
                    )
                )
        stored.append((x_half, na, nb, pre, hidden, qkv, ctx, lse))
        if l == 0:
            grad_low_half = chip_gather(after(cotangent, x_next[0]))
        x_half = x_next
    output = x_half[0]

    grad = cotangent.astype(F32)
    big = [None] * LAYERS
    small_all = [None] * LAYERS
    small_dp = [None] * LAYERS
    summed = None
    for l in reversed(range(LAYERS)):
        x_half, na, nb, pre, hidden, qkv, ctx, lse = stored[l]
        gains = norm_gain[l].astype(F32)
        low = grad.astype(B16)
        if l < LAYERS - 1:
            grad_low_half = chip_gather(low)
        g = [core_gather(item) for item in grad_low_half]
        g[0] = after(g[0], tick)
        d_pre, d_qkv, d_z = [None] * chips, [None] * chips, [None] * chips
        down_g = sum(dot_tn(hidden[k], g[k]) for k in streams)
        up_bias_g = jnp.zeros((ff,), F32)
        qkv_bias_g = jnp.zeros((1, 3 * w), F32)
        sums = 0.0
        for k in streams:
            d_pre[k] = (dot_nt(g[k], down_weight[l]) * gelu_slope(pre[k])).astype(B16)
            up_bias_g = up_bias_g + jnp.sum(d_pre[k], axis=0, dtype=F32)
        up_g = sum(dot_tn(nb[k], d_pre[k]) for k in streams)
        first = (down_g.astype(B16), up_g.astype(B16))
        if summed is not None:
            first = lax.optimization_barrier(first + summed[:1])[:2]
        first = lax.psum(first, "dp")
        tick = up_g
        for k in reversed(streams):
            d_ctx = dot_nt(g[k], out_weight[l]).astype(B16)
            d_qkv[k], bias_k = attend_backward(qkv[k], after(d_ctx, tick), lse[k], tables)
            tick = d_qkv[k]
            qkv_bias_g = qkv_bias_g + bias_k
            d_na = core_product(d_qkv[k], qkv_w[l], dot_nt)
            d_nb = core_product(d_pre[k], up_weight[l], dot_nt)
            z, inverse = standardize(x_half[k])
            sums = sums + jnp.stack(
                [
                    jnp.sum(d_na * z, axis=0),
                    jnp.sum(d_nb * z, axis=0),
                    jnp.sum(d_na, axis=0),
                    jnp.sum(d_nb, axis=0),
                ]
            )
            d_z[k] = d_na * gains[0] + d_nb * gains[1]
        total = chip_scatter(d_z)
        slope = total - jnp.mean(total, axis=-1, keepdims=True)
        slope = slope - z * jnp.mean(total * z, axis=-1, keepdims=True)
        bias_g = jnp.sum(low, axis=0, dtype=F32)
        grad = grad + slope * inverse
        out_g = sum(dot_tn(ctx[k], g[k]) for k in streams)
        qkv_g = sum(dot_tn(na[k], d_qkv[k]) for k in streams)
        second = (qkv_g.astype(B16), out_g.astype(B16))
        second = lax.optimization_barrier(second + first[:1])[:2]
        second = lax.psum(second, "dp")
        small_all[l] = jnp.concatenate(
            [sums, bias_g[None], jnp.pad(stat_terms[l], (0, features - 3))[None]], axis=0
        )
        small_dp[l] = jnp.concatenate([up_bias_g, qkv_bias_g[0]])
        big[l] = first + second
        summed = second
    small = jnp.stack(small_all)
    for bit in all_bits(tensor):
        small = small + swap(small, "tensor", bit)
    vector = jnp.stack(small_dp)
    for bit in dp_bits:
        small = small + swap(small, "dp", bit)
        vector = vector + swap(vector, "dp", bit)
    down_all = jnp.stack([item[0] for item in big]).astype(F32)
    up_all = jnp.stack([item[1] for item in big]).astype(F32)
    qkv_all = jnp.stack([regroup(item[2], True) for item in big]).astype(F32)
    out_w_all = jnp.stack([item[3] for item in big]).astype(F32)
    layer_stats = jnp.sqrt(small[:, 5, :3] / (rows * dp * tensor * features))
    bias_all = small[:, 4]
    return (
        output,
        grad,
        qkv_all,
        regroup(vector[:, ff:], True),
        out_w_all,
        bias_all,
        up_all,
        vector[:, :ff],
        down_all,
        bias_all,
        small[:, 0:2],
        small[:, 2:4],
        layer_stats,
    )


MESH = pl.DeviceIdType.MESH
ANY = pl.BlockSpec(memory_space=pl.ANY)
VMEM = pl.BlockSpec(memory_space=pltpu.VMEM)
DMA = pltpu.SemaphoreType.DMA


def partners():
    me = lax.axis_index("tensor")
    return me + 1 - 2 * lax.rem(me, 2), lax.rem(me + 2, 4)


def greet(others, more=0):
    barrier = pltpu.get_barrier_semaphore()
    for other in others:
        pl.semaphore_signal(barrier, inc=1, device_id={"tensor": other}, device_id_type=MESH)
    pl.semaphore_wait(barrier, len(others) + more)


def remote(src, dst, sems, index, target):
    return pltpu.make_async_remote_copy(
        src_ref=src,
        dst_ref=dst,
        send_sem=sems[0].at[index],
        recv_sem=sems[1].at[index],
        device_id={"tensor": target},
        device_id_type=MESH,
    )


def block(i, size=QB):
    return pl.ds(pl.multiple_of(i * size, size), size)


def loader(sems, **pairs):
    waiting = {}
    for i, (name, (src, dst)) in enumerate(pairs.items()):
        waiting[name] = pltpu.make_async_copy(src, dst, sems.at[i])
        waiting[name].start()

    def need(*names):
        for name in names:
            if name in waiting:
                waiting.pop(name).wait()

    return need


def by_kind(rows, heads):
    return jnp.concatenate(
        [
            rows[:, (3 * h + j) * HEAD : (3 * h + j + 1) * HEAD]
            for j in range(3)
            for h in range(heads)
        ],
        axis=1,
    )


def by_head(rows, heads):
    return jnp.concatenate(
        [
            rows[:, (heads * j + h) * HEAD : (heads * j + h + 1) * HEAD]
            for h in range(heads)
            for j in range(3)
        ],
        axis=1,
    )


def causal(s, n):
    tri = lax.broadcasted_iota(jnp.int32, (QB, QB), 0) >= lax.broadcasted_iota(
        jnp.int32, (QB, QB), 1
    )
    last = jnp.where(tri, s[:, n - QB :], NEG)
    return last if n == QB else jnp.concatenate([s[:, : n - QB], last], axis=1)


def forward_layer_kernel(l, first, final, rows, w, *refs):
    it = iter(refs)
    x_ref, up_h, down_h, qkvw_h, out_h, cos_h, lo_h, hi_h = (next(it) for _ in range(8))
    upb_h, qkvb_h, ob_h, db_h, gain_h, shift_h = (next(it) for _ in range(6))
    cot_ref = next(it) if final else None
    na_o, nb_o, u_o, hid_o, qkv_o, ctx_o, lse_o, x_o = (next(it) for _ in range(8))
    far_o = next(it) if first or final else None
    na_s, nb_s, u_s, hid_s, psend, precv, ysend, yrecv = (next(it) for _ in range(8))
    qkv_s, ctx_s, lse_s = (next(it) for _ in range(3))
    far_s = next(it) if first or final else None
    mine_s = next(it)
    up_ref, down_ref, qkvw_ref, out_ref, cos_ref, lo_ref, hi_ref = (next(it) for _ in range(7))
    upb_ref, qkvb_ref, ob_ref, gain_ref, shift_ref = (next(it) for _ in range(5))
    send, recv, local, u_sem, load_sem = (next(it) for _ in range(5))
    sems = (send, recv)
    need = loader(
        load_sem,
        up=(up_h.at[l], up_ref),
        qkvw=(qkvw_h.at[l], qkvw_ref),
        cos=(cos_h, cos_ref),
        lo=(lo_h, lo_ref),
        hi=(hi_h, hi_ref),
        down=(down_h.at[l], down_ref),
        out=(out_h.at[l], out_ref),
    )

    seq = 2 * rows
    heads = w // HEAD
    blocks = seq // QB
    half_blocks = rows // QB
    shift = lax.rem(lax.axis_index("tensor"), 2) * half_blocks
    core, far = partners()
    upb_ref[...] = upb_h[l : l + 1, :].astype(F32)
    qkvb_ref[...] = qkvb_h[l : l + 1, :].astype(F32)
    ob_ref[...] = ob_h[l : l + 1, :].astype(F32) + db_h[l : l + 1, :].astype(F32)
    gain_ref[...] = gain_h[l].astype(F32)
    shift_ref[...] = shift_h[l].astype(F32)
    greet((core, far))
    outs = []

    def keep(src, dst, index):
        copy = pltpu.make_async_copy(src, dst, local.at[index])
        copy.start()
        outs.append(copy)

    far_copy = None
    if first or final:
        far_copy = remote(x_ref if first else cot_ref, far_s, sems, 0, far)
        far_copy.start()

    def x_rows(k, r):
        if not first:
            return x_ref[block(r + k * half_blocks), :]
        return (far_s if k else x_ref)[block(r), :].astype(F32)

    gathers = {}

    def norms(k):
        @pl.loop(0, half_blocks)
        def _(r):
            z, _ = standardize(x_rows(k, r))
            na_s[k, block(r), :] = (z * gain_ref[0:1, :] + shift_ref[0:1, :]).astype(B16)
            nb_s[k, block(r), :] = (z * gain_ref[1:2, :] + shift_ref[1:2, :]).astype(B16)

        gathers[k] = []
        for at, buf in ((0, nb_s), (1, na_s)):
            copy = remote(
                buf.at[k, pl.ds(0, rows), :],
                buf.at[k, pl.ds(rows, rows), :],
                sems,
                1 + 2 * k + at,
                core,
            )
            copy.start()
            gathers[k].append(copy)

    joined = []
    u_out = []

    def feed(k):
        gathers[k][0].wait()
        need("up")
        keep(nb_s.at[k], nb_o.at[pl.ds(k * seq, seq), :], 2 * k)
        for h in (1, 0):
            for copy in u_out:
                copy.wait()
            u_out.clear()

            @pl.loop(0, half_blocks)
            def _(r):
                at = block(r + h * half_blocks)
                u = dot_nn(nb_s[k, at, :], up_ref[...]) + upb_ref[...]
                value, slope = gelu_and_slope(u)
                u_s[r] = slope
                hid_s[k, at, :] = value.astype(B16)

            for r in range(half_blocks):
                copy = pltpu.make_async_copy(
                    u_s.at[r], u_o.at[pl.ds(k * seq + h * rows + r * QB, QB), :], u_sem.at[r]
                )
                copy.start()
                u_out.append(copy)
        keep(hid_s.at[k], hid_o.at[pl.ds(k * seq, seq), :], 2 * k + 1)

    def part(k, r):
        at = block(r)
        index = 9 + k * half_blocks + r
        return remote(psend.at[k, at, :], precv.at[k, at, :], sems, index, core)

    def join(k):
        need("down", "out")

        @pl.loop(0, half_blocks)
        def _(r):
            at = block(r + half_blocks)
            psend[k, block(r), :] = dot_nn(hid_s[k, at, :], down_ref[...]) + dot_nn(
                ctx_s[k, at, :], out_ref[...]
            )
            part(k, r).start()

        joined.append(k)

        @pl.loop(0, half_blocks)
        def _(r):
            at = block(r)
            mine_s[at, :] = dot_nn(hid_s[k, at, :], down_ref[...]) + dot_nn(
                ctx_s[k, at, :], out_ref[...]
            )

        @pl.loop(0, half_blocks)
        def _(r):
            at = block(r)
            part(k, r).wait_recv()
            total = precv[k, at, :] + mine_s[at, :]
            precv[k, at, :] = total
            if not (final and k == 0):
                ysend[k, at, :] = total.astype(B16)

        if not (final and k == 0):
            sums[k] = remote(ysend.at[k], yrecv.at[1 - k], sems, 7 + k, far)
            sums[k].start()

    sums = {}

    def attend(k):
        gathers[k][1].wait()
        need("qkvw", "cos", "lo", "hi")
        keep(na_s.at[k], na_o.at[pl.ds(k * seq, seq), :], 4 + 2 * k)
        swapped = lambda i: block(lax.rem(i + shift, blocks))

        @pl.loop(0, blocks)
        def _(r):
            acc = dot_nn(na_s[k, swapped(r), :], qkvw_ref[...]) + qkvb_ref[...]
            acc = by_kind(acc, heads)
            turned = rope(
                acc[:, : 2 * w], cos_ref[block(r), :], lo_ref[block(r), :], hi_ref[block(r), :], 1
            )
            qkv_s[k, block(r), : 2 * w] = turned.astype(B16)
            qkv_s[k, block(r), 2 * w :] = acc[:, 2 * w :].astype(B16)
            ctx_s[k, block(r), :] = jnp.zeros((QB, w), B16)
            lse_s[k, block(r), :] = jnp.zeros((QB, 128), F32)

        @pl.loop(0, heads)
        def _(h):
            mine = (lax.broadcasted_iota(jnp.int32, (1, w), 1) // HEAD) == h
            scale = jnp.where(mine, SCALE, 0.0).astype(B16)
            lane = lax.broadcasted_iota(jnp.int32, (QB, 128), 1)
            for i in range(blocks):
                n = (i + 1) * QB
                q = qkv_s[k, i * QB : n, :w] * scale
                s = causal(dot_nt(q, qkv_s[k, :n, w : 2 * w]), n)
                top = jnp.max(s, axis=1, keepdims=True)
                p = jnp.exp(s - top)
                total = jnp.sum(p, axis=1, keepdims=True)
                low = (p * (1.0 / total)).astype(B16)
                c = dot_nn(low, qkv_s[k, :n, 2 * w :])
                old = ctx_s[k, swapped(i), :]
                ctx_s[k, swapped(i), :] = jnp.where(mine, c, old.astype(F32)).astype(B16)
                lse_s[k, i * QB : n, :] = jnp.where(
                    lane == h, top + jnp.log(total), lse_s[k, i * QB : n, :]
                )

        keep(qkv_s.at[k], qkv_o.at[pl.ds(k * seq, seq), :], 5 + 2 * k)
        keep(ctx_s.at[k], ctx_o.at[pl.ds(k * seq, seq), :], 8 + 2 * k)
        keep(lse_s.at[k], lse_o.at[pl.ds(k * seq, seq), :], 9 + 2 * k)

    def finish(k):
        sums[1 - k].wait_recv()

        @pl.loop(0, half_blocks)
        def _(r):
            at = block(r)
            both = precv[k, at, :] + yrecv[k, at, :].astype(F32)
            precv[k, at, :] = x_rows(k, r) + (both + ob_ref[...])

        keep(precv.at[k], x_o.at[pl.ds(k * rows, rows), :], 12 + k)

    if first:
        norms(0)
        feed(0)
        attend(0)
        join(0)
        far_copy.wait_recv()
        norms(1)
        feed(1)
        attend(1)
        join(1)
    else:
        norms(1)
        norms(0)
        feed(1)
        attend(1)
        join(1)
        feed(0)
        attend(0)
        join(0)
    if final and not first:
        far_copy.wait_recv()
    if first or final:
        keep(far_s, far_o, 14)
    finish(0)
    if not final:
        finish(1)

    if first or final:
        far_copy.wait_send()
    for copy in u_out + outs:
        copy.wait()
    for k in joined:
        for r in range(half_blocks):
            part(k, r).wait_send()
    for copy in sums.values():
        copy.wait_send()


def forward_layer(
    l, layers, x, up, down, qkvw, out, tables, upb, qkvb, ob, db, gains, shifts, cot
):
    first, final = l == 0, l == layers - 1
    features = x.shape[1]
    rows = x.shape[0] if first else x.shape[0] // 2
    seq = 2 * rows
    w = qkvw.shape[2] // 3
    ff = up.shape[2]
    shape = jax.ShapeDtypeStruct
    out_shape = [
        shape((2 * seq, features), B16),
        shape((2 * seq, features), B16),
        shape((2 * seq, ff), F32),
        shape((2 * seq, ff), B16),
        shape((2 * seq, 3 * w), B16),
        shape((2 * seq, w), B16),
        shape((2 * seq, 128), F32),
        shape((rows if final else 2 * rows, features), F32),
    ]
    if first or final:
        out_shape.append(shape((rows, features), B16))
    args = [x, up, down, qkvw, out, *tables, upb, qkvb, ob, db, gains, shifts]
    if final:
        args.append(cot)
    scratch = [
        pltpu.VMEM((2, seq, features), B16),
        pltpu.VMEM((2, seq, features), B16),
        pltpu.VMEM((rows // QB, QB, ff), F32),
        pltpu.VMEM((2, seq, ff), B16),
        pltpu.VMEM((2, rows, features), F32),
        pltpu.VMEM((2, rows, features), F32),
        pltpu.VMEM((2, rows, features), B16),
        pltpu.VMEM((2, rows, features), B16),
        pltpu.VMEM((2, seq, 3 * w), B16),
        pltpu.VMEM((2, seq, w), B16),
        pltpu.VMEM((2, seq, 128), F32),
    ]
    if first or final:
        scratch.append(pltpu.VMEM((rows, features), B16))
    scratch.append(pltpu.VMEM((rows, features), F32))
    scratch += [pltpu.VMEM(item.shape[1:], B16) for item in (up, down, qkvw, out)]
    scratch += [pltpu.VMEM(item.shape, F32) for item in tables]
    scratch += [pltpu.VMEM((1, width), F32) for width in (ff, 3 * w, features)]
    scratch += [pltpu.VMEM((2, features), F32)] * 2
    sems = 9 + 2 * (rows // QB)
    scratch += [DMA((sems,)), DMA((sems,)), DMA((15,)), DMA((rows // QB,)), DMA((7,))]
    return pl.pallas_call(
        functools.partial(forward_layer_kernel, l, first, final, rows, w),
        in_specs=[VMEM] + [ANY] * 7 + [VMEM] * (len(args) - 8),
        out_specs=[ANY] * len(out_shape),
        out_shape=out_shape,
        scratch_shapes=scratch,
        compiler_params=pltpu.CompilerParams(
            vmem_limit_bytes=63 * MIB, collective_id=l, has_side_effects=True
        ),
        cost_estimate=pl.CostEstimate(
            flops=2 * 2 * seq * features * (3 * w + 2 * ff + w) * 2,
            bytes_accessed=40 * MIB,
            transcendentals=4 * seq * seq * w // HEAD,
        ),
        name="forward_layer",
    )(*args)


def ring_place(index, size):
    side = lax.rem(index, 2)
    level = index // 2
    return level * (1 - side) + (size - 1 - level) * side


def ring_device(place, size):
    side = place // (size // 2)
    return (1 - side) * 2 * place + side * (2 * (size - 1 - place) + 1)


class Ring:
    def __init__(self, n):
        self.n = n
        self.place = ring_place(lax.axis_index("dp"), n)
        self.targets = (
            ring_device(lax.rem(self.place + 1, n), n),
            ring_device(lax.rem(self.place + n - 1, n), n),
        )
        self.steps = n // 2

    def greet(self):
        barrier = pltpu.get_barrier_semaphore()
        for other in self.targets:
            pl.semaphore_signal(barrier, inc=1, device_id={"dp": other}, device_id_type=MESH)

    def rows(self, array, offset):
        size = array.shape[0] // self.n
        chunk = lax.rem(self.place + offset + 2 * self.n, self.n)
        return pl.ds(pl.multiple_of(chunk * size, size), size)

    def copy(self, src, dst, sems, at, way):
        return pltpu.make_async_remote_copy(
            src_ref=src,
            dst_ref=dst,
            send_sem=sems[0].at[at],
            recv_sem=sems[1].at[at],
            device_id={"dp": self.targets[way]},
            device_id_type=MESH,
        )


class Scatter:
    def __init__(self, ring, ins, turns, chunk, it):
        self.ring, self.ins, self.turns, self.chunk = ring, ins, turns, chunk
        self.slots = [next(it) for _ in ins]
        self.mine = [next(it) for _ in ins]
        self.sems = (next(it), next(it))
        self.load = next(it)
        self.parts = [(a, way) for a in range(len(ins)) for way in (0, 1)]

    @staticmethod
    def scratch(n, shapes, dtypes=None):
        count = len(shapes)
        kinds = [(a, b, B16) for a, b in shapes]
        if dtypes:
            kinds = [(a, b, dtype) for (a, b), dtype in zip(shapes, dtypes)]
        return (
            [pltpu.VMEM((2, n // 2, a // n, b), dtype) for a, b, dtype in kinds]
            + [pltpu.VMEM((2, a // n, b), dtype) for a, b, dtype in kinds]
            + [DMA((count, 2, n // 2)), DMA((count, 2, n // 2)), DMA((count, 2))]
        )

    def steps(self, a, way):
        return self.ring.steps - (way ^ self.turns[a])

    def rows(self, a, way, offset):
        return self.ring.rows(self.ins[a], -offset if way else offset)

    def sent(self, a, way, step):
        if step:
            src = self.slots[a].at[way, step - 1]
        else:
            src = self.ins[a].at[self.rows(a, way, self.steps(a, way)), :]
        return self.ring.copy(src, self.slots[a].at[way, step], self.sems, (a, way, step), way)

    def fetch(self, a, way, step):
        at = self.rows(a, way, self.steps(a, way) - step - 1)
        return pltpu.make_async_copy(
            self.ins[a].at[at, :], self.mine[a].at[way], self.load.at[a, way]
        )

    def start(self):
        for part in self.parts:
            self.sent(*part, 0).start()
        for part in self.parts:
            self.fetch(*part, 0).start()

    def step(self, step):
        for a, way in self.parts:
            steps = self.steps(a, way)
            if step >= steps:
                continue
            self.sent(a, way, step).wait_recv()
            if step + 1 < steps:
                self.fetch(a, way, step).wait()
                total = self.slots[a][way, step].astype(F32) + self.mine[a][way].astype(F32)
                self.slots[a][way, step] = total.astype(self.slots[a].dtype)
                self.sent(a, way, step + 1).start()
                if way == 0 or step + 2 < steps:
                    self.fetch(a, way, step + 1).start()
        if step == self.ring.steps - 1:
            for a in range(len(self.ins)):
                self.fetch(a, 0, self.steps(a, 0) - 1).wait()
                total = self.mine[a][0].astype(F32)
                for way in (0, 1):
                    total = total + self.slots[a][way, self.steps(a, way) - 1].astype(F32)
                self.chunk[a][...] = total.astype(self.chunk[a].dtype)

    def finish(self):
        for part in self.parts:
            for step in range(self.steps(*part)):
                self.sent(*part, step).wait_send()


class Gather:
    def __init__(self, ring, chunk, turns, done, it):
        self.ring, self.chunk, self.turns, self.done = ring, chunk, turns, done
        self.sems = (next(it), next(it))
        self.local = next(it)
        self.parts = [(a, way) for a in range(len(chunk)) for way in (0, 1)]

    @staticmethod
    def scratch(n, count):
        return [DMA((count, 2, n // 2)), DMA((count, 2, n // 2)), DMA((count,))]

    steps = Scatter.steps

    def sent(self, a, way, step):
        at = self.ring.rows(self.done[a], step if way else -step)
        src = self.done[a].at[at, :] if step else self.chunk[a]
        return self.ring.copy(src, self.done[a].at[at, :], self.sems, (a, way, step), way)

    def own(self, a):
        at = self.ring.rows(self.done[a], 0)
        return pltpu.make_async_copy(self.chunk[a], self.done[a].at[at, :], self.local.at[a])

    def start(self):
        for part in self.parts:
            self.sent(*part, 0).start()
        for a in range(len(self.chunk)):
            self.own(a).start()

    def step(self, step):
        for a, way in self.parts:
            steps = self.steps(a, way)
            if step < steps:
                self.sent(a, way, step).wait_recv()
                if step + 1 < steps:
                    self.sent(a, way, step + 1).start()

    def finish(self):
        for part in self.parts:
            for step in range(self.steps(*part)):
                self.sent(*part, step).wait_send()
        for a in range(len(self.chunk)):
            self.own(a).wait()


class Total:
    def __init__(self, scatter, gather):
        self.phases = [item for item in (scatter, gather) if item is not None]
        self.steps = self.phases[0].ring.steps
        self.at = 0

    def start(self):
        self.phases[0].start()

    def step(self):
        which, step = divmod(self.at, self.steps)
        self.phases[which].step(step)
        self.at += 1
        if step == self.steps - 1 and which + 1 < len(self.phases):
            self.phases[which + 1].start()

    def finish(self):
        while self.at < len(self.phases) * self.steps:
            self.step()
        for item in self.phases:
            item.finish()


def halves(ref):
    width = ref.shape[1] // 2
    return [ref.at[:, pl.ds(0, width)], ref.at[:, pl.ds(width, width)]]


def half_shapes(shape):
    return [(shape[0], shape[1] // 2)] * 2


def chunk_scratch(n, shapes):
    return [pltpu.VMEM((a // n, b), B16) for a, b in shapes]


def last_sums_kernel(n, count, *refs):
    it = iter(refs)
    ins = [item for _ in range(count) for item in halves(next(it))]
    small_in = next(it)
    done = [item for _ in range(count) for item in halves(next(it))]
    small_out = next(it)
    small_s, small_d = next(it), next(it)
    ring = Ring(n)
    turns = (0, 1) * count + (0,)
    ins.append(small_s)
    done.append(small_d)
    chunk = [next(it) for _ in ins]
    total = Total(Scatter(ring, ins, turns, chunk, it), Gather(ring, chunk, turns, done, it))
    ring.greet()
    rows, width = small_in.shape[0], small_in.shape[1] // 2
    small_s[:rows, :] = small_in[:, :width]
    small_s[rows:, :] = small_in[:, width:]
    pl.semaphore_wait(pltpu.get_barrier_semaphore(), 2)
    total.start()
    total.finish()
    small_out[:, :width] = small_d[:rows, :]
    small_out[:, width:] = small_d[rows:, :]


def last_sums(arrays, small, collective_id):
    n = lax.axis_size("dp")
    shape = jax.ShapeDtypeStruct
    count = len(arrays)
    folded = (2 * small.shape[0], small.shape[1] // 2)
    shapes = [half for item in arrays for half in half_shapes(item.shape)] + [folded]
    dtypes = [B16] * (2 * count) + [F32]
    return pl.pallas_call(
        functools.partial(last_sums_kernel, n, count),
        in_specs=[ANY] * count + [VMEM],
        out_specs=[ANY] * count + [VMEM],
        out_shape=[shape(item.shape, B16) for item in arrays] + [shape(small.shape, F32)],
        scratch_shapes=[pltpu.VMEM(folded, F32)] * 2
        + [pltpu.VMEM((a // n, b), dtype) for (a, b), dtype in zip(shapes, dtypes)]
        + Scatter.scratch(n, shapes, dtypes)
        + Gather.scratch(n, len(shapes)),
        compiler_params=pltpu.CompilerParams(
            vmem_limit_bytes=40 * MIB, collective_id=collective_id, has_side_effects=True
        ),
        cost_estimate=pl.CostEstimate(
            flops=arrays[0].size, bytes_accessed=200 * MIB, transcendentals=0
        ),
        name="last_sums",
    )(*arrays, small)


def backward_layer_kernel(l, first, final, rows, w, n, *refs):
    it = iter(refs)
    grad_ref, u_ref, down_h, up_h, ow_h, qkvw_h = (next(it) for _ in range(6))
    cos_h, lo_h, hi_h = (next(it) for _ in range(3))
    qkv_h, lse_h, ctx_ref, xn_h, x_ref = (next(it) for _ in range(5))
    far_ref = next(it) if first else None
    farg_ref = next(it) if final else None
    gain_h, ob_h = (next(it) for _ in range(2))
    hid_h, nb_h, na_h = (next(it) for _ in range(3))
    chunk_in, ready = (next(it), next(it)) if first else (None, None)
    dx_o, small_ref = (next(it) for _ in range(2))
    down_g, out_g, up_g, qkv_g, down_done, out_done = (next(it) for _ in range(6))
    up_chunk = None if first else next(it)
    up_done, ready_done = (next(it), next(it)) if first else (None, None)
    g_s, dpre_s, dqkv_s, dq_s, dk_s, dv_s, dctx_s = (next(it) for _ in range(7))
    u_s, osend, brecv, arecv, ysend, yrecv = (next(it) for _ in range(6))
    cfull, got_s = (next(it) for _ in range(2))
    down_ref, up_ref, ow_ref, qkvw_ref, outall_ref = (next(it) for _ in range(5))
    cos_ref, lo_ref, hi_ref, qkv_ref, lse_ref = (next(it) for _ in range(5))
    gain_ref, ob_ref = (next(it) for _ in range(2))
    send, recv, local, u_sem, load_sem = (next(it) for _ in range(5))
    sems = (send, recv)
    a_s, o_s, a_sem, o_sem = (next(it) for _ in range(4))
    ring = Ring(n)
    sums = {}
    turns = (0, 1, 0)
    chunk = [next(it) for _ in range(3)]
    sums["a"] = Total(
        Scatter(ring, halves(down_g) + [out_g], turns, chunk, it),
        Gather(ring, chunk, turns, halves(down_done) + [out_done], it),
    )
    if not first:
        sums["b"] = Total(Scatter(ring, halves(up_g), turns, halves(up_chunk), it), None)
    else:
        chunk = [next(it) for _ in range(2)]
        sums["c"] = Total(
            Scatter(ring, halves(ready), turns, chunk, it),
            Gather(ring, chunk, turns, halves(ready_done), it),
        )
        sums["d"] = Total(None, Gather(ring, halves(chunk_in), turns, halves(up_done), it))
    need = loader(
        load_sem,
        down=(down_h.at[l], down_ref),
        up=(up_h.at[l], up_ref),
        ow=(ow_h.at[l], ow_ref),
        qkv=(qkv_h, qkv_ref),
        lse=(lse_h, lse_ref),
        cos=(cos_h, cos_ref),
        lo=(lo_h, lo_ref),
        hi=(hi_h, hi_ref),
        qkvw=(qkvw_h.at[l], qkvw_ref),
    )

    seq = 2 * rows
    ff = up_ref.shape[1]
    heads = w // HEAD
    blocks = seq // QB
    half_blocks = rows // QB
    shift = lax.rem(lax.axis_index("tensor"), 2) * half_blocks
    swapped = lambda i: block(lax.rem(i + shift, blocks))
    core, far = partners()
    diag = lax.rem(core + 2, 4)
    ring.greet()
    greet((core, far, diag), 2)
    def load_u(k, i):
        return pltpu.make_async_copy(
            u_ref.at[pl.ds(k * seq + i * QB, QB), :], u_s.at[i % 2], u_sem.at[i % 2]
        )

    small_ref[...] = jnp.zeros_like(small_ref)
    gain_ref[...] = gain_h[l].astype(F32)
    ob_ref[...] = ob_h[l : l + 1, :].astype(F32)
    load_u(0, 0).start()
    load_u(0, 1).start()

    @pl.loop(0, half_blocks)
    def _(r):
        low = grad_ref[block(r), :].astype(B16)
        g_s[0, block(r), :] = low
        small_ref[4:5, :] += jnp.sum(low.astype(F32), axis=0, keepdims=True)

    own_half = lambda buf, k: buf.at[k, pl.ds(0, rows), :]
    other_half = lambda buf, k: buf.at[k, pl.ds(rows, rows), :]
    if final:
        g_s[1, :rows, :] = farg_ref[...]
    else:
        across = remote(own_half(g_s, 0), own_half(g_s, 1), sems, 0, far)
        across.start()
    near0 = remote(own_half(g_s, 0), other_half(g_s, 0), sems, 1, core)
    near0.start()
    if first:
        sums["c"].start()
        sums["d"].start()
    cfull[:, :w] = ctx_ref[:rows, :]
    contexts = [
        remote(ctx_ref.at[pl.ds(rows, rows), :], cfull.at[:, pl.ds(w, w)], sems, 8, core),
        remote(ctx_ref.at[pl.ds(seq, rows), :], cfull.at[:, pl.ds(2 * w, w)], sems, 9, far),
        remote(ctx_ref.at[pl.ds(seq + rows, rows), :], cfull.at[:, pl.ds(3 * w, w)], sems, 10, diag),
    ]
    need("ow")
    outall_ref[:w, :] = ow_ref[...]
    for i, other in enumerate((core, far, diag)):
        contexts.append(
            remote(ow_ref, outall_ref.at[pl.ds((i + 1) * w, w), :], sems, 13 + i, other)
        )
    for copy in contexts:
        copy.start()

    swaps = {}
    latest = []

    def feed(k):
        need("down")
        for i in range(blocks):
            load_u(k, i).wait()
            at = pl.ds(i * QB, QB)
            d_hidden = dot_nt(g_s[k, at, :], down_ref[...])
            d_pre = (d_hidden * u_s[i % 2]).astype(B16)
            dpre_s[k, at, :] = d_pre
            small_ref[8:9, :ff] += jnp.sum(d_pre.astype(F32), axis=0, keepdims=True)
            if i + 2 < blocks:
                load_u(k, i + 2).start()
            elif k == 0:
                load_u(1, i + 2 - blocks).start()
            if 2 * (i + 1) == blocks:
                pump("feed%d half" % k)

        need("up")
        for copy in latest:
            copy.wait_send()
        latest.clear()

        @pl.loop(0, half_blocks)
        def _(r):
            osend[block(r), :] = dot_nt(dpre_s[k, block(r + half_blocks), :], up_ref[...])

        swaps[k] = [remote(osend, brecv.at[k], sems, 3 + 2 * k, core)]
        swaps[k][0].start()
        latest.append(swaps[k][0])

    def attend(k, pump):
        need("ow", "qkv", "lse", "cos", "lo", "hi", "qkvw")

        @pl.loop(0, blocks)
        def _(r):
            dctx_s[block(r), :] = dot_nt(g_s[k, swapped(r), :], ow_ref[...]).astype(B16)
            dq_s[block(r), :] = jnp.zeros((QB, w), F32)
            dk_s[block(r), :] = jnp.zeros((QB, w), F32)
            dv_s[block(r), :] = jnp.zeros((QB, w), F32)

        base = k * seq

        @pl.loop(0, heads)
        def _(h):
            mine = (lax.broadcasted_iota(jnp.int32, (1, w), 1) // HEAD) == h
            scale = jnp.where(mine, SCALE, 0.0).astype(B16)
            only = jnp.where(mine, 1.0, 0.0).astype(B16)
            lane = lax.broadcasted_iota(jnp.int32, (QB, 128), 1)
            for i in range(blocks):
                n = (i + 1) * QB
                q = qkv_ref[base + i * QB : base + n, :w] * scale
                d = dctx_s[i * QB : n, :] * only
                s = causal(dot_nt(q, qkv_ref[base : base + n, w : 2 * w]), n)
                lse = jnp.sum(
                    jnp.where(lane == h, lse_ref[base + i * QB : base + n, :], 0.0),
                    axis=1,
                    keepdims=True,
                )
                p = jnp.exp(s - lse)
                dp = dot_nt(d, qkv_ref[base : base + n, 2 * w :])
                inner = jnp.sum(p * dp, axis=1, keepdims=True)
                ds = (p * (dp - inner)).astype(B16)
                dq_s[i * QB : n, :] += dot_nn(ds, qkv_ref[base : base + n, w : 2 * w] * scale)
                dk_s[:n, :] += dot_tn(ds, q)
                dv_s[:n, :] += dot_tn(p.astype(B16), d)
            pump(h)

        @pl.loop(0, blocks)
        def _(r):
            at = block(r)
            qk = jnp.concatenate([dq_s[at, :], dk_s[at, :]], axis=1)
            qk = rope(qk, cos_ref[at, :], lo_ref[at, :], hi_ref[at, :], -1)
            low = by_head(jnp.concatenate([qk, dv_s[at, :]], axis=1), heads).astype(B16)
            dqkv_s[k, swapped(r), :] = low
            small_ref[9:10, : 3 * w] += jnp.sum(low.astype(F32), axis=0, keepdims=True)

        for copy in latest:
            copy.wait_send()
        latest.clear()

        @pl.loop(0, half_blocks)
        def _(r):
            osend[block(r), :] = dot_nt(dqkv_s[k, block(r + half_blocks), :], qkvw_ref[...])
            piece(k, r).start()

        latest.extend(piece(k, r) for r in range(half_blocks))

    def piece(k, r):
        at = block(r)
        index = 16 + k * half_blocks + r
        return remote(osend.at[at, :], arecv.at[k, at, :], sems, index, core)

    def x_rows(k, r):
        if not first:
            return x_ref[block(r + k * half_blocks), :]
        return (far_ref if k else x_ref)[block(r), :].astype(F32)

    def fold(k):
        swaps[k][0].wait_recv()

        @pl.loop(0, half_blocks)
        def _(r):
            piece(k, r).wait_recv()
            at = block(r)
            d_na = dot_nt(dqkv_s[k, at, :], qkvw_ref[...]) + arecv[k, at, :]
            d_nb = dot_nt(dpre_s[k, at, :], up_ref[...]) + brecv[k, at, :]
            z, _ = standardize(x_rows(k, r))
            small_ref[0:1, :] += jnp.sum(d_na * z, axis=0, keepdims=True)
            small_ref[1:2, :] += jnp.sum(d_nb * z, axis=0, keepdims=True)
            small_ref[2:3, :] += jnp.sum(d_na, axis=0, keepdims=True)
            small_ref[3:4, :] += jnp.sum(d_nb, axis=0, keepdims=True)
            d_z = d_na * gain_ref[0:1, :] + d_nb * gain_ref[1:2, :]
            if k == 0:
                arecv[0, at, :] = d_z
            else:
                ysend[at, :] = d_z.astype(B16)

    def weight_grad(left, right, out):
        tiles = left.shape[1] // QB
        width = out.shape[1]

        def load(i):
            slot = lax.rem(i, 2)
            return pltpu.make_async_copy(left.at[:, block(i)], a_s.at[slot], a_sem.at[slot])

        def store(i):
            slot = lax.rem(i, 2)
            return pltpu.make_async_copy(
                o_s.at[slot, :, pl.ds(0, width)], out.at[block(i), :], o_sem.at[slot]
            )

        load(0).start()

        @pl.loop(0, tiles)
        def _(i):
            slot = lax.rem(i, 2)
            load(i).wait()

            @pl.when(i + 1 < tiles)
            def _():
                load(i + 1).start()

            @pl.when(i >= 2)
            def _():
                store(i - 2).wait()

            total = dot_tn(a_s[slot, :seq, :], right[0]) + dot_tn(a_s[slot, seq:, :], right[1])
            o_s[slot, :, :width] = total.astype(B16)
            store(i).start()

        for i in range(max(tiles - 2, 0), tiles):
            store(i).wait()

    if first:
        plan = {
            "feed0": "cd",
            "attend0 2": "cd",
            "near": "cd",
            "hid": "cd",
            "feed1 half": "c",
            "feed1": "a",
            "nb": "c",
            "attend1 1": "a",
            "attend1 2": "c",
            "after1": "a",
            "fold1": "ac",
            "stats": "a",
            "na": "a",
            "back": "a",
        }
    else:
        plan = {
            "feed0": "a",
            "feed1": "a",
            "attend1 0": "a",
            "attend1 1": "a",
            "attend1 2": "b",
            "after1": "a",
            "attend0 0": "b",
            "attend0 1": "a",
            "attend0 3": "b",
            "fold0": "a",
            "stats": "b",
            "na": "a",
        }

    def pump(point):
        for name in plan.get(point, ""):
            sums[name].step()

    def at_heads(k):
        def at_head(h):
            for i in range(heads):
                if "attend%d %d" % (k, i) in plan:

                    @pl.when(h == i)
                    def _():
                        pump("attend%d %d" % (k, i))

        return at_head

    def early_grads():
        weight_grad(hid_h, g_s, down_g)
        pump("hid")
        weight_grad(ctx_ref, g_s, out_g)
        sums["a"].start()
        pump("ctx")

    near0.wait()
    if first:
        feed(0)
        pump("feed0")
        attend(0, at_heads(0))
        across.wait()
    near1 = remote(own_half(g_s, 1), other_half(g_s, 1), sems, 2, core)
    near1.start()
    pump("near")
    near1.wait()
    early_grads()
    if not first:
        feed(0)
        pump("feed0")
    feed(1)
    pump("feed1")
    weight_grad(nb_h, dpre_s, up_g)
    if not first:
        sums["b"].start()
    pump("nb")
    attend(1, at_heads(1))
    pump("after1")
    fold(1)
    back = remote(ysend, yrecv, sems, 7, far)
    back.start()
    next_rows = pltpu.make_async_copy(xn_h.at[pl.ds(0, rows), :], arecv.at[1], local.at[0])
    next_rows.start()
    pump("fold1")
    if not first:
        attend(0, at_heads(0))
    fold(0)
    pump("fold0")
    next_rows.wait()
    for copy in contexts:
        copy.wait()

    @pl.loop(0, half_blocks)
    def _(r):
        at = block(r)
        attn = dot_nn(cfull[at, :], outall_ref[...]) + ob_ref[...]
        x_next = arecv[1, at, :]
        feed_out = x_next - x_rows(0, r) - attn
        small_ref[5:6, :] += jnp.sum(x_next * x_next, axis=0, keepdims=True)
        small_ref[6:7, :] += jnp.sum(attn * attn, axis=0, keepdims=True)
        small_ref[7:8, :] += jnp.sum(feed_out * feed_out, axis=0, keepdims=True)

    pump("stats")
    near_sums = remote(small_ref.at[pl.ds(0, 8), :], got_s.at[0], sems, 11, core)
    near_sums.start()
    weight_grad(na_h, dqkv_s, qkv_g)
    near_sums.wait()
    small_ref[0:8, :] += got_s[0]
    far_sums = remote(small_ref.at[pl.ds(0, 8), :], got_s.at[1], sems, 12, far)
    far_sums.start()
    pump("na")
    back.wait()
    pump("back")

    @pl.loop(0, half_blocks)
    def _(r):
        at = block(r)
        total = arecv[0, at, :] + yrecv[at, :].astype(F32)
        z, inverse = standardize(x_rows(0, r))
        slope = total - jnp.mean(total, axis=-1, keepdims=True)
        slope = slope - z * jnp.mean(total * z, axis=-1, keepdims=True)
        arecv[0, at, :] = grad_ref[at, :].astype(F32) + slope * inverse

    grad_out = pltpu.make_async_copy(arecv.at[0], dx_o, local.at[1])
    grad_out.start()
    far_sums.wait()
    small_ref[0:8, :] += got_s[1]
    for copy in latest:
        copy.wait_send()
    pump("end")
    for item in sums.values():
        item.finish()
    grad_out.wait()


def backward_layer(
    l,
    layers,
    grad,
    u,
    down,
    up,
    out_w,
    qkvw,
    tables,
    qkv,
    lse,
    ctx,
    xn,
    x,
    far_x,
    far_g,
    gains,
    ob,
    hidden,
    nb,
    na,
    ready,
):
    first, final = l == 0, l == layers - 1
    rows, features = grad.shape
    seq = 2 * rows
    w = qkvw.shape[2] // 3
    ff = up.shape[2]
    n = lax.axis_size("dp")
    down_shape, out_w_shape, up_shape, qkv_shape = (
        (ff, features),
        (w, features),
        (features, ff),
        (features, 3 * w),
    )
    shape = jax.ShapeDtypeStruct
    args = [grad, u, down, up, out_w, qkvw, *tables, qkv, lse, ctx, xn, x]
    in_specs = [VMEM] + [ANY] * 10 + [VMEM, ANY, VMEM]
    if first:
        args.append(far_x)
        in_specs.append(VMEM)
    if final:
        args.append(far_g)
        in_specs.append(VMEM)
    args += [gains, ob, hidden, nb, na, *ready]
    in_specs += [VMEM] * 2 + [ANY] * 3
    if first:
        in_specs += [VMEM, ANY]
    low = lambda shapes: [shape(item, B16) for item in shapes]
    out_shape = [shape((rows, features), F32), shape((16, features), F32)]
    out_shape += low([down_shape, out_w_shape, up_shape, qkv_shape, down_shape, out_w_shape])
    out_specs = [ANY, VMEM] + [ANY] * 6
    if first:
        out_shape += low([up_shape, qkv_shape])
        out_specs += [ANY] * 2
    else:
        out_shape += low([(features // n, ff)])
        out_specs += [VMEM]
    scratch = [
        pltpu.VMEM((2, seq, features), B16),
        pltpu.VMEM((2, seq, ff), B16),
        pltpu.VMEM((2, seq, 3 * w), B16),
        pltpu.VMEM((seq, w), F32),
        pltpu.VMEM((seq, w), F32),
        pltpu.VMEM((seq, w), F32),
        pltpu.VMEM((seq, w), B16),
        pltpu.VMEM((2, QB, ff), F32),
        pltpu.VMEM((rows, features), F32),
        pltpu.VMEM((2, rows, features), F32),
        pltpu.VMEM((2, rows, features), F32),
        pltpu.VMEM((rows, features), B16),
        pltpu.VMEM((rows, features), B16),
        pltpu.VMEM((rows, 4 * w), B16),
        pltpu.VMEM((2, 8, features), F32),
    ]
    scratch += [pltpu.VMEM(item.shape[1:], B16) for item in (down, up, out_w, qkvw)]
    scratch += [pltpu.VMEM((4 * w, features), B16)]
    scratch += [pltpu.VMEM(item.shape, F32) for item in tables]
    scratch += [pltpu.VMEM(qkv.shape, B16), pltpu.VMEM(lse.shape, F32)]
    scratch += [pltpu.VMEM((2, features), F32), pltpu.VMEM((1, features), F32)]
    sems = 16 + 2 * (rows // QB)
    scratch += [DMA((sems,)), DMA((sems,)), DMA((2,)), DMA((2,)), DMA((9,))]
    scratch += [pltpu.VMEM((2, 2 * seq, QB), B16), pltpu.VMEM((2, QB, features), B16)]
    scratch += [DMA((2,)), DMA((2,))]
    shapes = half_shapes(down_shape) + [out_w_shape]
    scratch += chunk_scratch(n, shapes) + Scatter.scratch(n, shapes) + Gather.scratch(n, 3)
    if not first:
        scratch += Scatter.scratch(n, half_shapes(up_shape))
    else:
        shapes = half_shapes(qkv_shape)
        scratch += chunk_scratch(n, shapes) + Scatter.scratch(n, shapes)
        scratch += Gather.scratch(n, 2) * 2
    return pl.pallas_call(
        functools.partial(backward_layer_kernel, l, first, final, rows, w, n),
        in_specs=in_specs,
        out_specs=out_specs,
        out_shape=out_shape,
        scratch_shapes=scratch,
        compiler_params=pltpu.CompilerParams(
            vmem_limit_bytes=63 * MIB, collective_id=layers + l, has_side_effects=True
        ),
        cost_estimate=pl.CostEstimate(
            flops=2 * 2 * seq * features * (3 * w + 2 * ff + w) * 2,
            bytes_accessed=40 * MIB,
            transcendentals=4 * seq * seq * w // HEAD,
        ),
        name="backward_layer",
    )(*args)


def on_group(
    tokens,
    cotangent,
    qkv_weight,
    qkv_bias,
    out_weight,
    out_bias,
    up_weight,
    up_bias,
    down_weight,
    down_bias,
    norm_gain,
    norm_shift,
):
    rows, features = tokens.shape
    tensor = lax.axis_size("tensor")
    dp = lax.axis_size("dp")
    w = qkv_weight.shape[2] // 3
    ff = up_weight.shape[2]
    tables = rope_tables(SEQ_LEN, 128)

    x = tokens
    stored = []
    far_x = None
    for l in range(LAYERS):
        got = forward_layer(
            l,
            LAYERS,
            x,
            up_weight,
            down_weight,
            qkv_weight,
            out_weight,
            tables,
            up_bias,
            qkv_bias,
            out_bias,
            down_bias,
            norm_gain,
            norm_shift,
            cotangent,
        )
        na, nb, u, hidden, qkv, ctx, lse, x_next = got[:8]
        if l == 0:
            far_x = got[8]
        if l == LAYERS - 1:
            far_g = got[8]
        stored.append((x, na, nb, u, hidden, qkv, ctx, lse, x_next))
        x = x_next
    output = x

    grad = cotangent
    down_sums, out_sums, up_sums, qkv_sums = ([None] * LAYERS for _ in range(4))
    ready = ()
    small = [None] * LAYERS
    for l in reversed(range(LAYERS)):
        x, na, nb, u, hidden, qkv, ctx, lse, x_next = stored[l]
        grad, small[l], *found = backward_layer(
            l,
            LAYERS,
            grad,
            u,
            down_weight,
            up_weight,
            out_weight,
            qkv_weight,
            tables,
            qkv,
            lse,
            ctx,
            x_next,
            x,
            far_x,
            far_g,
            norm_gain,
            out_bias,
            hidden,
            nb,
            na,
            ready,
        )
        down_sums[l], out_sums[l] = found[4:6]
        if l < LAYERS - 1:
            up_sums[l + 1], qkv_sums[l + 1] = found[6:]
        else:
            ready = (found[6], found[3])
    up_sums[0], qkv_sums[0], small = last_sums(found[2:4], jnp.concatenate(small), 2 * LAYERS)
    small = small.reshape(LAYERS, 16, features)
    down_all, up_all, qkv_all, out_w_all = (
        jnp.stack(item).astype(F32) for item in (down_sums, up_sums, qkv_sums, out_sums)
    )
    layer_stats = jnp.sqrt(jnp.sum(small[:, 5:8], axis=2) / (rows * dp * tensor * features))
    bias_all = small[:, 4]
    return (
        output,
        grad,
        qkv_all,
        small[:, 9, : 3 * w],
        out_w_all,
        bias_all,
        up_all,
        small[:, 8, :ff],
        down_all,
        bias_all,
        small[:, 0:2],
        small[:, 2:4],
        layer_stats,
    )


def solution(mesh):
    in_specs = (
        P(("dp", "tensor"), None),
        P(("dp", "tensor"), None),
        P(None, None, "tensor"),
        P(None, "tensor"),
        P(None, "tensor", None),
        P(),
        P(None, None, "tensor"),
        P(None, "tensor"),
        P(None, "tensor", None),
        P(),
        P(),
        P(),
    )
    out_specs = (
        P(("dp", "tensor"), None),
        P(("dp", "tensor"), None),
        P(None, None, "tensor"),
        P(None, "tensor"),
        P(None, "tensor", None),
        P(),
        P(None, None, "tensor"),
        P(None, "tensor"),
        P(None, "tensor", None),
        P(),
        P(),
        P(),
        P(),
    )
    small = mesh.shape["tensor"] == 4 and mesh.shape["dp"] == 8
    return jax.shard_map(
        on_group if small else on_device,
        mesh=mesh, in_specs=in_specs, out_specs=out_specs, check_vma=False
    )
```
